128 devices in a mesh: src: 4 (over y), tile: 32 (over z, x, core).
Axes of the slice: x: 4, y: 4, z: 4, core: 2. Of those that a mesh axis runs over, the one named last changes fastest.
Arguments:
- exposure: bfloat16 [4, 4096, 8192], P('src', 'tile'), may hold values from -6 to 6
- row_bases: bfloat16 [27, 41], replicated, may hold values from -1 to 1
- col_bases: bfloat16 [27, 41], replicated, may hold values from -1 to 1
- coefficients: float32 [4, 32, 64, 27], P('src', 'tile'), may hold values from -1.2 to 1.2
- warp_rows: bfloat16 [4, 32, 64, 128, 128], P('src', 'tile'), may hold values from -0.4 to 1.4, as said below
- warp_cols: bfloat16 [4, 32, 64, 128, 128], P('src', 'tile'), may hold values from -0.4 to 1.4, as said below
- variance: float32 [4, 32, 64], P('src', 'tile'), may hold values from 0.25 to 4
- footprint: int32 [4, 32, 64, 1], P('src', 'tile'), may hold values from 0 to 31; in each aligned block of 64 rows (0 to 63, 64 to 127, ..., all dimensions but the last counted through in order) at most 4 rows name the same one
- slot_index: int32 [4, 32, 64], P('src', 'tile'), may hold values from 0 to 63
Outputs:
- coadd: float32 [128, 512, 512], P('tile', 'src')
The draws below stay inside these ranges and needn't reach their ends.
Inputs may be any that keep to these rules, and one draw needn't show every extreme that they name: `footprint`: within the blocks of one index of src and tile, no tile owner is named more than 4 times, a bound that some block reaches. `warp_rows`: each row holds the Lanczos weights of one output pixel. `warp_cols`: each row holds the Lanczos weights of one output pixel.
All inputs are finite; a program needn't handle non-finite values.
Results may differ from the reference program's by a relative error of at most 0.014.
Values may be sent and summed in bfloat16 or wider, within the bound.
A program may use at most 128 MiB of HBM per device.

```python
import math
import jax
import jax.numpy as jnp
import numpy as np
from jax import lax

BLOCK = 128
KSIZE = 41
BASES = 27
VISITS = 4
TILE = 512
TILES = 128
SLOTS = 64
BLK_COLS = 64
EXP_COLS = 8192
EXP_ROWS = 4096
CAP = 4
N_SRC = 4
N_TILE = 32


def lanczos(key, leading):
    subkeys = jax.random.split(key, 2)
    shifts = jax.random.uniform(subkeys[0], leading + (1, 1), jnp.float32, 0.15, 0.85)
    stretch = jax.random.uniform(subkeys[1], leading + (1, 1), jnp.float32, 0.995, 1.005)
    out_pos = jnp.arange(BLOCK, dtype=jnp.float32)[:, None]
    in_pos = jnp.arange(BLOCK, dtype=jnp.float32)[None, :]
    centre = 0.5 * BLOCK
    centres = jnp.clip(shifts + stretch * (out_pos - centre) + centre, 2.0, BLOCK - 3.0)
    offset = in_pos - centres
    tap_values = jnp.where(jnp.abs(offset) < 3.0, jnp.sinc(offset) * jnp.sinc(offset / 3.0), 0.0)
    return tap_values / jnp.sum(tap_values, axis=-1, keepdims=True)


def draw_warp_rows(key, part):
    key = jax.random.fold_in(key, 5)
    return lanczos(key, (VISITS, N_TILE, BLK_COLS)).astype(jnp.bfloat16)


def draw_warp_cols(key, part):
    key = jax.random.fold_in(key, 9)
    return lanczos(key, (VISITS, N_TILE, BLK_COLS)).astype(jnp.bfloat16)


def set_ends(result, stream_key, smallest, high):
    spot = [jax.random.randint(jax.random.fold_in(stream_key, axis), (), 0, length) for axis, length in enumerate(result.shape)]
    longest = result.shape.index(max(result.shape))
    beside = spot[:longest] + [(spot[longest] + 1) % result.shape[longest]] + spot[longest + 1:]
    return result.at[tuple(spot)].set(smallest).at[tuple(beside)].set(high)


def shard_levels(stream_key, extent, cuts, least, high):
    loudness = 1.0
    for dim, shards_of in cuts:
        heights = jax.random.uniform(jax.random.fold_in(jax.random.fold_in(stream_key, 6), dim), (shards_of,), jnp.float32, least / len(cuts), high / len(cuts))
        loudness = loudness * jnp.repeat(jnp.exp(heights), extent[dim] // shards_of).reshape((-1,) + (1,) * (len(extent) - 1 - dim))
    return loudness


def assign_block(key, own, number, rows, amount, top, bound, lean):
    sequence = jax.random.permutation(key, amount)
    packed, usual = shares(amount, rows * top, bound, lean, True), shares(amount, rows * top, bound, lean, False)
    places = jnp.arange(amount)

    def named(lengths, rotation):
        used = int((lengths > 0).sum())
        fixed = max(1, used // 4)
        shifted = fixed + (places - fixed + rotation * (used - fixed)) % max(1, amount - fixed)
        return jnp.zeros((amount,), jnp.int32).at[sequence[jnp.where(places < fixed, places, shifted)]].set(jnp.asarray(lengths, jnp.int32))

    lengths = jnp.where(number % 4 == 0, named(packed, number // 4), named(usual, number - number // 4 - 1))
    mixed = jax.random.permutation(jax.random.fold_in(own, 3), amount)
    giver, taker = mixed[0:amount // 2 * 2:2], mixed[1:amount // 2 * 2:2]
    margin = jnp.minimum(lengths[giver] - 1, bound - lengths[taker]) // 2
    margin = jnp.where((giver == sequence[0]) | (taker == sequence[0]) | (lengths[taker] == 0), 0, jnp.maximum(margin, 0))
    shifted = jax.random.randint(jax.random.fold_in(own, 4), (amount // 2,), 0, 1 << 20) % (margin + 1)
    lengths = lengths.at[giver].add(-shifted).at[taker].add(shifted)
    members = jnp.searchsorted(jnp.cumsum(lengths), jnp.arange(rows * top), side="right").astype(jnp.int32)
    table = members.reshape(top, rows).T
    table = table[jax.random.permutation(jax.random.fold_in(own, 1), rows)]
    rotation = jax.random.randint(jax.random.fold_in(own, 2), (rows, 1), 0, top)
    return jnp.take_along_axis(table, (jnp.arange(top)[None, :] + rotation) % top, axis=1)


def shares(amount, total, reach, lean, full):
    loads = [(1 << 20) // math.isqrt(standing ** lean) + 1 for standing in range(1, amount + 1)]
    largest = reach if full else min(reach, max(-(-total // amount), total * loads[0] // sum(loads)))
    least = 1 if total - largest >= amount - 1 else 0
    given, rest = [largest] + [least] * (amount - 1), total - largest - least * (amount - 1)
    while rest > 0:
        candidates = [i for i in range(1, amount) if given[i] < largest] or [i for i in range(1, amount) if given[i] < reach]
        pool, budget = sum([loads[i] for i in candidates]), rest
        for i in candidates:
            extra = min(reach - given[i], max(1, budget * loads[i] // pool), rest)
            given[i] = given[i] + extra
            rest = rest - extra
    return np.array(given)


def scatter_about(stream_key, shape, width, reach, cuts=(), held_as=jnp.bfloat16):
    array = jax.random.normal(stream_key, shape, jnp.float32) * width
    if len(cuts) > 0:
        array = shard_levels(stream_key, shape, cuts, -0.22, 0.18) * array
    return jnp.clip(array, min=-reach, max=reach).astype(held_as)


def setup_inputs(seed: int = 0) -> dict:
    key_of = jax.random.split(jax.random.key(seed), 10)
    exposure = scatter_about(key_of[0], (VISITS, EXP_ROWS, EXP_COLS), 1.0, 6.0, ((0, 4), (1, 32)))
    row_bases = scatter_about(key_of[1], (BASES, KSIZE), KSIZE ** -0.5, 1.0)
    col_bases = scatter_about(key_of[2], (BASES, KSIZE), KSIZE ** -0.5, 1.0)
    coefficients = scatter_about(key_of[3], (VISITS, N_TILE, BLK_COLS, BASES), 0.2, 1.2, ((0, 4), (1, 32)), jnp.float32)
    warp_rows = draw_warp_rows(jax.random.fold_in(key_of[9], 71), 0)
    warp_cols = draw_warp_cols(jax.random.fold_in(key_of[9], 71), 0)
    variance = jnp.clip(jnp.exp(math.log(4.0) - 2.7725887 * jax.random.uniform(key_of[6], (VISITS, N_TILE, BLK_COLS), jnp.float32) ** shard_levels(key_of[6], (VISITS, N_TILE, BLK_COLS), ((0, 4), (1, 32)), -0.2, 0.2)), 0.25, 4.0)
    footprint_keys = jax.random.split(jax.random.fold_in(key_of[7], 1), VISITS * N_TILE * BLK_COLS // BLK_COLS)
    footprint_turns = jax.random.permutation(jax.random.fold_in(key_of[7], 3), VISITS * N_TILE * BLK_COLS // BLK_COLS)
    footprint = jax.vmap(lambda own, number: assign_block(jax.random.fold_in(key_of[7], 2), own, number, BLK_COLS, N_TILE, 1, CAP, 2))(footprint_keys, footprint_turns).reshape((VISITS, N_TILE, BLK_COLS, 1))
    slot_index = set_ends(jax.random.randint(key_of[8], (VISITS, N_TILE, BLK_COLS), 0, SLOTS), jax.random.fold_in(key_of[8], 1), 0, SLOTS - 1).astype(jnp.int32)
    return dict(exposure=exposure, row_bases=row_bases, col_bases=col_bases, coefficients=coefficients, warp_rows=warp_rows, warp_cols=warp_cols, variance=variance, footprint=footprint, slot_index=slot_index)


def banded(tap_table, rows_out, rows_in):
    tap_total = tap_table.shape[-1]
    grid_shape = (tap_total, rows_out, rows_in)
    offset = lax.broadcasted_iota(jnp.int32, grid_shape, 2) - lax.broadcasted_iota(jnp.int32, grid_shape, 1)
    tap_index = lax.broadcasted_iota(jnp.int32, grid_shape, 0)
    selector = (offset == tap_index).astype(jnp.float32)
    return jnp.einsum('kt,toi->koi', tap_table.astype(jnp.float32), selector).astype(jnp.bfloat16)


def match_strip(padded, vertical, block_coefficients, col_bases):
    basis_count, tap_count = col_bases.shape
    block_side = vertical.shape[1]
    span = vertical.shape[2]
    group_total = block_coefficients.shape[0] // 4

    def one_group(group_id):
        portion = lax.dynamic_slice_in_dim(padded, group_id * 4 * block_side, 3 * block_side + span, 1)
        vertical_pass = jnp.einsum('kor,rc->koc', vertical.astype(jnp.float32), portion.astype(jnp.float32)).astype(jnp.bfloat16)
        windows = jnp.stack([vertical_pass[:, :, column * block_side: column * block_side + span] for column in range(4)], 2)
        weights = lax.dynamic_slice_in_dim(block_coefficients, group_id * 4, 4, 0)
        kernels = (weights[:, :, None] * col_bases.astype(jnp.float32)[None]).astype(jnp.bfloat16)
        across = banded(kernels.reshape(4 * basis_count, tap_count), block_side, span).reshape(4, basis_count, block_side, span)
        return jnp.einsum('kobw,bkcw->boc', windows.astype(jnp.float32), across.astype(jnp.float32)).astype(jnp.bfloat16)

    return lax.map(one_group, jnp.arange(group_total, dtype=jnp.int32)).reshape(-1, block_side, block_side)


def reference(exposure, row_bases, col_bases, coefficients, warp_rows, warp_cols, variance, footprint, slot_index):
    half_reach = KSIZE // 2
    vertical = banded(row_bases, BLOCK, BLOCK + 2 * half_reach)
    padded = jnp.pad(exposure, ((0, 0), (half_reach, half_reach), (half_reach, half_reach)))

    def one_row(flat_index):
        which_visit = flat_index // N_TILE
        block_row = flat_index % N_TILE
        strip_rows = lax.dynamic_slice(padded, (which_visit, block_row * BLOCK, jnp.int32(0)), (1, BLOCK + 2 * half_reach, EXP_COLS + 2 * half_reach))[0]
        matched = match_strip(strip_rows, vertical, coefficients[which_visit, block_row], col_bases)
        across = jnp.einsum('bor,brc->boc', warp_rows[which_visit, block_row].astype(jnp.float32), matched.astype(jnp.float32)).astype(jnp.bfloat16)
        return jnp.einsum('boc,bpc->bop', across.astype(jnp.float32), warp_cols[which_visit, block_row].astype(jnp.float32)).astype(jnp.bfloat16)

    warped = lax.map(one_row, jnp.arange(VISITS * N_TILE, dtype=jnp.int32)).reshape(-1, BLOCK, BLOCK)
    weight = (1.0 / variance).astype(jnp.bfloat16).astype(jnp.float32).reshape(-1)
    targets = (footprint[..., 0] * SLOTS + slot_index).reshape(-1).astype(jnp.int32)
    weighted = weight[:, None, None] * warped.astype(jnp.float32)
    numerator = jax.ops.segment_sum(weighted, targets, TILES * N_SRC * N_SRC)
    denominator = jax.ops.segment_sum(weight, targets, TILES * N_SRC * N_SRC)
    sub_blocks = numerator / jnp.maximum(denominator, 1.0)[:, None, None]
    shaped = sub_blocks.reshape(TILES, N_SRC, N_SRC, BLOCK, BLOCK).transpose(0, 1, 3, 2, 4)
    return shaped.reshape(TILES, TILE, TILE)
```

```python
import functools

import jax
import jax.numpy as jnp
import numpy as np
from jax import lax
from jax.experimental import pallas as pl
from jax.experimental.pallas import tpu as pltpu
from jax.sharding import PartitionSpec as P

TILES_DEV = 4


HALO = 32
GROUP = 8
SPAN = 128


def halo_rows(exposure, width):
    count, length = lax.axis_size("tile"), exposure.shape[0]
    up = [(i, i + 1) for i in range(count - 1)]
    down = [(j, i) for i, j in up]
    before = lax.ppermute(exposure[length - width :], "tile", up)
    after = lax.ppermute(exposure[:width], "tile", down)
    return before, after


def wave_tables(taps, side, tall, wide, frame, skip):
    low, lanes = -(-(tall // 2 + 1) // 16) * 16, SPAN
    u, v = np.arange(low), np.arange(lanes)
    keep_u, keep_v = u <= tall // 2, v <= wide // 2
    twice_u = np.where((u == 0) | (2 * u == tall), 1.0, 2.0) * keep_u
    twice_v = np.where((v == 0) | (2 * v == wide), 1.0, 2.0) * keep_v
    turn = lambda one, other, length: 2.0 * np.pi / length * (np.outer(one, other) % length)
    place = np.arange(frame) - skip
    down = turn(u, place, tall)
    used = (place >= 0) & (place < side + taps - 1)
    rows_in = np.concatenate([np.cos(down), np.sin(down)]) * np.tile(keep_u, 2)[:, None] * used
    back = turn(np.arange(side), u, tall)
    rows_out = np.concatenate([np.cos(back) * twice_u, -np.sin(back) * twice_u], axis=1) / tall
    along = turn(np.arange(2 * side), v, wide)
    inside = (np.arange(2 * side) < wide)[:, None]
    cols_in = np.concatenate([np.cos(along), -np.sin(along)], axis=1) * inside * np.tile(keep_v, 2)
    front = turn(v, np.arange(side), wide)
    cols_out = np.concatenate([np.cos(front), -np.sin(front)]) * np.tile(twice_v, 2)[:, None] / wide
    tap_u, tap_v = turn(u, np.arange(taps), tall), turn(np.arange(taps), v, wide)
    row_taps = np.concatenate([np.cos(tap_u), np.sin(tap_u)]) * np.tile(keep_u, 2)[:, None]
    col_taps = np.concatenate([np.cos(tap_v), np.sin(tap_v)], axis=1) * np.tile(keep_v, 2)
    narrow = lambda table: jnp.asarray(table, jnp.bfloat16)
    exact = lambda table: jnp.asarray(table, jnp.float32)
    return (
        narrow(rows_in), narrow(rows_out), narrow(cols_in), narrow(cols_out),
        exact(row_taps), exact(col_taps),
    )


MESH = pl.DeviceIdType.MESH
LINE, CORES = 4, 2
PARTS = 4
WEIGHT_UNIT = 512.0


def greet(sides):
    barrier = pltpu.get_barrier_semaphore()
    for axis, count, me in sides:
        for hop in range(1, count):
            pl.semaphore_signal(
                barrier, inc=1, device_id={axis: lax.rem(me + hop, count)}, device_id_type=MESH
            )
    return barrier, sum(count - 1 for _, count, _ in sides)


def receiver(me, hop, count):
    turn = lax.rem(hop + 1, count)
    pair = turn // CORES
    dx = lax.rem(pair, LINE)
    dz = lax.rem(pair // LINE + pair, LINE)
    z, x, core = me // (LINE * CORES), lax.rem(me // CORES, LINE), lax.rem(me, CORES)
    sign = 1 - 2 * core
    z, x = lax.rem(z + sign * dz + LINE, LINE), lax.rem(x + sign * dx + LINE, LINE)
    core = lax.rem(core + turn, CORES)
    return (z * LINE + x) * CORES + core


def hop_to(owner, me, count):
    split = lambda index: (index // (LINE * CORES), index // CORES % LINE, index % CORES)
    (z, x, core), (my_z, my_x, my_core) = split(owner), split(me)
    sign = 1 - 2 * my_core
    dz, dx, dc = sign * (z - my_z) % LINE, sign * (x - my_x) % LINE, (core - my_core) % CORES
    turn = CORES * (LINE * ((dz - dx) % LINE) + dx) + dc
    return (turn + count - 1) % count


def lay_image(reach, before, exposure, after, image):
    columns = exposure.shape[1]
    tiles = 4
    wide = tiles * SPAN

    def rows(begin, width):
        return jnp.concatenate(
            [ref[:, pl.ds(begin, width)] for ref in (before, exposure, after)], axis=0
        )

    def store(number, old):
        moved = old[:, SPAN - reach : SPAN - reach + wide]
        for tile in range(tiles):
            image[number * tiles + tile] = moved[:, tile * SPAN : (tile + 1) * SPAN]

    def piece(number, carry):
        begin = pl.multiple_of(number * wide, wide)
        store(number, rows(pl.multiple_of(begin - SPAN, SPAN), wide + SPAN))
        return carry

    zeros = jnp.zeros((image.shape[1], SPAN), image.dtype)
    store(0, jnp.concatenate([zeros, rows(0, wide)], axis=1))
    lax.fori_loop(1, columns // wide, piece, 0)
    last = jnp.concatenate([rows(columns - SPAN, SPAN), zeros], axis=1)
    image[columns // SPAN] = last[:, SPAN - reach : 2 * SPAN - reach]


def match_group(
    step, order, rows_in, rows_out, cols_in, cols_out, row_wave, col_wave, coef_ref,
    image, rows_ref, cols_ref, spectrum, response, waves, warped,
):
    low, frame = rows_in.shape[0] // 2, rows_in.shape[1]
    side = warped.shape[1]
    numbers = [order[step * GROUP + q] for q in range(GROUP)]
    strips = [jnp.concatenate([image[number], image[number + 1]], axis=1) for number in numbers]
    spectrum[...] = jnp.dot(
        jnp.concatenate(strips, axis=0), cols_in[...], preferred_element_type=jnp.float32
    ).astype(jnp.bfloat16)
    scaled = [
        (row_wave[...] * coef_ref[number]).astype(jnp.bfloat16) for number in numbers
    ]
    response[...] = jnp.dot(
        jnp.concatenate(scaled, axis=0), col_wave[...], preferred_element_type=jnp.float32
    )
    for q in range(GROUP):
        both = jnp.dot(
            rows_in[...], spectrum[q * frame : (q + 1) * frame, :], preferred_element_type=jnp.float32
        )
        p_re, p_im, q_re, q_im = both[:low, :SPAN], both[:low, SPAN:], both[low:, :SPAN], both[low:, SPAN:]
        start = q * 2 * low
        a_re, a_im = response[start : start + low, :SPAN], response[start : start + low, SPAN:]
        b_re, b_im = (
            response[start + low : start + 2 * low, :SPAN],
            response[start + low : start + 2 * low, SPAN:],
        )
        even_re = p_re * a_re - p_im * a_im + q_re * b_re - q_im * b_im
        even_im = p_re * a_im + p_im * a_re + q_re * b_im + q_im * b_re
        odd_re = p_re * b_re - p_im * b_im - q_re * a_re + q_im * a_im
        odd_im = p_re * b_im + p_im * b_re - q_re * a_im - q_im * a_re
        stacked = jnp.concatenate(
            [
                jnp.concatenate([even_re, even_im], axis=1),
                jnp.concatenate([odd_re, odd_im], axis=1),
            ],
            axis=0,
        ).astype(jnp.bfloat16)
        waves[q * side : (q + 1) * side, :] = jnp.dot(
            rows_out[...], stacked, preferred_element_type=jnp.float32
        ).astype(jnp.bfloat16)
    matched = jnp.dot(waves[...], cols_out[...], preferred_element_type=jnp.float32).astype(
        jnp.bfloat16
    )
    for q in range(GROUP):
        across = jnp.dot(
            rows_ref[numbers[q]],
            matched[q * side : (q + 1) * side],
            preferred_element_type=jnp.float32,
        ).astype(jnp.bfloat16)
        warped[step * GROUP + q] = lax.dot_general(
            across,
            cols_ref[numbers[q]],
            (((1,), (1,)), ((), ())),
            preferred_element_type=jnp.float32,
        ).astype(jnp.bfloat16)


def slot_order(label_in, table_int, table_float, weight_sum, slots):
    labels = label_in[0]
    for source in range(1, label_in.shape[0]):
        labels = labels + label_in[source]
    places = labels.shape[1]
    square = (places, places)
    down, along = (lax.broadcasted_iota(jnp.int32, square, axis) for axis in (0, 1))
    slot_along = jnp.broadcast_to(labels[1:2], square)
    weight_along = jnp.broadcast_to(labels[0:1].astype(jnp.float32) / WEIGHT_UNIT, square)
    slot_down, weight_down = slot_along.T, weight_along.T
    ahead = (slot_along < slot_down) | ((slot_along == slot_down) & (along < down))
    rank = jnp.sum(ahead.astype(jnp.int32), axis=1, keepdims=True)
    chosen = rank == along
    order = jnp.sum(jnp.where(chosen, down, 0), axis=0, keepdims=True)
    slot = jnp.sum(jnp.where(chosen, slot_down, 0), axis=0, keepdims=True)
    weight = jnp.sum(jnp.where(chosen, weight_down, 0.0), axis=0, keepdims=True)
    goes_on = ((slot == pltpu.roll(slot, 1, axis=1)) & (along[:1] > 0)).astype(jnp.float32)
    up_to = jnp.sum((slot_down <= along).astype(jnp.int32), axis=0, keepdims=True)
    inside = jnp.sum((slot_down == along).astype(jnp.int32), axis=0, keepdims=True)
    last = jnp.maximum(up_to - 1, 0)
    table_int[...] = jnp.concatenate([order, last] + [order] * (table_int.shape[0] - 2), axis=0)
    table_float[...] = jnp.concatenate(
        [weight, goes_on, (inside > 0).astype(jnp.float32)] + [weight] * (table_float.shape[0] - 3),
        axis=0,
    )
    mine = jnp.where(slot_along[:slots] == down[:slots], weight_along[:slots], 0.0)
    weight_sum[...] = jnp.broadcast_to(jnp.sum(mine, axis=1, keepdims=True), (slots, places))


def coadd_kernel(
    reach, capacity, order, source, before, exposure, after, labels, rows_in, rows_out, cols_in,
    cols_out, row_wave, col_wave, coef_ref, rows_hbm, cols_hbm, coadd,
    image, spectrum, response, waves, warped, rows_ref, cols_ref,
    outgoing, label_in, table_int, table_float, weight_sum, weight_in, scale, running,
    int_smem, float_smem,
    send_sem, recv_sem, label_send, label_recv, load_sem, table_sem,
    sum_send, sum_recv, weight_send, weight_recv, *pieces,
):
    parts = len(pieces) // 3
    arrived, partial, gathered = pieces[:parts], pieces[parts : 2 * parts], pieces[2 * parts :]
    me, my_src = lax.axis_index("tile"), lax.axis_index("src")
    blocks, side = warped.shape[:2]
    count, peers = outgoing.shape[1], partial[0].shape[0]
    high = side // parts
    tiles, across = coadd.shape[0], peers
    barrier, greetings = greet((("tile", count, me), ("src", peers, my_src)))
    loads = [
        pltpu.make_async_copy(rows_hbm, rows_ref, load_sem.at[0]),
        pltpu.make_async_copy(cols_hbm, cols_ref, load_sem.at[1]),
    ]
    for load in loads:
        load.start()
    warped[...] = jnp.zeros_like(warped)
    lay_image(reach, before, exposure, after, image)
    for load in loads:
        load.wait()
    pl.semaphore_wait(barrier, greetings)

    def label_message(hop):
        return pltpu.make_async_remote_copy(
            src_ref=labels.at[hop],
            dst_ref=label_in.at[me],
            send_sem=label_send.at[hop],
            recv_sem=label_recv.at[hop],
            device_id={"tile": receiver(me, hop, count)},
            device_id_type=MESH,
        )

    def message(part, hop):
        return pltpu.make_async_remote_copy(
            src_ref=outgoing.at[part, hop],
            dst_ref=arrived[part].at[pl.ds(me * capacity, capacity)],
            send_sem=send_sem.at[part, hop],
            recv_sem=recv_sem.at[part, hop],
            device_id={"tile": receiver(me, hop, count)},
            device_id_type=MESH,
        )

    def each_hop(begin, end, act):
        def one(hop, carry):
            act(hop)
            return carry

        lax.fori_loop(begin, end, one, 0)

    def piece(hop, r, part):
        return warped[source[hop * capacity + r], part * high : (part + 1) * high, :]

    def send(part, hop):
        for r in range(capacity):
            outgoing[part, hop, r] = piece(hop, r, part)
        message(part, hop).start()

    ready = GROUP // capacity
    steps = blocks // GROUP
    each_hop(0, count - 1, lambda hop: label_message(hop).start())

    def group(step, carry):
        match_group(
            step, order, rows_in, rows_out, cols_in, cols_out, row_wave, col_wave, coef_ref,
            image, rows_ref, cols_ref, spectrum, response, waves, warped,
        )
        for hop in range(ready):
            for part in range(parts):
                send(part, step * ready + hop)
        return carry

    lax.fori_loop(0, steps, group, 0)
    for part in range(parts):
        each_hop(steps * ready, count - 1, lambda hop, part=part: send(part, hop))
        for r in range(capacity):
            arrived[part][me * capacity + r] = piece(count - 1, r, part)

    label_in[me] = labels[count - 1]
    each_hop(0, count - 1, lambda hop: label_message(hop).wait())
    slot_order(label_in, table_int, table_float, weight_sum, tiles * across * across)
    moves = [
        pltpu.make_async_copy(table_int, int_smem, table_sem.at[0]),
        pltpu.make_async_copy(table_float, float_smem, table_sem.at[1]),
    ]
    for move in moves:
        move.start()

    def to_peer(hop, from_ref, to_ref, send_sem, recv_sem):
        return pltpu.make_async_remote_copy(
            src_ref=from_ref,
            dst_ref=to_ref,
            send_sem=send_sem,
            recv_sem=recv_sem,
            device_id={"src": lax.rem(my_src + hop, peers)},
            device_id_type=MESH,
        )

    def weight_message(hop):
        return to_peer(
            hop, weight_sum, weight_in.at[hop - 1], weight_send.at[hop - 1], weight_recv.at[hop - 1]
        )

    def sum_message(part, hop):
        return to_peer(
            hop,
            partial[part].at[lax.rem(my_src + hop, peers)],
            gathered[part].at[hop - 1],
            sum_send.at[part, hop - 1],
            sum_recv.at[part, hop - 1],
        )

    for hop in range(1, peers):
        weight_message(hop).start()
    for move in moves:
        move.wait()

    def stack(part):
        def add(place, total):
            block = arrived[part][int_smem[0, place]].astype(jnp.float32)
            total = total * float_smem[1, place] + float_smem[0, place] * block
            running[place] = total
            return total

        lax.fori_loop(
            0, arrived[part].shape[0], add, jnp.zeros((high, side), jnp.float32), unroll=4
        )

        def take(slot, carry):
            row = lax.rem(slot // across, across)
            place = slot // (across * across) * across + lax.rem(slot, across)
            total = running[int_smem[1, slot]] * float_smem[2, slot]
            partial[part][row, place] = total.astype(jnp.bfloat16)
            return carry

        lax.fori_loop(0, tiles * across * across, take, 0, unroll=4)

    def finish(part):
        for hop in range(1, peers):
            sum_message(part, hop).wait()
        for tile in range(tiles):
            for column in range(across):
                place = tile * across + column
                total = partial[part][my_src, place].astype(jnp.float32)
                for hop in range(peers - 1):
                    total = total + gathered[part][hop, place].astype(jnp.float32)
                slot = (tile * across + my_src) * across + column
                coadd[
                    tile, part * high : (part + 1) * high, column * side : (column + 1) * side
                ] = total * scale[slot]

    for part in range(parts):
        each_hop(0, count - 1, lambda hop, part=part: message(part, hop).wait_recv())
        stack(part)
        for hop in range(1, peers):
            sum_message(part, hop).start()
        if part == 0:
            for hop in range(1, peers):
                weight_message(hop).wait()
            weight = weight_sum[...]
            for hop in range(peers - 1):
                weight = weight + weight_in[hop]
            factor = 1.0 / jnp.maximum(weight, 1.0)
            for slot in range(scale.shape[0]):
                scale[slot] = factor[slot : slot + 1]
        else:
            finish(part - 1)
    finish(parts - 1)
    for part in range(parts):
        each_hop(0, count - 1, lambda hop, part=part: message(part, hop).wait_send())


def coadd_tiles(
    exposure, row_bases, col_bases, coefficients, warp_rows, warp_cols, order, source, labels, capacity
):
    before, after = halo_rows(exposure, HALO)
    blocks, side = warp_rows.shape[:2]
    count, tall_label, places = labels.shape
    peers = lax.axis_size("src")
    slots = TILES_DEV * peers * peers
    basis_count, taps = row_bases.shape
    columns = exposure.shape[1]
    reach = taps // 2
    frame = side + 2 * HALO
    tall = -(-(side + taps - 1) // 16) * 16
    rows_in, rows_out, cols_in, cols_out, row_taps, col_taps = wave_tables(
        taps, side, tall, side + taps - 1, frame, HALO - reach
    )
    spare = SPAN - basis_count
    exact = lax.Precision.HIGHEST
    row_wave = jnp.dot(
        row_taps, jnp.pad(row_bases.astype(jnp.float32).T, ((0, 0), (0, spare))), precision=exact
    )
    col_wave = jnp.dot(
        jnp.pad(col_bases.astype(jnp.float32), ((0, spare), (0, 0))), col_taps, precision=exact
    ).astype(jnp.bfloat16)
    padded_coefficients = jnp.pad(coefficients, ((0, 0), (0, spare)))[:, None, :]
    near, far = pl.BlockSpec(memory_space=pltpu.VMEM), pl.BlockSpec(memory_space=pl.ANY)
    table = pl.BlockSpec(memory_space=pltpu.SMEM)
    high = side // PARTS
    per = slots // peers
    narrow, dma = jnp.bfloat16, pltpu.SemaphoreType.DMA
    return pl.pallas_call(
        functools.partial(coadd_kernel, reach, capacity),
        in_specs=[table, table] + [near] * 11 + [far, far],
        out_specs=near,
        out_shape=jax.ShapeDtypeStruct((TILES_DEV, side, peers * side), jnp.float32),
        scratch_shapes=[
            pltpu.VMEM((columns // SPAN + 1, frame, SPAN), narrow),
            pltpu.VMEM((GROUP * frame, 2 * SPAN), narrow),
            pltpu.VMEM((GROUP * rows_in.shape[0], 2 * SPAN), jnp.float32),
            pltpu.VMEM((GROUP * side, 2 * SPAN), narrow),
            pltpu.VMEM((blocks, side, side), narrow),
            pltpu.VMEM((blocks, side, side), narrow),
            pltpu.VMEM((blocks, side, side), narrow),
            pltpu.VMEM((PARTS, count, capacity, high, side), narrow),
            pltpu.VMEM(labels.shape, jnp.int32),
            pltpu.VMEM((tall_label, places), jnp.int32),
            pltpu.VMEM((tall_label, places), jnp.float32),
            pltpu.VMEM((slots, places), jnp.float32),
            pltpu.VMEM((peers - 1, slots, places), jnp.float32),
            pltpu.VMEM((slots, 1, places), jnp.float32),
            pltpu.VMEM((count * capacity, high, side), jnp.float32),
            pltpu.SMEM((tall_label, places), jnp.int32),
            pltpu.SMEM((tall_label, places), jnp.float32),
            dma((PARTS, count)),
            dma((PARTS, count)),
            dma((count,)),
            dma((count,)),
            dma((2,)),
            dma((2,)),
            dma((PARTS, peers - 1)),
            dma((PARTS, peers - 1)),
            dma((peers - 1,)),
            dma((peers - 1,)),
            *[pltpu.VMEM((count * capacity, high, side), narrow) for _ in range(PARTS)],
            *[pltpu.VMEM((peers, per, high, side), narrow) for _ in range(PARTS)],
            *[pltpu.VMEM((peers - 1, per, high, side), narrow) for _ in range(PARTS)],
        ],
        compiler_params=pltpu.CompilerParams(
            collective_id=0, has_side_effects=True, vmem_limit_bytes=50 * 1024 * 1024
        ),
        cost_estimate=pl.CostEstimate(flops=4 << 30, bytes_accessed=10 << 20, transcendentals=0),
    )(
        order, source, before, exposure, after, labels, rows_in, rows_out, cols_in, cols_out,
        row_wave, col_wave, padded_coefficients, warp_rows, warp_cols,
    )


def route(owner, count, capacity):
    blocks = owner.shape[0]
    hop = hop_to(owner, lax.axis_index("tile"), count)
    square = (blocks, blocks)
    number = lax.broadcasted_iota(jnp.int32, square, 1)
    earlier = number < lax.broadcasted_iota(jnp.int32, square, 0)
    same, before = hop[:, None] == hop[None, :], hop[None, :] < hop[:, None]
    rank = jnp.sum((same & earlier).astype(jnp.int32), axis=1)
    position = rank + jnp.sum(before.astype(jnp.int32), axis=1)
    order = jnp.sum(
        jnp.where(lax.broadcasted_iota(jnp.int32, square, 0) == position[None, :], number, 0), axis=1
    )
    place = hop * capacity + rank
    found = lax.broadcasted_iota(jnp.int32, (count * capacity, blocks), 0) == place[None, :]
    source = jnp.sum(jnp.where(found, position[None, :], 0), axis=1)
    return order, source, found


def body(
    exposure,
    row_bases,
    col_bases,
    coefficients,
    warp_rows,
    warp_cols,
    variance,
    footprint,
    slot_index,
):
    count = lax.axis_size("tile")
    blocks = warp_rows.shape[2]
    capacity = max(2, 2 * blocks // count)
    order, source, found = route(footprint[0, 0, :, 0], count, capacity)
    weight = (1.0 / variance[0, 0]).astype(jnp.bfloat16).astype(jnp.float32)
    units = (weight * WEIGHT_UNIT).astype(jnp.int32)
    fields = [
        jnp.sum(jnp.where(found, values[None, :], 0), axis=1).reshape(count, capacity)
        for values in (units, slot_index[0, 0])
    ]
    labels = jnp.stack([jnp.tile(field, (1, count)) for field in fields], axis=1)
    mine = lax.broadcasted_iota(jnp.int32, labels.shape, 2) // capacity == lax.axis_index("tile")
    labels = jnp.pad(jnp.where(mine, labels, 0), ((0, 0), (0, 6), (0, 0)))
    return coadd_tiles(
        exposure[0], row_bases, col_bases, coefficients[0, 0], warp_rows[0, 0], warp_cols[0, 0],
        order, source, labels, capacity,
    )


def solution(mesh):
    placed = (
        P("src", "tile", None),
        P(),
        P(),
        P("src", "tile", None, None),
        P("src", "tile", None, None, None),
        P("src", "tile", None, None, None),
        P("src", "tile", None),
        P("src", "tile", None, None),
        P("src", "tile", None),
    )
    return jax.shard_map(
        body, mesh=mesh, in_specs=placed, out_specs=P("tile", "src", None), check_vma=False
    )
```

```python
import functools

import jax
import jax.numpy as jnp
import numpy as np
from jax import lax
from jax.experimental import pallas as pl
from jax.experimental.pallas import tpu as pltpu
from jax.sharding import PartitionSpec as P

TILES_DEV = 4


HALO = 32
GROUP = 8
SPAN = 128


def wave_tables(taps, side, tall, wide, frame, skip):
    low, lanes = -(-(tall // 2 + 1) // 16) * 16, SPAN
    u, v = np.arange(low), np.arange(lanes)
    keep_u, keep_v = u <= tall // 2, v <= wide // 2
    twice_u = np.where((u == 0) | (2 * u == tall), 1.0, 2.0) * keep_u
    twice_v = np.where((v == 0) | (2 * v == wide), 1.0, 2.0) * keep_v
    turn = lambda one, other, length: 2.0 * np.pi / length * (np.outer(one, other) % length)
    place = np.arange(frame) - skip
    down = turn(u, place, tall)
    used = (place >= 0) & (place < side + taps - 1)
    rows_in = np.concatenate([np.cos(down), np.sin(down)]) * np.tile(keep_u, 2)[:, None] * used
    back = turn(np.arange(side), u, tall)
    rows_out = np.concatenate([np.cos(back) * twice_u, -np.sin(back) * twice_u], axis=1) / tall
    along = turn(np.arange(2 * side), v, wide)
    inside = (np.arange(2 * side) < wide)[:, None]
    cols_in = np.concatenate([np.cos(along), -np.sin(along)], axis=1) * inside * np.tile(keep_v, 2)
    front = turn(v, np.arange(side), wide)
    cols_out = np.concatenate([np.cos(front), -np.sin(front)]) * np.tile(twice_v, 2)[:, None] / wide
    tap_u, tap_v = turn(u, np.arange(taps), tall), turn(np.arange(taps), v, wide)
    row_taps = np.concatenate([np.cos(tap_u), np.sin(tap_u)]) * np.tile(keep_u, 2)[:, None]
    col_taps = np.concatenate([np.cos(tap_v), np.sin(tap_v)], axis=1) * np.tile(keep_v, 2)
    places, rows = [], []
    for table in (rows_in, rows_out, cols_in, cols_out, row_taps, col_taps):
        places.append((sum(part.shape[0] for part in rows), *table.shape))
        rows.append(np.pad(table, ((0, -table.shape[0] % 16), (0, 2 * side - table.shape[1]))))
    return jnp.asarray(np.concatenate(rows), jnp.float32), places


MESH = pl.DeviceIdType.MESH
LINE, CORES = 4, 2
PARTS = 4
WEIGHT_UNIT = 512.0


def greet(sides):
    barrier = pltpu.get_barrier_semaphore()
    for axis, count, me in sides:
        for hop in range(1, count):
            pl.semaphore_signal(
                barrier, inc=1, device_id={axis: lax.rem(me + hop, count)}, device_id_type=MESH
            )
    return barrier, sum(count - 1 for _, count, _ in sides)


def receiver(me, hop, count):
    turn = lax.rem(hop + 1, count)
    pair = turn // CORES
    dx = lax.rem(pair, LINE)
    dz = lax.rem(pair // LINE + pair, LINE)
    z, x, core = me // (LINE * CORES), lax.rem(me // CORES, LINE), lax.rem(me, CORES)
    sign = 1 - 2 * core
    z, x = lax.rem(z + sign * dz + LINE, LINE), lax.rem(x + sign * dx + LINE, LINE)
    core = lax.rem(core + turn, CORES)
    return (z * LINE + x) * CORES + core


def hop_to(owner, me):
    wide, line = LINE * CORES, LINE - 1
    sign = 1 - 2 * lax.rem(me, CORES)
    dz = (sign * (owner // wide - me // wide)) & line
    dx = (sign * (((owner // CORES) & line) - lax.rem(me // CORES, LINE))) & line
    dc = (owner - me) & (CORES - 1)
    turn = CORES * (LINE * ((dz - dx) & line) + dx) + dc
    return (turn - 1) & (LINE * wide - 1)


def route(me, capacity, owner_ref, slot_ref, variance_ref, route_table, fields):
    blocks, places = owner_ref.shape[1], route_table.shape[1]
    square = (blocks, blocks)
    down, along = (lax.broadcasted_iota(jnp.int32, square, axis) for axis in (0, 1))
    hop_along = jnp.broadcast_to(hop_to(owner_ref[...], me), square)
    hop_down = hop_along.T
    count = lambda mask: jnp.sum(mask.astype(jnp.int32), axis=1, keepdims=True)
    rank = count((hop_along == hop_down) & (along < down))
    position = rank + count(hop_along < hop_down)
    weight = (1.0 / variance_ref[...]).astype(jnp.bfloat16).astype(jnp.float32)
    units = (jnp.broadcast_to(weight, square).T * WEIGHT_UNIT).astype(jnp.int32)[:, :1]
    slot = jnp.broadcast_to(slot_ref[...], square).T[:, :1]
    table = (blocks, places)
    number = lax.broadcasted_iota(jnp.int32, table, 0)
    lane = lax.broadcasted_iota(jnp.int32, table, 1)
    found = lane == hop_down[:, :1] * capacity + rank
    pick = lambda mask, values: jnp.sum(jnp.where(mask, values, 0), axis=0, keepdims=True)
    order = pick(lane == position, number)
    source = pick(found, position)
    route_table[...] = jnp.concatenate([order, source] + [order] * (route_table.shape[0] - 2), axis=0)
    row = [pick(found, units), pick(found, slot)]
    fields[...] = jnp.concatenate(row + [jnp.zeros_like(row[0])] * (fields.shape[0] - 2), axis=0)


def transform_rows(reach, rows_in, before, exposure, after, strip):
    columns = exposure.shape[1]
    tiles = 4
    wide = tiles * SPAN

    def rows(begin, width):
        return jnp.concatenate(
            [ref[:, pl.ds(begin, width)] for ref in (before, exposure, after)], axis=0
        )

    def spectra(window):
        return jnp.dot(rows_in[...], window, preferred_element_type=jnp.float32).astype(strip.dtype)

    def store(number, old):
        moved = spectra(old[:, SPAN - reach : SPAN - reach + wide])
        for tile in range(tiles):
            strip[number * tiles + tile] = moved[:, tile * SPAN : (tile + 1) * SPAN]

    def piece(number, carry):
        begin = pl.multiple_of(number * wide, wide)
        store(number, rows(pl.multiple_of(begin - SPAN, SPAN), wide + SPAN))
        return carry

    zeros = jnp.zeros((rows_in.shape[1], SPAN), exposure.dtype)
    store(0, jnp.concatenate([zeros, rows(0, wide)], axis=1))
    lax.fori_loop(1, columns // wide, piece, 0)
    last = jnp.concatenate([rows(columns - SPAN, SPAN), zeros], axis=1)
    strip[columns // SPAN] = spectra(last[:, SPAN - reach : 2 * SPAN - reach])


def match_group(
    step, route_smem, rows_out, cols_in, cols_out, row_wave, col_wave, coef_ref,
    strip, rows_ref, cols_ref, spectrum, response, warps, waves, warped,
):
    low = row_wave.shape[0] // 2
    side = warped.shape[1]
    numbers = [route_smem[0, step * GROUP + q] for q in range(GROUP)]
    windows = [jnp.concatenate([strip[number], strip[number + 1]], axis=1) for number in numbers]
    spectrum[...] = jnp.dot(
        jnp.concatenate(windows, axis=0), cols_in[...], preferred_element_type=jnp.float32
    )
    scaled = [(row_wave[...] * coef_ref[number]).astype(jnp.bfloat16) for number in numbers]
    response[...] = jnp.dot(
        jnp.concatenate(scaled, axis=0), col_wave[...], preferred_element_type=jnp.float32
    )
    warps[...] = jnp.dot(
        jnp.concatenate([rows_ref[number] for number in numbers], axis=0),
        rows_out[...],
        preferred_element_type=jnp.float32,
    ).astype(jnp.bfloat16)
    for q in range(GROUP):
        top = slice(q * 2 * low, q * 2 * low + low)
        end = slice(q * 2 * low + low, (q + 1) * 2 * low)
        p_re, p_im = spectrum[top, :SPAN], spectrum[top, SPAN:]
        q_re, q_im = spectrum[end, :SPAN], spectrum[end, SPAN:]
        a_re, a_im = response[top, :SPAN], response[top, SPAN:]
        b_re, b_im = response[end, :SPAN], response[end, SPAN:]
        even_re = p_re * a_re - p_im * a_im + q_re * b_re - q_im * b_im
        even_im = p_re * a_im + p_im * a_re + q_re * b_im + q_im * b_re
        odd_re = p_re * b_re - p_im * b_im - q_re * a_re + q_im * a_im
        odd_im = p_re * b_im + p_im * b_re - q_re * a_im - q_im * a_re
        stacked = jnp.concatenate(
            [
                jnp.concatenate([even_re, even_im], axis=1),
                jnp.concatenate([odd_re, odd_im], axis=1),
            ],
            axis=0,
        ).astype(jnp.bfloat16)
        waves[q * side : (q + 1) * side, :] = jnp.dot(
            warps[q * side : (q + 1) * side, :], stacked, preferred_element_type=jnp.float32
        ).astype(jnp.bfloat16)
    across = jnp.dot(waves[...], cols_out[...], preferred_element_type=jnp.float32).astype(
        jnp.bfloat16
    )
    for q in range(GROUP):
        warped[step * GROUP + q] = lax.dot_general(
            across[q * side : (q + 1) * side],
            cols_ref[numbers[q]],
            (((1,), (1,)), ((), ())),
            preferred_element_type=jnp.float32,
        ).astype(jnp.bfloat16)


def slot_order(label_in, table_int, table_float, weight_sum, slots):
    labels = label_in[0]
    for source in range(1, label_in.shape[0]):
        labels = labels + label_in[source]
    places = labels.shape[1]
    square = (places, places)
    down, along = (lax.broadcasted_iota(jnp.int32, square, axis) for axis in (0, 1))
    slot_along = jnp.broadcast_to(labels[1:2], square)
    weight_along = jnp.broadcast_to(labels[0:1].astype(jnp.float32) / WEIGHT_UNIT, square)
    slot_down, weight_down = slot_along.T, weight_along.T
    ahead = (slot_along < slot_down) | ((slot_along == slot_down) & (along < down))
    rank = jnp.sum(ahead.astype(jnp.int32), axis=1, keepdims=True)
    chosen = rank == along
    order = jnp.sum(jnp.where(chosen, down, 0), axis=0, keepdims=True)
    slot = jnp.sum(jnp.where(chosen, slot_down, 0), axis=0, keepdims=True)
    weight = jnp.sum(jnp.where(chosen, weight_down, 0.0), axis=0, keepdims=True)
    goes_on = ((slot == pltpu.roll(slot, 1, axis=1)) & (along[:1] > 0)).astype(jnp.float32)
    up_to = jnp.sum((slot_down <= along).astype(jnp.int32), axis=0, keepdims=True)
    inside = jnp.sum((slot_down == along).astype(jnp.int32), axis=0, keepdims=True)
    last = jnp.maximum(up_to - 1, 0)
    table_int[...] = jnp.concatenate([order, last] + [order] * (table_int.shape[0] - 2), axis=0)
    table_float[...] = jnp.concatenate(
        [weight, goes_on, (inside > 0).astype(jnp.float32)] + [weight] * (table_float.shape[0] - 3),
        axis=0,
    )
    mine = jnp.where(slot_along[:slots] == down[:slots], weight_along[:slots], 0.0)
    weight_sum[...] = jnp.broadcast_to(jnp.sum(mine, axis=1, keepdims=True), (slots, places))


def coadd_kernel(
    reach, capacity, places, exposure_hbm, rows_hbm, cols_hbm, tables_hbm,
    row_bases, col_bases, coefficients, variance, owner, slot_index, coadd,
    exposure, before, after, strip, tables, wave_table, row_wave, col_wave, coef_ref,
    route_table, fields, labels,
    spectrum, response, warps, waves, warped, rows_ref, cols_ref,
    outgoing, label_in, table_int, table_float, weight_sum, weight_in, scale, running,
    route_smem, int_smem, float_smem,
    halo_send, halo_recv, send_sem, recv_sem, label_send, label_recv, load_sem, table_sem,
    sum_send, sum_recv, weight_send, weight_recv, *pieces,
):
    parts = len(pieces) // 3
    arrived, partial, gathered = pieces[:parts], pieces[parts : 2 * parts], pieces[2 * parts :]
    me, my_src = lax.axis_index("tile"), lax.axis_index("src")
    blocks, side = warped.shape[:2]
    count, peers = outgoing.shape[1], partial[0].shape[0]
    high = side // parts
    tiles, across = coadd.shape[0], peers
    barrier, greetings = greet((("tile", count, me), ("src", peers, my_src)))
    loads = [
        pltpu.make_async_copy(from_ref, to_ref, load_sem.at[number])
        for number, (from_ref, to_ref) in enumerate(
            (
                (tables_hbm, wave_table),
                (exposure_hbm, exposure),
                (rows_hbm, rows_ref),
                (cols_hbm, cols_ref),
            )
        )
    ]
    for load in loads:
        load.start()
    route(me, capacity, owner, slot_index, variance, route_table, fields)
    move = pltpu.make_async_copy(route_table, route_smem, table_sem.at[0])
    move.start()
    by_block = jnp.concatenate([coefficients[k] for k in range(coefficients.shape[0])], axis=0).T
    for number in range(blocks):
        coef_ref[number] = by_block[number : number + 1, :]
    lane = lax.broadcasted_iota(jnp.int32, fields.shape, 1)
    for hop in range(count):
        moved = pltpu.roll(
            fields[...], lax.rem((me - hop + count) * capacity, lane.shape[1]), axis=1
        )
        labels[hop] = jnp.where(lane // capacity == me, moved, 0)
    pl.semaphore_wait(barrier, greetings)

    def halo(number, begin, to_ref, neighbour):
        return pltpu.make_async_remote_copy(
            src_ref=exposure_hbm.at[pl.ds(begin, HALO)],
            dst_ref=to_ref,
            send_sem=halo_send.at[number],
            recv_sem=halo_recv.at[number],
            device_id={"tile": neighbour},
            device_id_type=MESH,
        )

    down = halo(0, side - HALO, before, lax.rem(me + 1, count))
    up = halo(1, 0, after, lax.rem(me + count - 1, count))

    @pl.when(me < count - 1)
    def _():
        down.start()

    @pl.when(me > 0)
    def _():
        up.start()

    @pl.when(me == 0)
    def _():
        before[...] = jnp.zeros_like(before)

    @pl.when(me == count - 1)
    def _():
        after[...] = jnp.zeros_like(after)

    def label_message(hop):
        return pltpu.make_async_remote_copy(
            src_ref=labels.at[hop],
            dst_ref=label_in.at[me],
            send_sem=label_send.at[hop],
            recv_sem=label_recv.at[hop],
            device_id={"tile": receiver(me, hop, count)},
            device_id_type=MESH,
        )

    def message(part, hop):
        return pltpu.make_async_remote_copy(
            src_ref=outgoing.at[part, hop],
            dst_ref=arrived[part].at[pl.ds(me * capacity, capacity)],
            send_sem=send_sem.at[part, hop],
            recv_sem=recv_sem.at[part, hop],
            device_id={"tile": receiver(me, hop, count)},
            device_id_type=MESH,
        )

    def each_hop(begin, end, act):
        def one(hop, carry):
            act(hop)
            return carry

        lax.fori_loop(begin, end, one, 0)

    def piece(hop, r, part):
        return warped[route_smem[1, hop * capacity + r], part * high : (part + 1) * high, :]

    def send(part, hop):
        for r in range(capacity):
            outgoing[part, hop, r] = piece(hop, r, part)
        message(part, hop).start()

    ready = GROUP // capacity
    steps = blocks // GROUP
    each_hop(0, count - 1, lambda hop: label_message(hop).start())
    warped[...] = jnp.zeros_like(warped)
    view = lambda ref, place: ref.at[pl.ds(place[0], place[1]), pl.ds(0, place[2])]
    rows_in, rows_out, cols_in, cols_out = (view(tables, place) for place in places[:4])
    row_taps, col_taps = (view(wave_table, place) for place in places[4:])
    loads[0].wait()
    tables[...] = wave_table[: tables.shape[0], :].astype(tables.dtype)
    row_wave[...] = lax.dot_general(
        row_taps[...],
        row_bases[...].astype(jnp.float32),
        (((1,), (1,)), ((), ())),
        precision=lax.Precision.HIGHEST,
        preferred_element_type=jnp.float32,
    )
    col_wave[...] = jnp.dot(
        col_bases[...].astype(jnp.float32),
        col_taps[...],
        precision=lax.Precision.HIGHEST,
        preferred_element_type=jnp.float32,
    ).astype(col_wave.dtype)
    for load in loads[1:]:
        load.wait()
    move.wait()

    @pl.when(me > 0)
    def _():
        down.wait_recv()

    @pl.when(me < count - 1)
    def _():
        up.wait_recv()

    transform_rows(reach, rows_in, before, exposure, after, strip)

    def group(step, carry):
        match_group(
            step, route_smem, rows_out, cols_in, cols_out, row_wave, col_wave, coef_ref,
            strip, rows_ref, cols_ref, spectrum, response, warps, waves, warped,
        )
        for hop in range(ready):
            for part in range(parts):
                send(part, step * ready + hop)
        return carry

    lax.fori_loop(0, steps, group, 0)
    for part in range(parts):
        each_hop(steps * ready, count - 1, lambda hop, part=part: send(part, hop))
        for r in range(capacity):
            arrived[part][me * capacity + r] = piece(count - 1, r, part)

    label_in[me] = labels[count - 1]
    each_hop(0, count - 1, lambda hop: label_message(hop).wait())
    slot_order(label_in, table_int, table_float, weight_sum, tiles * across * across)
    moves = [
        pltpu.make_async_copy(table_int, int_smem, table_sem.at[1]),
        pltpu.make_async_copy(table_float, float_smem, table_sem.at[2]),
    ]
    for move in moves:
        move.start()

    def to_peer(hop, from_ref, to_ref, send_sem, recv_sem):
        return pltpu.make_async_remote_copy(
            src_ref=from_ref,
            dst_ref=to_ref,
            send_sem=send_sem,
            recv_sem=recv_sem,
            device_id={"src": lax.rem(my_src + hop, peers)},
            device_id_type=MESH,
        )

    def weight_message(hop):
        return to_peer(
            hop, weight_sum, weight_in.at[hop - 1], weight_send.at[hop - 1], weight_recv.at[hop - 1]
        )

    def sum_message(part, hop):
        return to_peer(
            hop,
            partial[part].at[lax.rem(my_src + hop, peers)],
            gathered[part].at[hop - 1],
            sum_send.at[part, hop - 1],
            sum_recv.at[part, hop - 1],
        )

    for hop in range(1, peers):
        weight_message(hop).start()
    for move in moves:
        move.wait()

    def stack(part):
        def add(place, total):
            block = arrived[part][int_smem[0, place]].astype(jnp.float32)
            total = total * float_smem[1, place] + float_smem[0, place] * block
            running[place] = total
            return total

        lax.fori_loop(
            0, arrived[part].shape[0], add, jnp.zeros((high, side), jnp.float32), unroll=4
        )

        def take(slot, carry):
            row = lax.rem(slot // across, across)
            place = slot // (across * across) * across + lax.rem(slot, across)
            total = running[int_smem[1, slot]] * float_smem[2, slot]
            partial[part][row, place] = total.astype(jnp.bfloat16)
            return carry

        lax.fori_loop(0, tiles * across * across, take, 0, unroll=4)

    def finish(part):
        for hop in range(1, peers):
            sum_message(part, hop).wait()
        for tile in range(tiles):
            for column in range(across):
                place = tile * across + column
                total = partial[part][my_src, place].astype(jnp.float32)
                for hop in range(peers - 1):
                    total = total + gathered[part][hop, place].astype(jnp.float32)
                slot = (tile * across + my_src) * across + column
                coadd[
                    tile, part * high : (part + 1) * high, column * side : (column + 1) * side
                ] = total * scale[slot]

    for part in range(parts):
        each_hop(0, count - 1, lambda hop, part=part: message(part, hop).wait_recv())
        stack(part)
        for hop in range(1, peers):
            sum_message(part, hop).start()
        if part == 0:
            for hop in range(1, peers):
                weight_message(hop).wait()
            weight = weight_sum[...]
            for hop in range(peers - 1):
                weight = weight + weight_in[hop]
            factor = 1.0 / jnp.maximum(weight, 1.0)
            for slot in range(scale.shape[0]):
                scale[slot] = factor[slot : slot + 1]
        else:
            finish(part - 1)
    finish(parts - 1)
    for part in range(parts):
        each_hop(0, count - 1, lambda hop, part=part: message(part, hop).wait_send())

    @pl.when(me < count - 1)
    def _():
        down.wait_send()

    @pl.when(me > 0)
    def _():
        up.wait_send()


def body(
    exposure,
    row_bases,
    col_bases,
    coefficients,
    warp_rows,
    warp_cols,
    variance,
    footprint,
    slot_index,
):
    blocks, side = warp_rows.shape[2:4]
    columns = exposure.shape[2]
    basis_count, taps = row_bases.shape
    peers, count = lax.axis_size("src"), lax.axis_size("tile")
    capacity = max(2, 2 * blocks // count)
    slots, sends = TILES_DEV * peers * peers, count * capacity
    reach = taps // 2
    tall = -(-(side + taps - 1) // 16) * 16
    tables, places = wave_tables(
        taps, side, tall, side + taps - 1, side + 2 * HALO, HALO - reach
    )
    spectra = places[0][1]
    near, far = pl.BlockSpec(memory_space=pltpu.VMEM), pl.BlockSpec(memory_space=pl.ANY)
    high, per = side // PARTS, slots // peers
    narrow, wide, whole = jnp.bfloat16, jnp.float32, jnp.int32
    vmem, smem, dma = pltpu.VMEM, pltpu.SMEM, pltpu.SemaphoreType.DMA
    return pl.pallas_call(
        functools.partial(coadd_kernel, reach, capacity, places),
        in_specs=[far] * 4 + [near] * 6,
        out_specs=near,
        out_shape=jax.ShapeDtypeStruct((TILES_DEV, side, peers * side), wide),
        scratch_shapes=[
            vmem((side, columns), narrow),
            vmem((HALO, columns), narrow),
            vmem((HALO, columns), narrow),
            vmem((columns // SPAN + 1, spectra, SPAN), narrow),
            vmem((places[4][0], 2 * SPAN), narrow),
            vmem(tables.shape, wide),
            vmem((spectra, basis_count), wide),
            vmem((basis_count, 2 * SPAN), narrow),
            vmem((blocks, 1, basis_count), wide),
            vmem((8, sends), whole),
            vmem((8, sends), whole),
            vmem((count, 8, sends), whole),
            vmem((GROUP * spectra, 2 * SPAN), wide),
            vmem((GROUP * spectra, 2 * SPAN), wide),
            vmem((GROUP * side, spectra), narrow),
            vmem((GROUP * side, 2 * SPAN), narrow),
            vmem((blocks, side, side), narrow),
            vmem((blocks, side, side), narrow),
            vmem((blocks, side, side), narrow),
            vmem((PARTS, count, capacity, high, side), narrow),
            vmem((count, 8, sends), whole),
            vmem((8, sends), whole),
            vmem((8, sends), wide),
            vmem((slots, sends), wide),
            vmem((peers - 1, slots, sends), wide),
            vmem((slots, 1, sends), wide),
            vmem((sends, high, side), wide),
            smem((8, sends), whole),
            smem((8, sends), whole),
            smem((8, sends), wide),
            dma((2,)),
            dma((2,)),
            dma((PARTS, count)),
            dma((PARTS, count)),
            dma((count,)),
            dma((count,)),
            dma((4,)),
            dma((3,)),
            dma((PARTS, peers - 1)),
            dma((PARTS, peers - 1)),
            dma((peers - 1,)),
            dma((peers - 1,)),
            *[vmem((sends, high, side), narrow) for _ in range(PARTS)],
            *[vmem((peers, per, high, side), narrow) for _ in range(PARTS)],
            *[vmem((peers - 1, per, high, side), narrow) for _ in range(PARTS)],
        ],
        compiler_params=pltpu.CompilerParams(
            collective_id=0, has_side_effects=True, vmem_limit_bytes=60 * 1024 * 1024
        ),
        cost_estimate=pl.CostEstimate(flops=4 << 30, bytes_accessed=10 << 20, transcendentals=0),
    )(
        exposure[0], warp_rows[0, 0], warp_cols[0, 0], tables, row_bases, col_bases,
        coefficients[0].transpose(2, 0, 1), variance[0], footprint.reshape(1, blocks), slot_index[0],
    )


def solution(mesh):
    placed = (
        P("src", "tile", None),
        P(),
        P(),
        P("src", "tile", None, None),
        P("src", "tile", None, None, None),
        P("src", "tile", None, None, None),
        P("src", "tile", None),
        P("src", "tile", None, None),
        P("src", "tile", None),
    )
    return jax.shard_map(
        body, mesh=mesh, in_specs=placed, out_specs=P("tile", "src", None), check_vma=False
    )
```

```python
import functools

import jax
import jax.numpy as jnp
import numpy as np
from jax import lax
from jax.experimental import pallas as pl
from jax.experimental.pallas import tpu as pltpu
from jax.sharding import PartitionSpec as P

TILES_DEV = 4


HALO = 32
GROUP = 4
SPAN = 128


def wave_tables(taps, side, tall, wide, frame, skip):
    low, lanes = -(-(tall // 2 + 1) // 16) * 16, SPAN
    u, v = np.arange(low), np.arange(lanes)
    keep_u, keep_v = u <= tall // 2, v <= wide // 2
    twice_u = np.where((u == 0) | (2 * u == tall), 1.0, 2.0) * keep_u
    twice_v = np.where((v == 0) | (2 * v == wide), 1.0, 2.0) * keep_v
    turn = lambda one, other, length: 2.0 * np.pi / length * (np.outer(one, other) % length)
    place = np.arange(frame) - skip
    down = turn(u, place, tall)
    used = (place >= 0) & (place < side + taps - 1)
    rows_in = np.concatenate([np.cos(down), np.sin(down)]) * np.tile(keep_u, 2)[:, None] * used
    back = turn(np.arange(side), u, tall)
    rows_out = np.concatenate([np.cos(back) * twice_u, -np.sin(back) * twice_u], axis=1) / tall
    along = turn(np.arange(2 * side), v, wide)
    inside = (np.arange(2 * side) < wide)[:, None]
    cols_in = np.concatenate([np.cos(along), -np.sin(along)], axis=1) * inside * np.tile(keep_v, 2)
    front = turn(v, np.arange(side), wide)
    cols_out = np.concatenate([np.cos(front), -np.sin(front)]) * np.tile(twice_v, 2)[:, None] / wide
    tap_u, tap_v = turn(u, np.arange(taps), tall), turn(np.arange(taps), v, wide)
    row_taps = np.concatenate([np.cos(tap_u), np.sin(tap_u)]) * np.tile(keep_u, 2)[:, None]
    col_taps = np.concatenate([np.cos(tap_v), np.sin(tap_v)], axis=1) * np.tile(keep_v, 2)
    places, rows = [], []
    for table in (rows_in, rows_out, cols_in, cols_out, row_taps, col_taps):
        places.append((sum(part.shape[0] for part in rows), *table.shape))
        rows.append(np.pad(table, ((0, -table.shape[0] % 16), (0, 2 * side - table.shape[1]))))
    return jnp.asarray(np.concatenate(rows), jnp.float32), places


MESH = pl.DeviceIdType.MESH
LINE, CORES = 4, 2
PARTS = (32, 32, 32, 16, 16)
WEIGHT_UNIT = 512.0


def greet(sides):
    barrier = pltpu.get_barrier_semaphore()
    for axis, count, me in sides:
        for hop in range(1, count):
            pl.semaphore_signal(
                barrier, inc=1, device_id={axis: lax.rem(me + hop, count)}, device_id_type=MESH
            )
    return barrier, sum(count - 1 for _, count, _ in sides)


def receiver(me, hop, count):
    turn = lax.rem(hop + 1, count)
    pair = turn // CORES
    dx = lax.rem(pair, LINE)
    dz = lax.rem(pair // LINE + pair, LINE)
    z, x, core = me // (LINE * CORES), lax.rem(me // CORES, LINE), lax.rem(me, CORES)
    sign = 1 - 2 * core
    z, x = lax.rem(z + sign * dz + LINE, LINE), lax.rem(x + sign * dx + LINE, LINE)
    core = lax.rem(core + turn, CORES)
    return (z * LINE + x) * CORES + core


def hop_to(owner, me):
    wide, line = LINE * CORES, LINE - 1
    sign = 1 - 2 * lax.rem(me, CORES)
    dz = (sign * (owner // wide - me // wide)) & line
    dx = (sign * (((owner // CORES) & line) - lax.rem(me // CORES, LINE))) & line
    dc = (owner - me) & (CORES - 1)
    turn = CORES * (LINE * ((dz - dx) & line) + dx) + dc
    return (turn - 1) & (LINE * wide - 1)


def route(me, capacity, owner_ref, slot_ref, variance_ref, route_table, fields):
    blocks, places = owner_ref.shape[1], route_table.shape[1]
    square = (blocks, blocks)
    down, along = (lax.broadcasted_iota(jnp.int32, square, axis) for axis in (0, 1))
    hop_along = jnp.broadcast_to(hop_to(owner_ref[...], me), square)
    hop_down = hop_along.T
    count = lambda mask: jnp.sum(mask.astype(jnp.int32), axis=1, keepdims=True)
    rank = count((hop_along == hop_down) & (along < down))
    position = rank + count(hop_along < hop_down)
    weight = (1.0 / variance_ref[...]).astype(jnp.bfloat16).astype(jnp.float32)
    units = (jnp.broadcast_to(weight, square).T * WEIGHT_UNIT).astype(jnp.int32)[:, :1]
    slot = jnp.broadcast_to(slot_ref[...], square).T[:, :1]
    table = (blocks, places)
    number = lax.broadcasted_iota(jnp.int32, table, 0)
    lane = lax.broadcasted_iota(jnp.int32, table, 1)
    found = lane == hop_down[:, :1] * capacity + rank
    pick = lambda mask, values: jnp.sum(jnp.where(mask, values, 0), axis=0, keepdims=True)
    order = pick(lane == position, number)
    source = pick(found, position)
    route_table[...] = jnp.concatenate([order, source] + [order] * (route_table.shape[0] - 2), axis=0)
    row = [pick(found, units), pick(found, slot)]
    fields[...] = jnp.concatenate(row + [jnp.zeros_like(row[0])] * (fields.shape[0] - 2), axis=0)


def transform_rows(reach, rows_in, before, exposure, after, strip):
    columns = exposure.shape[1]
    tiles = 4
    wide = tiles * SPAN

    def rows(begin, width):
        return jnp.concatenate(
            [ref[:, pl.ds(begin, width)] for ref in (before, exposure, after)], axis=0
        )

    def spectra(window):
        return jnp.dot(rows_in[...], window, preferred_element_type=jnp.float32).astype(strip.dtype)

    def store(number, old):
        moved = spectra(old[:, SPAN - reach : SPAN - reach + wide])
        for tile in range(tiles):
            strip[number * tiles + tile] = moved[:, tile * SPAN : (tile + 1) * SPAN]

    def piece(number, carry):
        begin = pl.multiple_of(number * wide, wide)
        store(number, rows(pl.multiple_of(begin - SPAN, SPAN), wide + SPAN))
        return carry

    zeros = jnp.zeros((rows_in.shape[1], SPAN), exposure.dtype)
    store(0, jnp.concatenate([zeros, rows(0, wide)], axis=1))
    lax.fori_loop(1, columns // wide, piece, 0)
    last = jnp.concatenate([rows(columns - SPAN, SPAN), zeros], axis=1)
    strip[columns // SPAN] = spectra(last[:, SPAN - reach : 2 * SPAN - reach])


def match_group(
    step, route_smem, rows_out, cols_in, cols_out, row_wave, col_wave, coef_ref,
    strip, rows_ref, cols_ref, spectrum, response, warps, waves, warped,
):
    low = row_wave.shape[0] // 2
    side = warped.shape[1]
    numbers = [route_smem[0, step * GROUP + q] for q in range(GROUP)]
    windows = [jnp.concatenate([strip[number], strip[number + 1]], axis=1) for number in numbers]
    spectrum[...] = jnp.dot(
        jnp.concatenate(windows, axis=0), cols_in[...], preferred_element_type=jnp.float32
    )
    scaled = [(row_wave[...] * coef_ref[number]).astype(jnp.bfloat16) for number in numbers]
    response[...] = jnp.dot(
        jnp.concatenate(scaled, axis=0), col_wave[...], preferred_element_type=jnp.float32
    )
    warps[...] = jnp.dot(
        jnp.concatenate([rows_ref[number] for number in numbers], axis=0),
        rows_out[...],
        preferred_element_type=jnp.float32,
    ).astype(jnp.bfloat16)
    for q in range(GROUP):
        top = slice(q * 2 * low, q * 2 * low + low)
        end = slice(q * 2 * low + low, (q + 1) * 2 * low)
        p_re, p_im = spectrum[top, :SPAN], spectrum[top, SPAN:]
        q_re, q_im = spectrum[end, :SPAN], spectrum[end, SPAN:]
        a_re, a_im = response[top, :SPAN], response[top, SPAN:]
        b_re, b_im = response[end, :SPAN], response[end, SPAN:]
        even_re = p_re * a_re - p_im * a_im + q_re * b_re - q_im * b_im
        even_im = p_re * a_im + p_im * a_re + q_re * b_im + q_im * b_re
        odd_re = p_re * b_re - p_im * b_im - q_re * a_re + q_im * a_im
        odd_im = p_re * b_im + p_im * b_re - q_re * a_im - q_im * a_re
        stacked = jnp.concatenate(
            [
                jnp.concatenate([even_re, even_im], axis=1),
                jnp.concatenate([odd_re, odd_im], axis=1),
            ],
            axis=0,
        ).astype(jnp.bfloat16)
        waves[q * side : (q + 1) * side, :] = jnp.dot(
            warps[q * side : (q + 1) * side, :], stacked, preferred_element_type=jnp.float32
        ).astype(jnp.bfloat16)
    across = jnp.dot(waves[...], cols_out[...], preferred_element_type=jnp.float32).astype(
        jnp.bfloat16
    )
    for q in range(GROUP):
        warped[step * GROUP + q] = lax.dot_general(
            across[q * side : (q + 1) * side],
            cols_ref[numbers[q]],
            (((1,), (1,)), ((), ())),
            preferred_element_type=jnp.float32,
        ).astype(jnp.bfloat16)


def slot_order(label_in, table_int, table_float, weight_sum, slots):
    labels = label_in[0]
    for source in range(1, label_in.shape[0]):
        labels = labels + label_in[source]
    places = labels.shape[1]
    square = (places, places)
    down, along = (lax.broadcasted_iota(jnp.int32, square, axis) for axis in (0, 1))
    slot_along = jnp.broadcast_to(labels[1:2], square)
    weight_along = jnp.broadcast_to(labels[0:1].astype(jnp.float32) / WEIGHT_UNIT, square)
    slot_down, weight_down = slot_along.T, weight_along.T
    ahead = (slot_along < slot_down) | ((slot_along == slot_down) & (along < down))
    rank = jnp.sum(ahead.astype(jnp.int32), axis=1, keepdims=True)
    chosen = rank == along
    order = jnp.sum(jnp.where(chosen, down, 0), axis=0, keepdims=True)
    slot = jnp.sum(jnp.where(chosen, slot_down, 0), axis=0, keepdims=True)
    weight = jnp.sum(jnp.where(chosen, weight_down, 0.0), axis=0, keepdims=True)
    goes_on = ((slot == pltpu.roll(slot, 1, axis=1)) & (along[:1] > 0)).astype(jnp.float32)
    up_to = jnp.sum((slot_down <= along).astype(jnp.int32), axis=0, keepdims=True)
    inside = jnp.sum((slot_down == along).astype(jnp.int32), axis=0, keepdims=True)
    last = jnp.maximum(up_to - 1, 0)
    table_int[...] = jnp.concatenate([order, last] + [order] * (table_int.shape[0] - 2), axis=0)
    table_float[...] = jnp.concatenate(
        [weight, goes_on, (inside > 0).astype(jnp.float32)] + [weight] * (table_float.shape[0] - 3),
        axis=0,
    )
    mine = jnp.where(slot_along[:slots] == down[:slots], weight_along[:slots], 0.0)
    weight_sum[...] = jnp.broadcast_to(jnp.sum(mine, axis=1, keepdims=True), (slots, places))


def coadd_kernel(
    reach, capacity, places, exposure_hbm, rows_hbm, cols_hbm, tables_hbm,
    row_bases, col_bases, coefficients, variance, owner, slot_index, coadd,
    exposure, before, after, strip, tables, wave_table, row_wave, col_wave, coef_ref,
    route_table, fields, labels,
    spectrum, response, warps, waves, warped, rows_ref, cols_ref,
    label_in, table_int, table_float, weight_sum, weight_in, scale, running,
    route_smem, int_smem, float_smem,
    halo_send, halo_recv, send_sem, recv_sem, label_send, label_recv, load_sem, table_sem,
    sum_send, sum_recv, weight_send, weight_recv, *pieces,
):
    parts = len(PARTS)
    outgoing, arrived, partial, gathered = (
        pieces[kind * parts : (kind + 1) * parts] for kind in range(4)
    )
    me, my_src = lax.axis_index("tile"), lax.axis_index("src")
    blocks, side = warped.shape[:2]
    count, peers = labels.shape[0], partial[0].shape[0]
    rows_of = [slice(sum(PARTS[:part]), sum(PARTS[: part + 1])) for part in range(parts)]
    tiles, across = coadd.shape[0], peers
    barrier, greetings = greet((("tile", count, me), ("src", peers, my_src)))
    loads = [
        pltpu.make_async_copy(from_ref, to_ref, load_sem.at[number])
        for number, (from_ref, to_ref) in enumerate(
            (
                (tables_hbm, wave_table),
                (exposure_hbm, exposure),
                (rows_hbm, rows_ref),
                (cols_hbm, cols_ref),
            )
        )
    ]
    for load in loads:
        load.start()
    route(me, capacity, owner, slot_index, variance, route_table, fields)
    move = pltpu.make_async_copy(route_table, route_smem, table_sem.at[0])
    move.start()
    by_block = jnp.concatenate([coefficients[k] for k in range(coefficients.shape[0])], axis=0).T
    for number in range(blocks):
        coef_ref[number] = by_block[number : number + 1, :]
    lane = lax.broadcasted_iota(jnp.int32, fields.shape, 1)
    for hop in range(count):
        moved = pltpu.roll(
            fields[...], lax.rem((me - hop + count) * capacity, lane.shape[1]), axis=1
        )
        labels[hop] = jnp.where(lane // capacity == me, moved, 0)
    pl.semaphore_wait(barrier, greetings)

    def halo(number, begin, to_ref, neighbour):
        return pltpu.make_async_remote_copy(
            src_ref=exposure_hbm.at[pl.ds(begin, HALO)],
            dst_ref=to_ref,
            send_sem=halo_send.at[number],
            recv_sem=halo_recv.at[number],
            device_id={"tile": neighbour},
            device_id_type=MESH,
        )

    down = halo(0, side - HALO, before, lax.rem(me + 1, count))
    up = halo(1, 0, after, lax.rem(me + count - 1, count))

    @pl.when(me < count - 1)
    def _():
        down.start()

    @pl.when(me > 0)
    def _():
        up.start()

    @pl.when(me == 0)
    def _():
        before[...] = jnp.zeros_like(before)

    @pl.when(me == count - 1)
    def _():
        after[...] = jnp.zeros_like(after)

    def label_message(hop):
        return pltpu.make_async_remote_copy(
            src_ref=labels.at[hop],
            dst_ref=label_in.at[me],
            send_sem=label_send.at[hop],
            recv_sem=label_recv.at[hop],
            device_id={"tile": receiver(me, hop, count)},
            device_id_type=MESH,
        )

    def message(part, hop):
        return pltpu.make_async_remote_copy(
            src_ref=outgoing[part].at[hop],
            dst_ref=arrived[part].at[pl.ds(me * capacity, capacity)],
            send_sem=send_sem.at[part, hop],
            recv_sem=recv_sem.at[part, hop],
            device_id={"tile": receiver(me, hop, count)},
            device_id_type=MESH,
        )

    def each_hop(begin, end, act):
        def one(hop, carry):
            act(hop)
            return carry

        lax.fori_loop(begin, end, one, 0)

    def piece(hop, r, part):
        return warped[route_smem[1, hop * capacity + r], rows_of[part], :]

    def send(part, hop):
        for r in range(capacity):
            outgoing[part][hop, r] = piece(hop, r, part)
        message(part, hop).start()

    ready = GROUP // capacity
    steps = blocks // GROUP
    each_hop(0, count - 1, lambda hop: label_message(hop).start())
    warped[...] = jnp.zeros_like(warped)
    view = lambda ref, place: ref.at[pl.ds(place[0], place[1]), pl.ds(0, place[2])]
    rows_in, rows_out, cols_in, cols_out = (view(tables, place) for place in places[:4])
    row_taps, col_taps = (view(wave_table, place) for place in places[4:])
    loads[0].wait()
    tables[...] = wave_table[: tables.shape[0], :].astype(tables.dtype)
    row_wave[...] = lax.dot_general(
        row_taps[...],
        row_bases[...].astype(jnp.float32),
        (((1,), (1,)), ((), ())),
        precision=lax.Precision.HIGHEST,
        preferred_element_type=jnp.float32,
    )
    col_wave[...] = jnp.dot(
        col_bases[...].astype(jnp.float32),
        col_taps[...],
        precision=lax.Precision.HIGHEST,
        preferred_element_type=jnp.float32,
    ).astype(col_wave.dtype)
    for load in loads[1:]:
        load.wait()
    move.wait()

    @pl.when(me > 0)
    def _():
        down.wait_recv()

    @pl.when(me < count - 1)
    def _():
        up.wait_recv()

    transform_rows(reach, rows_in, before, exposure, after, strip)

    def group(step, carry):
        match_group(
            step, route_smem, rows_out, cols_in, cols_out, row_wave, col_wave, coef_ref,
            strip, rows_ref, cols_ref, spectrum, response, warps, waves, warped,
        )
        for hop in range(ready):
            for part in range(parts):
                send(part, step * ready + hop)
        return carry

    lax.fori_loop(0, steps, group, 0)
    for part in range(parts):
        each_hop(steps * ready, count - 1, lambda hop, part=part: send(part, hop))
        for r in range(capacity):
            arrived[part][me * capacity + r] = piece(count - 1, r, part)

    label_in[me] = labels[count - 1]
    each_hop(0, count - 1, lambda hop: label_message(hop).wait())
    slot_order(label_in, table_int, table_float, weight_sum, tiles * across * across)
    moves = [
        pltpu.make_async_copy(table_int, int_smem, table_sem.at[1]),
        pltpu.make_async_copy(table_float, float_smem, table_sem.at[2]),
    ]
    for move in moves:
        move.start()

    def to_peer(hop, from_ref, to_ref, send_sem, recv_sem):
        return pltpu.make_async_remote_copy(
            src_ref=from_ref,
            dst_ref=to_ref,
            send_sem=send_sem,
            recv_sem=recv_sem,
            device_id={"src": lax.rem(my_src + hop, peers)},
            device_id_type=MESH,
        )

    def weight_message(hop):
        return to_peer(
            hop, weight_sum, weight_in.at[hop - 1], weight_send.at[hop - 1], weight_recv.at[hop - 1]
        )

    def sum_message(part, hop):
        return to_peer(
            hop,
            partial[part].at[lax.rem(my_src + hop, peers)],
            gathered[part].at[hop - 1],
            sum_send.at[part, hop - 1],
            sum_recv.at[part, hop - 1],
        )

    for hop in range(1, peers):
        weight_message(hop).start()
    for move in moves:
        move.wait()

    def stack(part):
        high = PARTS[part]

        def add(place, total):
            block = arrived[part][int_smem[0, place]].astype(jnp.float32)
            total = total * float_smem[1, place] + float_smem[0, place] * block
            running[place, :high] = total
            return total

        lax.fori_loop(
            0, arrived[part].shape[0], add, jnp.zeros((high, side), jnp.float32), unroll=4
        )

        def take(slot, carry):
            row = lax.rem(slot // across, across)
            place = slot // (across * across) * across + lax.rem(slot, across)
            total = running[int_smem[1, slot], :high] * float_smem[2, slot]
            partial[part][row, place] = total.astype(jnp.bfloat16)
            return carry

        lax.fori_loop(0, tiles * across * across, take, 0, unroll=4)

    def finish(part):
        for hop in range(1, peers):
            sum_message(part, hop).wait()
        for tile in range(tiles):
            for column in range(across):
                place = tile * across + column
                total = partial[part][my_src, place].astype(jnp.float32)
                for hop in range(peers - 1):
                    total = total + gathered[part][hop, place].astype(jnp.float32)
                slot = (tile * across + my_src) * across + column
                coadd[tile, rows_of[part], column * side : (column + 1) * side] = total * scale[slot]

    for part in range(parts):
        each_hop(0, count - 1, lambda hop, part=part: message(part, hop).wait_recv())
        stack(part)
        for hop in range(1, peers):
            sum_message(part, hop).start()
        if part == 0:
            for hop in range(1, peers):
                weight_message(hop).wait()
            weight = weight_sum[...]
            for hop in range(peers - 1):
                weight = weight + weight_in[hop]
            factor = 1.0 / jnp.maximum(weight, 1.0)
            for slot in range(scale.shape[0]):
                scale[slot] = factor[slot : slot + 1]
        else:
            finish(part - 1)
    finish(parts - 1)
    for part in range(parts):
        each_hop(0, count - 1, lambda hop, part=part: message(part, hop).wait_send())

    @pl.when(me < count - 1)
    def _():
        down.wait_send()

    @pl.when(me > 0)
    def _():
        up.wait_send()


def body(
    exposure,
    row_bases,
    col_bases,
    coefficients,
    warp_rows,
    warp_cols,
    variance,
    footprint,
    slot_index,
):
    blocks, side = warp_rows.shape[2:4]
    columns = exposure.shape[2]
    basis_count, taps = row_bases.shape
    peers, count = lax.axis_size("src"), lax.axis_size("tile")
    capacity = max(2, 2 * blocks // count)
    slots, sends = TILES_DEV * peers * peers, count * capacity
    reach = taps // 2
    tall = -(-(side + taps - 1) // 16) * 16
    tables, places = wave_tables(
        taps, side, tall, side + taps - 1, side + 2 * HALO, HALO - reach
    )
    spectra = places[0][1]
    near, far = pl.BlockSpec(memory_space=pltpu.VMEM), pl.BlockSpec(memory_space=pltpu.HBM)
    parts, per = len(PARTS), slots // peers
    narrow, wide, whole = jnp.bfloat16, jnp.float32, jnp.int32
    vmem, smem, dma = pltpu.VMEM, pltpu.SMEM, pltpu.SemaphoreType.DMA
    return pl.pallas_call(
        functools.partial(coadd_kernel, reach, capacity, places),
        in_specs=[far] * 4 + [near] * 6,
        out_specs=near,
        out_shape=jax.ShapeDtypeStruct((TILES_DEV, side, peers * side), wide),
        scratch_shapes=[
            vmem((side, columns), narrow),
            vmem((HALO, columns), narrow),
            vmem((HALO, columns), narrow),
            vmem((columns // SPAN + 1, spectra, SPAN), narrow),
            vmem((places[4][0], 2 * SPAN), narrow),
            vmem(tables.shape, wide),
            vmem((spectra, basis_count), wide),
            vmem((basis_count, 2 * SPAN), narrow),
            vmem((blocks, 1, basis_count), wide),
            vmem((8, sends), whole),
            vmem((8, sends), whole),
            vmem((count, 8, sends), whole),
            vmem((GROUP * spectra, 2 * SPAN), wide),
            vmem((GROUP * spectra, 2 * SPAN), wide),
            vmem((GROUP * side, spectra), narrow),
            vmem((GROUP * side, 2 * SPAN), narrow),
            vmem((blocks, side, side), narrow),
            vmem((blocks, side, side), narrow),
            vmem((blocks, side, side), narrow),
            vmem((count, 8, sends), whole),
            vmem((8, sends), whole),
            vmem((8, sends), wide),
            vmem((slots, sends), wide),
            vmem((peers - 1, slots, sends), wide),
            vmem((slots, 1, sends), wide),
            vmem((sends, max(PARTS), side), wide),
            smem((8, sends), whole),
            smem((8, sends), whole),
            smem((8, sends), wide),
            dma((2,)),
            dma((2,)),
            dma((parts, count)),
            dma((parts, count)),
            dma((count,)),
            dma((count,)),
            dma((4,)),
            dma((3,)),
            dma((parts, peers - 1)),
            dma((parts, peers - 1)),
            dma((peers - 1,)),
            dma((peers - 1,)),
            *[vmem((count, capacity, high, side), narrow) for high in PARTS],
            *[vmem((sends, high, side), narrow) for high in PARTS],
            *[vmem((peers, per, high, side), narrow) for high in PARTS],
            *[vmem((peers - 1, per, high, side), narrow) for high in PARTS],
        ],
        compiler_params=pltpu.CompilerParams(
            collective_id=0, has_side_effects=True, vmem_limit_bytes=50 * 1024 * 1024
        ),
        cost_estimate=pl.CostEstimate(flops=4 << 30, bytes_accessed=10 << 20, transcendentals=0),
    )(
        exposure[0], warp_rows[0, 0], warp_cols[0, 0], tables, row_bases, col_bases,
        coefficients[0].transpose(2, 0, 1), variance[0], footprint.reshape(1, blocks), slot_index[0],
    )


def solution(mesh):
    placed = (
        P("src", "tile", None),
        P(),
        P(),
        P("src", "tile", None, None),
        P("src", "tile", None, None, None),
        P("src", "tile", None, None, None),
        P("src", "tile", None),
        P("src", "tile", None, None),
        P("src", "tile", None),
    )
    return jax.shard_map(
        body, mesh=mesh, in_specs=placed, out_specs=P("tile", "src", None), check_vma=False
    )
```

```python
import functools

import jax
import jax.numpy as jnp
import numpy as np
from jax import lax
from jax.experimental import pallas as pl
from jax.experimental.pallas import tpu as pltpu
from jax.sharding import PartitionSpec as P

TILES_DEV = 4


EDGE = 16
FOLDS = 4
GROUP = 4
SPAN = 128


def wave_tables(taps, side, tall, wide):
    low, lanes = -(-(tall // 2 + 1) // 16) * 16, SPAN
    u, v = np.arange(low), np.arange(lanes)
    keep_u, keep_v = u <= tall // 2, v <= wide // 2
    twice_u = np.where((u == 0) | (2 * u == tall), 1.0, 2.0) * keep_u
    twice_v = np.where((v == 0) | (2 * v == wide), 1.0, 2.0) * keep_v
    turn = lambda one, other, length: 2.0 * np.pi / length * (np.outer(one, other) % length)
    reach, edge = taps // 2, np.arange(EDGE)
    fold = edge % (reach - EDGE)
    starts = (reach + np.arange(side), reach - EDGE + edge, reach + side + edge, fold, reach + side + EDGE + fold)
    down = turn(u, np.concatenate(starts), tall)
    rows_in = np.concatenate([np.cos(down), np.sin(down)]) * np.tile(keep_u, 2)[:, None]
    back = turn(np.arange(side), u, tall)
    rows_out = np.concatenate([np.cos(back) * twice_u, -np.sin(back) * twice_u], axis=1) / tall
    along = turn(np.arange(2 * side), v, wide)
    inside = (np.arange(2 * side) < wide)[:, None]
    cols_in = np.concatenate([np.cos(along), -np.sin(along)], axis=1) * inside * np.tile(keep_v, 2)
    front = turn(v, np.arange(side), wide)
    cols_out = np.concatenate([np.cos(front), -np.sin(front)]) * np.tile(twice_v, 2)[:, None] / wide
    tap_u, tap_v = turn(u, np.arange(taps), tall), turn(np.arange(taps), v, wide)
    row_taps = np.concatenate([np.cos(tap_u), np.sin(tap_u)]) * np.tile(keep_u, 2)[:, None]
    col_taps = np.concatenate([np.cos(tap_v), np.sin(tap_v)], axis=1) * np.tile(keep_v, 2)
    places, rows = [], []
    for table in (rows_in, rows_out, cols_in, cols_out, row_taps, col_taps):
        places.append((sum(part.shape[0] for part in rows), *table.shape))
        rows.append(np.pad(table, ((0, -table.shape[0] % 16), (0, 2 * side - table.shape[1]))))
    return jnp.asarray(np.concatenate(rows), jnp.float32), places


MESH = pl.DeviceIdType.MESH
LINE, CORES = 4, 2
PARTS = (32, 32, 32, 16, 16)
WEIGHT_UNIT = 512.0


def greet(sides):
    barrier = pltpu.get_barrier_semaphore()
    for axis, count, me in sides:
        for hop in range(1, count):
            pl.semaphore_signal(
                barrier, inc=1, device_id={axis: lax.rem(me + hop, count)}, device_id_type=MESH
            )
    return barrier, sum(count - 1 for _, count, _ in sides)


def receiver(me, hop, count):
    turn = lax.rem(hop + 1, count)
    pair = turn // CORES
    dx = lax.rem(pair, LINE)
    dz = lax.rem(pair // LINE + pair, LINE)
    z, x, core = me // (LINE * CORES), lax.rem(me // CORES, LINE), lax.rem(me, CORES)
    sign = 1 - 2 * core
    z, x = lax.rem(z + sign * dz + LINE, LINE), lax.rem(x + sign * dx + LINE, LINE)
    core = lax.rem(core + turn, CORES)
    return (z * LINE + x) * CORES + core


def hop_to(owner, me):
    wide, line = LINE * CORES, LINE - 1
    sign = 1 - 2 * lax.rem(me, CORES)
    dz = (sign * (owner // wide - me // wide)) & line
    dx = (sign * (((owner // CORES) & line) - lax.rem(me // CORES, LINE))) & line
    dc = (owner - me) & (CORES - 1)
    turn = CORES * (LINE * ((dz - dx) & line) + dx) + dc
    return (turn - 1) & (LINE * wide - 1)


def route(me, capacity, owner_ref, slot_ref, variance_ref, route_table, fields):
    blocks, places = owner_ref.shape[1], route_table.shape[1]
    square = (blocks, blocks)
    down, along = (lax.broadcasted_iota(jnp.int32, square, axis) for axis in (0, 1))
    hop_along = jnp.broadcast_to(hop_to(owner_ref[...], me), square)
    hop_down = hop_along.T
    count = lambda mask: jnp.sum(mask.astype(jnp.int32), axis=1, keepdims=True)
    rank = count((hop_along == hop_down) & (along < down))
    position = rank + count(hop_along < hop_down)
    weight = (1.0 / variance_ref[...]).astype(jnp.bfloat16).astype(jnp.float32)
    units = (jnp.broadcast_to(weight, square).T * WEIGHT_UNIT).astype(jnp.int32)[:, :1]
    slot = jnp.broadcast_to(slot_ref[...], square).T[:, :1]
    table = (blocks, places)
    number = lax.broadcasted_iota(jnp.int32, table, 0)
    lane = lax.broadcasted_iota(jnp.int32, table, 1)
    found = lane == hop_down[:, :1] * capacity + rank
    pick = lambda mask, values: jnp.sum(jnp.where(mask, values, 0), axis=0, keepdims=True)
    order = pick(lane == position, number)
    source = pick(found, position)
    route_table[...] = jnp.concatenate([order, source] + [order] * (route_table.shape[0] - 2), axis=0)
    row = [pick(found, units), pick(found, slot)]
    fields[...] = jnp.concatenate(row + [jnp.zeros_like(row[0])] * (fields.shape[0] - 2), axis=0)


def fold_rows(rows):
    part = rows.shape[1] // FOLDS
    zeros = jnp.zeros((rows.shape[0], SPAN), rows.dtype)
    quarters = []
    for fold in range(FOLDS):
        begin = fold * part
        ahead = rows[:, begin - SPAN : begin] if fold else zeros
        quarters.append(jnp.concatenate([ahead, rows[:, begin : begin + part]], axis=1))
    return jnp.concatenate(quarters, axis=0)


def transform_rows(reach, rows_in, exposure, edges, folds, strip):
    columns = exposure.shape[1]
    tiles = 4
    wide = tiles * SPAN
    per_fold = columns // wide // FOLDS
    fold_of_row = lax.broadcasted_iota(jnp.int32, (EDGE, 1), 0) // (EDGE // FOLDS)

    def rows(begin, width):
        return jnp.concatenate([ref[:, pl.ds(begin, width)] for ref in (exposure, *edges)], axis=0)

    def folded(fold, begin, width):
        pieces = [ref[:, pl.ds(begin, width)] for ref in folds]
        mine = fold_of_row == fold
        return jnp.concatenate([jnp.where(mine, piece, 0) for piece in pieces], axis=0)

    def spectra(window):
        return jnp.dot(rows_in[...], window, preferred_element_type=jnp.float32).astype(strip.dtype)

    def store(number, old):
        moved = spectra(old[:, SPAN - reach : SPAN - reach + wide])
        for tile in range(tiles):
            strip[number * tiles + tile] = moved[:, tile * SPAN : (tile + 1) * SPAN]

    def piece(number, carry):
        begin = pl.multiple_of(number * wide - SPAN, SPAN)
        inside = pl.multiple_of(lax.rem(number, per_fold) * wide, wide)
        over = wide + SPAN
        store(
            number,
            jnp.concatenate([rows(begin, over), folded(number // per_fold, inside, over)], axis=0),
        )
        return carry

    total = exposure.shape[0] + EDGE * (len(edges) + len(folds))
    zeros = jnp.zeros((total, SPAN), exposure.dtype)
    first = jnp.concatenate([rows(0, wide), folded(0, SPAN, wide)], axis=0)
    store(0, jnp.concatenate([zeros, first], axis=1))
    lax.fori_loop(1, columns // wide, piece, 0)
    last = [rows(columns - SPAN, SPAN), folded(FOLDS - 1, columns // FOLDS, SPAN)]
    last = jnp.concatenate([jnp.concatenate(last, axis=0), zeros], axis=1)
    strip[columns // SPAN] = spectra(last[:, SPAN - reach : 2 * SPAN - reach])


def match_group(
    step, route_smem, rows_out, cols_in, cols_out, row_wave, col_wave, coef_ref,
    strip, rows_ref, cols_ref, spectrum, response, warps, waves, warped,
):
    low = row_wave.shape[0] // 2
    side = warped.shape[1]
    numbers = [route_smem[0, step * GROUP + q] for q in range(GROUP)]
    windows = [jnp.concatenate([strip[number], strip[number + 1]], axis=1) for number in numbers]
    spectrum[...] = jnp.dot(
        jnp.concatenate(windows, axis=0), cols_in[...], preferred_element_type=jnp.float32
    )
    scaled = [(row_wave[...] * coef_ref[number]).astype(jnp.bfloat16) for number in numbers]
    response[...] = jnp.dot(
        jnp.concatenate(scaled, axis=0), col_wave[...], preferred_element_type=jnp.float32
    )
    warps[...] = jnp.dot(
        jnp.concatenate([rows_ref[number] for number in numbers], axis=0),
        rows_out[...],
        preferred_element_type=jnp.float32,
    ).astype(jnp.bfloat16)
    for q in range(GROUP):
        top = slice(q * 2 * low, q * 2 * low + low)
        end = slice(q * 2 * low + low, (q + 1) * 2 * low)
        p_re, p_im = spectrum[top, :SPAN], spectrum[top, SPAN:]
        q_re, q_im = spectrum[end, :SPAN], spectrum[end, SPAN:]
        a_re, a_im = response[top, :SPAN], response[top, SPAN:]
        b_re, b_im = response[end, :SPAN], response[end, SPAN:]
        even_re = p_re * a_re - p_im * a_im + q_re * b_re - q_im * b_im
        even_im = p_re * a_im + p_im * a_re + q_re * b_im + q_im * b_re
        odd_re = p_re * b_re - p_im * b_im - q_re * a_re + q_im * a_im
        odd_im = p_re * b_im + p_im * b_re - q_re * a_im - q_im * a_re
        stacked = jnp.concatenate(
            [
                jnp.concatenate([even_re, even_im], axis=1),
                jnp.concatenate([odd_re, odd_im], axis=1),
            ],
            axis=0,
        ).astype(jnp.bfloat16)
        waves[q * side : (q + 1) * side, :] = jnp.dot(
            warps[q * side : (q + 1) * side, :], stacked, preferred_element_type=jnp.float32
        ).astype(jnp.bfloat16)
    across = jnp.dot(waves[...], cols_out[...], preferred_element_type=jnp.float32).astype(
        jnp.bfloat16
    )
    for q in range(GROUP):
        warped[step * GROUP + q] = lax.dot_general(
            across[q * side : (q + 1) * side],
            cols_ref[numbers[q]],
            (((1,), (1,)), ((), ())),
            preferred_element_type=jnp.float32,
        ).astype(jnp.bfloat16)


def slot_order(label_in, table_int, table_float, weight_sum, slots):
    labels = label_in[0]
    for source in range(1, label_in.shape[0]):
        labels = labels + label_in[source]
    places = labels.shape[1]
    square = (places, places)
    down, along = (lax.broadcasted_iota(jnp.int32, square, axis) for axis in (0, 1))
    slot_along = jnp.broadcast_to(labels[1:2], square)
    weight_along = jnp.broadcast_to(labels[0:1].astype(jnp.float32) / WEIGHT_UNIT, square)
    slot_down, weight_down = slot_along.T, weight_along.T
    ahead = (slot_along < slot_down) | ((slot_along == slot_down) & (along < down))
    rank = jnp.sum(ahead.astype(jnp.int32), axis=1, keepdims=True)
    chosen = rank == along
    order = jnp.sum(jnp.where(chosen, down, 0), axis=0, keepdims=True)
    slot = jnp.sum(jnp.where(chosen, slot_down, 0), axis=0, keepdims=True)
    weight = jnp.sum(jnp.where(chosen, weight_down, 0.0), axis=0, keepdims=True)
    goes_on = ((slot == pltpu.roll(slot, 1, axis=1)) & (along[:1] > 0)).astype(jnp.float32)
    up_to = jnp.sum((slot_down <= along).astype(jnp.int32), axis=0, keepdims=True)
    inside = jnp.sum((slot_down == along).astype(jnp.int32), axis=0, keepdims=True)
    last = jnp.maximum(up_to - 1, 0)
    table_int[...] = jnp.concatenate([order, last] + [order] * (table_int.shape[0] - 2), axis=0)
    table_float[...] = jnp.concatenate(
        [weight, goes_on, (inside > 0).astype(jnp.float32)] + [weight] * (table_float.shape[0] - 3),
        axis=0,
    )
    mine = jnp.where(slot_along[:slots] == down[:slots], weight_along[:slots], 0.0)
    weight_sum[...] = jnp.broadcast_to(jnp.sum(mine, axis=1, keepdims=True), (slots, places))


def coadd_kernel(
    reach, capacity, places, exposure_hbm, rows_hbm, cols_hbm, tables_hbm,
    row_bases, col_bases, coefficients, variance, owner, slot_index, coadd,
    exposure, before, after, fold_before, fold_after, fold_down, fold_up, strip, tables, wave_table, row_wave, col_wave, coef_ref,
    route_table, fields, labels,
    spectrum, response, warps, waves, warped, rows_ref, cols_ref,
    label_in, table_int, table_float, weight_sum, weight_in, scale, running,
    route_smem, int_smem, float_smem,
    halo_send, halo_recv, send_sem, recv_sem, label_send, label_recv, load_sem, table_sem,
    sum_send, sum_recv, weight_send, weight_recv, *pieces,
):
    parts = len(PARTS)
    outgoing, arrived, partial, gathered = (
        pieces[kind * parts : (kind + 1) * parts] for kind in range(4)
    )
    me, my_src = lax.axis_index("tile"), lax.axis_index("src")
    blocks, side = warped.shape[:2]
    count, peers = labels.shape[0], partial[0].shape[0]
    rows_of = [slice(sum(PARTS[:part]), sum(PARTS[: part + 1])) for part in range(parts)]
    tiles, across = coadd.shape[0], peers
    barrier, greetings = greet((("tile", count, me), ("src", peers, my_src)))
    loads = [
        pltpu.make_async_copy(from_ref, to_ref, load_sem.at[number])
        for number, (from_ref, to_ref) in enumerate(
            (
                (tables_hbm, wave_table),
                (exposure_hbm, exposure),
                (rows_hbm, rows_ref),
                (cols_hbm, cols_ref),
            )
        )
    ]
    for load in loads:
        load.start()
    route(me, capacity, owner, slot_index, variance, route_table, fields)
    move = pltpu.make_async_copy(route_table, route_smem, table_sem.at[0])
    move.start()
    by_block = jnp.concatenate([coefficients[k] for k in range(coefficients.shape[0])], axis=0).T
    for number in range(blocks):
        coef_ref[number] = by_block[number : number + 1, :]
    lane = lax.broadcasted_iota(jnp.int32, fields.shape, 1)
    for hop in range(count):
        moved = pltpu.roll(
            fields[...], lax.rem((me - hop + count) * capacity, lane.shape[1]), axis=1
        )
        labels[hop] = jnp.where(lane // capacity == me, moved, 0)
    loads[1].wait()
    spare = reach - EDGE
    fold_down[...] = fold_rows(exposure[side - 2 * EDGE : side - EDGE, :][EDGE - spare :, :])
    fold_up[...] = fold_rows(exposure[EDGE : 2 * EDGE, :][:spare, :])
    pl.semaphore_wait(barrier, greetings)

    def halo(number, from_ref, to_ref, neighbour):
        return pltpu.make_async_remote_copy(
            src_ref=from_ref,
            dst_ref=to_ref,
            send_sem=halo_send.at[number],
            recv_sem=halo_recv.at[number],
            device_id={"tile": neighbour},
            device_id_type=MESH,
        )

    below, above = lax.rem(me + 1, count), lax.rem(me + count - 1, count)
    down = (
        halo(0, exposure.at[pl.ds(side - EDGE, EDGE)], before, below),
        halo(1, fold_down, fold_before, below),
    )
    up = (halo(2, exposure.at[pl.ds(0, EDGE)], after, above), halo(3, fold_up, fold_after, above))

    @pl.when(me < count - 1)
    def _():
        for copy in down:
            copy.start()

    @pl.when(me > 0)
    def _():
        for copy in up:
            copy.start()

    @pl.when(me == 0)
    def _():
        before[...] = jnp.zeros_like(before)
        fold_before[...] = jnp.zeros_like(fold_before)

    @pl.when(me == count - 1)
    def _():
        after[...] = jnp.zeros_like(after)
        fold_after[...] = jnp.zeros_like(fold_after)

    def label_message(hop):
        return pltpu.make_async_remote_copy(
            src_ref=labels.at[hop],
            dst_ref=label_in.at[me],
            send_sem=label_send.at[hop],
            recv_sem=label_recv.at[hop],
            device_id={"tile": receiver(me, hop, count)},
            device_id_type=MESH,
        )

    def message(part, hop):
        return pltpu.make_async_remote_copy(
            src_ref=outgoing[part].at[hop],
            dst_ref=arrived[part].at[pl.ds(me * capacity, capacity)],
            send_sem=send_sem.at[part, hop],
            recv_sem=recv_sem.at[part, hop],
            device_id={"tile": receiver(me, hop, count)},
            device_id_type=MESH,
        )

    def each_hop(begin, end, act):
        def one(hop, carry):
            act(hop)
            return carry

        lax.fori_loop(begin, end, one, 0)

    def piece(hop, r, part):
        return warped[route_smem[1, hop * capacity + r], rows_of[part], :]

    def send(part, hop):
        for r in range(capacity):
            outgoing[part][hop, r] = piece(hop, r, part)
        message(part, hop).start()

    ready = GROUP // capacity
    steps = blocks // GROUP
    each_hop(0, count - 1, lambda hop: label_message(hop).start())
    warped[...] = jnp.zeros_like(warped)
    view = lambda ref, place: ref.at[pl.ds(place[0], place[1]), pl.ds(0, place[2])]
    rows_in, rows_out, cols_in, cols_out = (view(tables, place) for place in places[:4])
    row_taps, col_taps = (view(wave_table, place) for place in places[4:])
    loads[0].wait()
    tables[...] = wave_table[: tables.shape[0], :].astype(tables.dtype)
    row_wave[...] = lax.dot_general(
        row_taps[...],
        row_bases[...].astype(jnp.float32),
        (((1,), (1,)), ((), ())),
        precision=lax.Precision.HIGHEST,
        preferred_element_type=jnp.float32,
    )
    col_wave[...] = jnp.dot(
        col_bases[...].astype(jnp.float32),
        col_taps[...],
        precision=lax.Precision.HIGHEST,
        preferred_element_type=jnp.float32,
    ).astype(col_wave.dtype)
    for load in loads[2:]:
        load.wait()
    move.wait()

    @pl.when(me > 0)
    def _():
        for copy in down:
            copy.wait_recv()

    @pl.when(me < count - 1)
    def _():
        for copy in up:
            copy.wait_recv()

    transform_rows(reach, rows_in, exposure, (before, after), (fold_before, fold_after), strip)

    def group(step, carry):
        match_group(
            step, route_smem, rows_out, cols_in, cols_out, row_wave, col_wave, coef_ref,
            strip, rows_ref, cols_ref, spectrum, response, warps, waves, warped,
        )
        for hop in range(ready):
            for part in range(parts):
                send(part, step * ready + hop)
        return carry

    lax.fori_loop(0, steps, group, 0)
    for part in range(parts):
        each_hop(steps * ready, count - 1, lambda hop, part=part: send(part, hop))
        for r in range(capacity):
            arrived[part][me * capacity + r] = piece(count - 1, r, part)

    label_in[me] = labels[count - 1]
    each_hop(0, count - 1, lambda hop: label_message(hop).wait())
    slot_order(label_in, table_int, table_float, weight_sum, tiles * across * across)
    moves = [
        pltpu.make_async_copy(table_int, int_smem, table_sem.at[1]),
        pltpu.make_async_copy(table_float, float_smem, table_sem.at[2]),
    ]
    for move in moves:
        move.start()

    def to_peer(hop, from_ref, to_ref, send_sem, recv_sem):
        return pltpu.make_async_remote_copy(
            src_ref=from_ref,
            dst_ref=to_ref,
            send_sem=send_sem,
            recv_sem=recv_sem,
            device_id={"src": lax.rem(my_src + hop, peers)},
            device_id_type=MESH,
        )

    def weight_message(hop):
        return to_peer(
            hop, weight_sum, weight_in.at[hop - 1], weight_send.at[hop - 1], weight_recv.at[hop - 1]
        )

    def sum_message(part, hop):
        return to_peer(
            hop,
            partial[part].at[lax.rem(my_src + hop, peers)],
            gathered[part].at[hop - 1],
            sum_send.at[part, hop - 1],
            sum_recv.at[part, hop - 1],
        )

    for hop in range(1, peers):
        weight_message(hop).start()
    for move in moves:
        move.wait()

    def stack(part):
        high = PARTS[part]

        def add(place, total):
            block = arrived[part][int_smem[0, place]].astype(jnp.float32)
            total = total * float_smem[1, place] + float_smem[0, place] * block
            running[place, :high] = total
            return total

        lax.fori_loop(
            0, arrived[part].shape[0], add, jnp.zeros((high, side), jnp.float32), unroll=4
        )

        def take(slot, carry):
            row = lax.rem(slot // across, across)
            place = slot // (across * across) * across + lax.rem(slot, across)
            total = running[int_smem[1, slot], :high] * float_smem[2, slot]
            partial[part][row, place] = total.astype(jnp.bfloat16)
            return carry

        lax.fori_loop(0, tiles * across * across, take, 0, unroll=4)

    def finish(part):
        for hop in range(1, peers):
            sum_message(part, hop).wait()
        for tile in range(tiles):
            for column in range(across):
                place = tile * across + column
                total = partial[part][my_src, place].astype(jnp.float32)
                for hop in range(peers - 1):
                    total = total + gathered[part][hop, place].astype(jnp.float32)
                slot = (tile * across + my_src) * across + column
                coadd[tile, rows_of[part], column * side : (column + 1) * side] = total * scale[slot]

    for part in range(parts):
        each_hop(0, count - 1, lambda hop, part=part: message(part, hop).wait_recv())
        stack(part)
        for hop in range(1, peers):
            sum_message(part, hop).start()
        if part == 0:
            for hop in range(1, peers):
                weight_message(hop).wait()
            weight = weight_sum[...]
            for hop in range(peers - 1):
                weight = weight + weight_in[hop]
            factor = 1.0 / jnp.maximum(weight, 1.0)
            for slot in range(scale.shape[0]):
                scale[slot] = factor[slot : slot + 1]
        else:
            finish(part - 1)
    finish(parts - 1)
    for part in range(parts):
        each_hop(0, count - 1, lambda hop, part=part: message(part, hop).wait_send())

    @pl.when(me < count - 1)
    def _():
        for copy in down:
            copy.wait_send()

    @pl.when(me > 0)
    def _():
        for copy in up:
            copy.wait_send()


def body(
    exposure,
    row_bases,
    col_bases,
    coefficients,
    warp_rows,
    warp_cols,
    variance,
    footprint,
    slot_index,
):
    blocks, side = warp_rows.shape[2:4]
    columns = exposure.shape[2]
    basis_count, taps = row_bases.shape
    peers, count = lax.axis_size("src"), lax.axis_size("tile")
    capacity = max(2, 2 * blocks // count)
    slots, sends = TILES_DEV * peers * peers, count * capacity
    reach = taps // 2
    tall = -(-(side + taps - 1) // 16) * 16
    tables, places = wave_tables(
        taps, side, tall, side + taps - 1
    )
    spectra = places[0][1]
    near, far = pl.BlockSpec(memory_space=pltpu.VMEM), pl.BlockSpec(memory_space=pl.ANY)
    parts, per = len(PARTS), slots // peers
    narrow, wide, whole = jnp.bfloat16, jnp.float32, jnp.int32
    vmem, smem, dma = pltpu.VMEM, pltpu.SMEM, pltpu.SemaphoreType.DMA
    return pl.pallas_call(
        functools.partial(coadd_kernel, reach, capacity, places),
        in_specs=[far] * 4 + [near] * 6,
        out_specs=near,
        out_shape=jax.ShapeDtypeStruct((TILES_DEV, side, peers * side), wide),
        scratch_shapes=[
            vmem((side, columns), narrow),
            vmem((EDGE, columns), narrow),
            vmem((EDGE, columns), narrow),
            *[vmem((EDGE, columns // FOLDS + SPAN), narrow)] * 4,
            vmem((columns // SPAN + 1, spectra, SPAN), narrow),
            vmem((places[4][0], 2 * SPAN), narrow),
            vmem(tables.shape, wide),
            vmem((spectra, basis_count), wide),
            vmem((basis_count, 2 * SPAN), narrow),
            vmem((blocks, 1, basis_count), wide),
            vmem((8, sends), whole),
            vmem((8, sends), whole),
            vmem((count, 8, sends), whole),
            vmem((GROUP * spectra, 2 * SPAN), wide),
            vmem((GROUP * spectra, 2 * SPAN), wide),
            vmem((GROUP * side, spectra), narrow),
            vmem((GROUP * side, 2 * SPAN), narrow),
            vmem((blocks, side, side), narrow),
            vmem((blocks, side, side), narrow),
            vmem((blocks, side, side), narrow),
            vmem((count, 8, sends), whole),
            vmem((8, sends), whole),
            vmem((8, sends), wide),
            vmem((slots, sends), wide),
            vmem((peers - 1, slots, sends), wide),
            vmem((slots, 1, sends), wide),
            vmem((sends, max(PARTS), side), wide),
            smem((8, sends), whole),
            smem((8, sends), whole),
            smem((8, sends), wide),
            dma((4,)),
            dma((4,)),
            dma((parts, count)),
            dma((parts, count)),
            dma((count,)),
            dma((count,)),
            dma((4,)),
            dma((3,)),
            dma((parts, peers - 1)),
            dma((parts, peers - 1)),
            dma((peers - 1,)),
            dma((peers - 1,)),
            *[vmem((count, capacity, high, side), narrow) for high in PARTS],
            *[vmem((sends, high, side), narrow) for high in PARTS],
            *[vmem((peers, per, high, side), narrow) for high in PARTS],
            *[vmem((peers - 1, per, high, side), narrow) for high in PARTS],
        ],
        compiler_params=pltpu.CompilerParams(
            collective_id=0, has_side_effects=True, vmem_limit_bytes=60 * 1024 * 1024
        ),
        cost_estimate=pl.CostEstimate(flops=4 << 30, bytes_accessed=10 << 20, transcendentals=0),
    )(
        exposure[0], warp_rows[0, 0], warp_cols[0, 0], tables, row_bases, col_bases,
        coefficients[0].transpose(2, 0, 1), variance[0], footprint.reshape(1, blocks), slot_index[0],
    )


def solution(mesh):
    placed = (
        P("src", "tile", None),
        P(),
        P(),
        P("src", "tile", None, None),
        P("src", "tile", None, None, None),
        P("src", "tile", None, None, None),
        P("src", "tile", None),
        P("src", "tile", None, None),
        P("src", "tile", None),
    )
    return jax.shard_map(
        body, mesh=mesh, in_specs=placed, out_specs=P("tile", "src", None), check_vma=False
    )
```

```python
import functools

import jax
import jax.numpy as jnp
import numpy as np
from jax import lax
from jax.experimental import pallas as pl
from jax.experimental.pallas import tpu as pltpu
from jax.sharding import PartitionSpec as P

TILES_DEV = 4


EDGE = 16
FOLDS = 4
GROUP = 8
SPAN = 128


def wave_tables(taps, side, tall, wide):
    low, lanes = -(-(tall // 2 + 1) // 16) * 16, SPAN
    u, v = np.arange(low), np.arange(lanes)
    keep_u, keep_v = u <= tall // 2, v <= wide // 2
    twice_u = np.where((u == 0) | (2 * u == tall), 1.0, 2.0) * keep_u
    twice_v = np.where((v == 0) | (2 * v == wide), 1.0, 2.0) * keep_v
    turn = lambda one, other, length: 2.0 * np.pi / length * (np.outer(one, other) % length)
    reach, edge = taps // 2, np.arange(EDGE)
    fold = edge % (reach - EDGE)
    starts = (reach + np.arange(side), reach - EDGE + edge, reach + side + edge, fold, reach + side + EDGE + fold)
    down = turn(u, np.concatenate(starts), tall)
    rows_in = np.concatenate([np.cos(down), np.sin(down)]) * np.tile(keep_u, 2)[:, None]
    back = turn(np.arange(side), u, tall)
    rows_out = np.concatenate([np.cos(back) * twice_u, -np.sin(back) * twice_u], axis=1) / tall
    along = turn(np.arange(2 * side), v, wide)
    inside = (np.arange(2 * side) < wide)[:, None]
    cols_in = np.concatenate([np.cos(along), -np.sin(along)], axis=1) * inside * np.tile(keep_v, 2)
    front = turn(v, np.arange(side), wide)
    cols_out = np.concatenate([np.cos(front), -np.sin(front)]) * np.tile(twice_v, 2)[:, None] / wide
    tap_u, tap_v = turn(u, np.arange(taps), tall), turn(np.arange(taps), v, wide)
    row_taps = np.concatenate([np.cos(tap_u), np.sin(tap_u)]) * np.tile(keep_u, 2)[:, None]
    col_taps = np.concatenate([np.cos(tap_v), np.sin(tap_v)], axis=1) * np.tile(keep_v, 2)
    places, rows = [], []
    for table in (rows_in, rows_out, cols_in, cols_out, row_taps, col_taps):
        places.append((sum(part.shape[0] for part in rows), *table.shape))
        rows.append(np.pad(table, ((0, -table.shape[0] % 16), (0, 2 * side - table.shape[1]))))
    return jnp.asarray(np.concatenate(rows), jnp.float32), places


MESH = pl.DeviceIdType.MESH
LINE, CORES = 4, 2
PARTS = (48, 32, 32, 16)
WEIGHT_UNIT = 512.0


def greet(sides):
    barrier = pltpu.get_barrier_semaphore()
    for axis, count, me in sides:
        for hop in range(1, count):
            pl.semaphore_signal(
                barrier, inc=1, device_id={axis: lax.rem(me + hop, count)}, device_id_type=MESH
            )
    return barrier, sum(count - 1 for _, count, _ in sides)


def receiver(me, hop, count):
    turn = lax.rem(hop + 1, count)
    pair = turn // CORES
    dx = lax.rem(pair, LINE)
    dz = lax.rem(pair // LINE + pair, LINE)
    z, x, core = me // (LINE * CORES), lax.rem(me // CORES, LINE), lax.rem(me, CORES)
    sign = 1 - 2 * core
    z, x = lax.rem(z + sign * dz + LINE, LINE), lax.rem(x + sign * dx + LINE, LINE)
    core = lax.rem(core + turn, CORES)
    return (z * LINE + x) * CORES + core


def hop_to(owner, me):
    wide, line = LINE * CORES, LINE - 1
    sign = 1 - 2 * lax.rem(me, CORES)
    dz = (sign * (owner // wide - me // wide)) & line
    dx = (sign * (((owner // CORES) & line) - lax.rem(me // CORES, LINE))) & line
    dc = (owner - me) & (CORES - 1)
    turn = CORES * (LINE * ((dz - dx) & line) + dx) + dc
    return (turn - 1) & (LINE * wide - 1)


def route(me, capacity, owner_ref, slot_ref, variance_ref, route_table, fields):
    blocks, places = owner_ref.shape[1], route_table.shape[1]
    square = (blocks, blocks)
    down, along = (lax.broadcasted_iota(jnp.int32, square, axis) for axis in (0, 1))
    hop_along = jnp.broadcast_to(hop_to(owner_ref[...], me), square)
    hop_down = hop_along.T
    count = lambda mask: jnp.sum(mask.astype(jnp.int32), axis=1, keepdims=True)
    rank = count((hop_along == hop_down) & (along < down))
    position = rank + count(hop_along < hop_down)
    weight = (1.0 / variance_ref[...]).astype(jnp.bfloat16).astype(jnp.float32)
    units = (jnp.broadcast_to(weight, square).T * WEIGHT_UNIT).astype(jnp.int32)[:, :1]
    slot = jnp.broadcast_to(slot_ref[...], square).T[:, :1]
    table = (blocks, places)
    number = lax.broadcasted_iota(jnp.int32, table, 0)
    lane = lax.broadcasted_iota(jnp.int32, table, 1)
    found = lane == hop_down[:, :1] * capacity + rank
    pick = lambda mask, values: jnp.sum(jnp.where(mask, values, 0), axis=0, keepdims=True)
    order = pick(lane == position, number)
    source = pick(found, position)
    route_table[...] = jnp.concatenate([order, source] + [order] * (route_table.shape[0] - 2), axis=0)
    row = [pick(found, units), pick(found, slot)]
    fields[...] = jnp.concatenate(row + [jnp.zeros_like(row[0])] * (fields.shape[0] - 2), axis=0)


def fold_rows(rows):
    part = rows.shape[1] // FOLDS
    zeros = jnp.zeros((rows.shape[0], SPAN), rows.dtype)
    quarters = []
    for fold in range(FOLDS):
        begin = fold * part
        ahead = rows[:, begin - SPAN : begin] if fold else zeros
        quarters.append(jnp.concatenate([ahead, rows[:, begin : begin + part]], axis=1))
    return jnp.concatenate(quarters, axis=0)


def transform_rows(reach, rows_in, exposure, edges, folds, strip):
    columns = exposure.shape[1]
    tiles = 4
    wide = tiles * SPAN
    per_fold = columns // wide // FOLDS
    fold_of_row = lax.broadcasted_iota(jnp.int32, (EDGE, 1), 0) // (EDGE // FOLDS)

    def rows(begin, width):
        return jnp.concatenate([ref[:, pl.ds(begin, width)] for ref in (exposure, *edges)], axis=0)

    def folded(fold, begin, width):
        pieces = [ref[:, pl.ds(begin, width)] for ref in folds]
        mine = fold_of_row == fold
        return jnp.concatenate([jnp.where(mine, piece, 0) for piece in pieces], axis=0)

    def spectra(window):
        return jnp.dot(rows_in[...], window, preferred_element_type=jnp.float32).astype(strip.dtype)

    def store(number, old):
        moved = spectra(old[:, SPAN - reach : SPAN - reach + wide])
        for tile in range(tiles):
            strip[number * tiles + tile] = moved[:, tile * SPAN : (tile + 1) * SPAN]

    def piece(number, carry):
        begin = pl.multiple_of(number * wide - SPAN, SPAN)
        inside = pl.multiple_of(lax.rem(number, per_fold) * wide, wide)
        over = wide + SPAN
        store(
            number,
            jnp.concatenate([rows(begin, over), folded(number // per_fold, inside, over)], axis=0),
        )
        return carry

    total = exposure.shape[0] + EDGE * (len(edges) + len(folds))
    zeros = jnp.zeros((total, SPAN), exposure.dtype)
    first = jnp.concatenate([rows(0, wide), folded(0, SPAN, wide)], axis=0)
    store(0, jnp.concatenate([zeros, first], axis=1))
    lax.fori_loop(1, columns // wide, piece, 0)
    last = [rows(columns - SPAN, SPAN), folded(FOLDS - 1, columns // FOLDS, SPAN)]
    last = jnp.concatenate([jnp.concatenate(last, axis=0), zeros], axis=1)
    strip[columns // SPAN] = spectra(last[:, SPAN - reach : 2 * SPAN - reach])


def match_group(
    step, route_smem, rows_out, cols_in, cols_out, row_wave, col_wave, coef_ref,
    strip, rows_ref, cols_ref, spectrum, response, warps, waves, warped,
):
    low = row_wave.shape[0] // 2
    side = warped.shape[1]
    numbers = [route_smem[0, step * GROUP + q] for q in range(GROUP)]
    windows = [jnp.concatenate([strip[number], strip[number + 1]], axis=1) for number in numbers]
    spectrum[...] = jnp.dot(
        jnp.concatenate(windows, axis=0), cols_in[...], preferred_element_type=jnp.float32
    )
    scaled = [(row_wave[...] * coef_ref[number]).astype(jnp.bfloat16) for number in numbers]
    response[...] = jnp.dot(
        jnp.concatenate(scaled, axis=0), col_wave[...], preferred_element_type=jnp.float32
    )
    warps[...] = jnp.dot(
        jnp.concatenate([rows_ref[number] for number in numbers], axis=0),
        rows_out[...],
        preferred_element_type=jnp.float32,
    ).astype(jnp.bfloat16)
    for q in range(GROUP):
        top = slice(q * 2 * low, q * 2 * low + low)
        end = slice(q * 2 * low + low, (q + 1) * 2 * low)
        p_re, p_im = spectrum[top, :SPAN], spectrum[top, SPAN:]
        q_re, q_im = spectrum[end, :SPAN], spectrum[end, SPAN:]
        a_re, a_im = response[top, :SPAN], response[top, SPAN:]
        b_re, b_im = response[end, :SPAN], response[end, SPAN:]
        even_re = p_re * a_re - p_im * a_im + q_re * b_re - q_im * b_im
        even_im = p_re * a_im + p_im * a_re + q_re * b_im + q_im * b_re
        odd_re = p_re * b_re - p_im * b_im - q_re * a_re + q_im * a_im
        odd_im = p_re * b_im + p_im * b_re - q_re * a_im - q_im * a_re
        stacked = jnp.concatenate(
            [
                jnp.concatenate([even_re, even_im], axis=1),
                jnp.concatenate([odd_re, odd_im], axis=1),
            ],
            axis=0,
        ).astype(jnp.bfloat16)
        waves[q * side : (q + 1) * side, :] = jnp.dot(
            warps[q * side : (q + 1) * side, :], stacked, preferred_element_type=jnp.float32
        ).astype(jnp.bfloat16)
    across = jnp.dot(waves[...], cols_out[...], preferred_element_type=jnp.float32).astype(
        jnp.bfloat16
    )
    for q in range(GROUP):
        warped[step * GROUP + q] = lax.dot_general(
            across[q * side : (q + 1) * side],
            cols_ref[numbers[q]],
            (((1,), (1,)), ((), ())),
            preferred_element_type=jnp.float32,
        ).astype(jnp.bfloat16)


def slot_order(label_in, table_int, table_float, weight_sum, slots):
    labels = label_in[0]
    for source in range(1, label_in.shape[0]):
        labels = labels + label_in[source]
    places = labels.shape[1]
    square = (places, places)
    down, along = (lax.broadcasted_iota(jnp.int32, square, axis) for axis in (0, 1))
    slot_along = jnp.broadcast_to(labels[1:2], square)
    weight_along = jnp.broadcast_to(labels[0:1].astype(jnp.float32) / WEIGHT_UNIT, square)
    late = along // (places // 2) * slots
    slot_plain, slot_along = slot_along, slot_along + late
    slot_down, weight_down = slot_along.T, weight_along.T
    ahead = (slot_along < slot_down) | ((slot_along == slot_down) & (along < down))
    rank = jnp.sum(ahead.astype(jnp.int32), axis=1, keepdims=True)
    chosen = rank == along
    order = jnp.sum(jnp.where(chosen, down, 0), axis=0, keepdims=True)
    slot = jnp.sum(jnp.where(chosen, slot_down, 0), axis=0, keepdims=True)
    weight = jnp.sum(jnp.where(chosen, weight_down, 0.0), axis=0, keepdims=True)
    goes_on = ((slot == pltpu.roll(slot, 1, axis=1)) & (along[:1] > 0)).astype(jnp.float32)
    up_to = jnp.sum((slot_down <= along).astype(jnp.int32), axis=0, keepdims=True)
    inside = jnp.sum((slot_down == along).astype(jnp.int32), axis=0, keepdims=True)
    half = late[:1] // slots * (places // 2)
    order, last = order - half, jnp.maximum(up_to - 1 - half, 0)
    table_int[...] = jnp.concatenate([order, last] + [order] * (table_int.shape[0] - 2), axis=0)
    table_float[...] = jnp.concatenate(
        [weight, goes_on, (inside > 0).astype(jnp.float32)] + [weight] * (table_float.shape[0] - 3),
        axis=0,
    )
    mine = jnp.where(slot_plain[:slots] == down[:slots], weight_along[:slots], 0.0)
    weight_sum[...] = jnp.broadcast_to(jnp.sum(mine, axis=1, keepdims=True), (slots, places))


def coadd_kernel(
    reach, capacity, places, exposure_hbm, rows_hbm, cols_hbm, tables_hbm,
    row_bases, col_bases, coefficients, variance, owner, slot_index, coadd,
    exposure, before, after, fold_before, fold_after, fold_down, fold_up, strip, tables, wave_table, row_wave, col_wave, coef_ref,
    route_table, fields, labels,
    spectrum, response, warps, waves, warped, rows_ref, cols_ref,
    blocks_out, blocks_in, block_sums, base,
    label_in, table_int, table_float, weight_sum, weight_in, scale, running,
    route_smem, int_smem, float_smem,
    halo_send, halo_recv, early_send, early_recv, send_sem, recv_sem, label_send, label_recv, load_sem, table_sem,
    sum_send, sum_recv, weight_send, weight_recv, *pieces,
):
    parts = len(PARTS)
    outgoing, arrived, partial, gathered = (
        pieces[kind * parts : (kind + 1) * parts] for kind in range(4)
    )
    early = blocks_out.shape[0]
    me, my_src = lax.axis_index("tile"), lax.axis_index("src")
    blocks, side = warped.shape[:2]
    count, peers = labels.shape[0], partial[0].shape[0]
    rows_of = [slice(sum(PARTS[:part]), sum(PARTS[: part + 1])) for part in range(parts)]
    tiles, across = coadd.shape[0], peers
    barrier, greetings = greet((("tile", count, me), ("src", peers, my_src)))
    loads = [
        pltpu.make_async_copy(from_ref, to_ref, load_sem.at[number])
        for number, (from_ref, to_ref) in enumerate(
            (
                (tables_hbm, wave_table),
                (exposure_hbm, exposure),
                (rows_hbm, rows_ref),
                (cols_hbm, cols_ref),
            )
        )
    ]
    for load in loads:
        load.start()
    route(me, capacity, owner, slot_index, variance, route_table, fields)
    move = pltpu.make_async_copy(route_table, route_smem, table_sem.at[0])
    move.start()
    by_block = jnp.concatenate([coefficients[k] for k in range(coefficients.shape[0])], axis=0).T
    for number in range(blocks):
        coef_ref[number] = by_block[number : number + 1, :]
    lane = lax.broadcasted_iota(jnp.int32, fields.shape, 1)
    for hop in range(count):
        labels[hop] = jnp.where(lane // capacity == hop, fields[...], 0)
    loads[1].wait()
    spare = reach - EDGE
    fold_down[...] = fold_rows(exposure[side - 2 * EDGE : side - EDGE, :][EDGE - spare :, :])
    fold_up[...] = fold_rows(exposure[EDGE : 2 * EDGE, :][:spare, :])
    pl.semaphore_wait(barrier, greetings)

    def halo(number, from_ref, to_ref, neighbour):
        return pltpu.make_async_remote_copy(
            src_ref=from_ref,
            dst_ref=to_ref,
            send_sem=halo_send.at[number],
            recv_sem=halo_recv.at[number],
            device_id={"tile": neighbour},
            device_id_type=MESH,
        )

    below, above = lax.rem(me + 1, count), lax.rem(me + count - 1, count)
    down = (
        halo(0, exposure.at[pl.ds(side - EDGE, EDGE)], before, below),
        halo(1, fold_down, fold_before, below),
    )
    up = (halo(2, exposure.at[pl.ds(0, EDGE)], after, above), halo(3, fold_up, fold_after, above))

    @pl.when(me < count - 1)
    def _():
        for copy in down:
            copy.start()

    @pl.when(me > 0)
    def _():
        for copy in up:
            copy.start()

    @pl.when(me == 0)
    def _():
        before[...] = jnp.zeros_like(before)
        fold_before[...] = jnp.zeros_like(fold_before)

    @pl.when(me == count - 1)
    def _():
        after[...] = jnp.zeros_like(after)
        fold_after[...] = jnp.zeros_like(fold_after)

    def label_message(hop):
        return pltpu.make_async_remote_copy(
            src_ref=labels.at[hop],
            dst_ref=label_in.at[hop],
            send_sem=label_send.at[hop],
            recv_sem=label_recv.at[hop],
            device_id={"tile": receiver(me, hop, count)},
            device_id_type=MESH,
        )

    def early_message(hop):
        return pltpu.make_async_remote_copy(
            src_ref=blocks_out.at[hop],
            dst_ref=blocks_in.at[pl.ds(hop * capacity, capacity)],
            send_sem=early_send.at[hop],
            recv_sem=early_recv.at[hop],
            device_id={"tile": receiver(me, hop, count)},
            device_id_type=MESH,
        )

    def message(part, hop):
        return pltpu.make_async_remote_copy(
            src_ref=outgoing[part].at[hop - early],
            dst_ref=arrived[part].at[pl.ds((hop - early) * capacity, capacity)],
            send_sem=send_sem.at[part, hop - early],
            recv_sem=recv_sem.at[part, hop - early],
            device_id={"tile": receiver(me, hop, count)},
            device_id_type=MESH,
        )

    def each_hop(begin, end, act):
        def one(hop, carry):
            act(hop)
            return carry

        lax.fori_loop(begin, end, one, 0)

    def piece(hop, r, part):
        return warped[route_smem[1, hop * capacity + r], rows_of[part], :]

    def send(part, hop):
        for r in range(capacity):
            outgoing[part][hop - early, r] = piece(hop, r, part)
        message(part, hop).start()

    ready = GROUP // capacity
    steps = blocks // GROUP
    each_hop(0, count - 1, lambda hop: label_message(hop).start())
    warped[...] = jnp.zeros_like(warped)
    view = lambda ref, place: ref.at[pl.ds(place[0], place[1]), pl.ds(0, place[2])]
    rows_in, rows_out, cols_in, cols_out = (view(tables, place) for place in places[:4])
    row_taps, col_taps = (view(wave_table, place) for place in places[4:])
    loads[0].wait()
    tables[...] = wave_table[: tables.shape[0], :].astype(tables.dtype)
    row_wave[...] = lax.dot_general(
        row_taps[...],
        row_bases[...].astype(jnp.float32),
        (((1,), (1,)), ((), ())),
        precision=lax.Precision.HIGHEST,
        preferred_element_type=jnp.float32,
    )
    col_wave[...] = jnp.dot(
        col_bases[...].astype(jnp.float32),
        col_taps[...],
        precision=lax.Precision.HIGHEST,
        preferred_element_type=jnp.float32,
    ).astype(col_wave.dtype)
    for load in loads[2:]:
        load.wait()
    move.wait()

    @pl.when(me > 0)
    def _():
        for copy in down:
            copy.wait_recv()

    @pl.when(me < count - 1)
    def _():
        for copy in up:
            copy.wait_recv()

    transform_rows(reach, rows_in, exposure, (before, after), (fold_before, fold_after), strip)

    def group(step, carry):
        match_group(
            step, route_smem, rows_out, cols_in, cols_out, row_wave, col_wave, coef_ref,
            strip, rows_ref, cols_ref, spectrum, response, warps, waves, warped,
        )
        for number in range(ready):
            hop = step * ready + number
            for r in range(capacity):
                blocks_out[hop, r] = warped[route_smem[1, hop * capacity + r]]
            early_message(hop).start()
        return carry

    lax.fori_loop(0, steps, group, 0)
    for part in range(parts):
        each_hop(early, count - 1, lambda hop, part=part: send(part, hop))
        for r in range(capacity):
            arrived[part][(count - 1 - early) * capacity + r] = piece(count - 1, r, part)

    label_in[count - 1] = labels[count - 1]
    each_hop(0, count - 1, lambda hop: label_message(hop).wait())
    slot_order(label_in, table_int, table_float, weight_sum, tiles * across * across)
    moves = [
        pltpu.make_async_copy(table_int, int_smem, table_sem.at[1]),
        pltpu.make_async_copy(table_float, float_smem, table_sem.at[2]),
    ]
    for move in moves:
        move.start()

    def to_peer(hop, from_ref, to_ref, send_sem, recv_sem):
        return pltpu.make_async_remote_copy(
            src_ref=from_ref,
            dst_ref=to_ref,
            send_sem=send_sem,
            recv_sem=recv_sem,
            device_id={"src": lax.rem(my_src + hop, peers)},
            device_id_type=MESH,
        )

    def weight_message(hop):
        return to_peer(
            hop, weight_sum, weight_in.at[hop - 1], weight_send.at[hop - 1], weight_recv.at[hop - 1]
        )

    def sum_message(part, hop):
        return to_peer(
            hop,
            partial[part].at[lax.rem(my_src + hop, peers)],
            gathered[part].at[hop - 1],
            sum_send.at[part, hop - 1],
            sum_recv.at[part, hop - 1],
        )

    for hop in range(1, peers):
        weight_message(hop).start()
    for move in moves:
        move.wait()

    half = blocks_in.shape[0]
    slots = tiles * across * across

    def stack_early():
        def add(place, total):
            block = blocks_in[int_smem[0, place]].astype(jnp.float32)
            total = total * float_smem[1, place] + float_smem[0, place] * block
            block_sums[place] = total
            return total

        lax.fori_loop(0, half, add, jnp.zeros((side, side), jnp.float32))

        def take(slot, carry):
            base[slot] = block_sums[int_smem[1, slot]] * float_smem[2, slot]
            return carry

        lax.fori_loop(0, slots, take, 0)

    def stack(part):
        high = PARTS[part]

        def add(place, total):
            block = arrived[part][int_smem[0, half + place]].astype(jnp.float32)
            total = total * float_smem[1, half + place] + float_smem[0, half + place] * block
            running[place, :high] = total
            return total

        lax.fori_loop(0, half, add, jnp.zeros((high, side), jnp.float32), unroll=4)

        def take(slot, carry):
            row = lax.rem(slot // across, across)
            place = slot // (across * across) * across + lax.rem(slot, across)
            total = running[int_smem[1, slots + slot], :high] * float_smem[2, slots + slot]
            partial[part][row, place] = (total + base[slot, rows_of[part], :]).astype(jnp.bfloat16)
            return carry

        lax.fori_loop(0, slots, take, 0, unroll=4)

    def finish(part):
        for hop in range(1, peers):
            sum_message(part, hop).wait()
        for tile in range(tiles):
            for column in range(across):
                place = tile * across + column
                total = partial[part][my_src, place].astype(jnp.float32)
                for hop in range(peers - 1):
                    total = total + gathered[part][hop, place].astype(jnp.float32)
                slot = (tile * across + my_src) * across + column
                coadd[tile, rows_of[part], column * side : (column + 1) * side] = total * scale[slot]

    each_hop(0, early, lambda hop: early_message(hop).wait_recv())
    stack_early()
    for part in range(parts):
        each_hop(early, count - 1, lambda hop, part=part: message(part, hop).wait_recv())
        stack(part)
        for hop in range(1, peers):
            sum_message(part, hop).start()
        if part == 0:
            for hop in range(1, peers):
                weight_message(hop).wait()
            weight = weight_sum[...]
            for hop in range(peers - 1):
                weight = weight + weight_in[hop]
            factor = 1.0 / jnp.maximum(weight, 1.0)
            for slot in range(scale.shape[0]):
                scale[slot] = factor[slot : slot + 1]
        else:
            finish(part - 1)
    finish(parts - 1)
    for part in range(parts):
        each_hop(early, count - 1, lambda hop, part=part: message(part, hop).wait_send())
    each_hop(0, early, lambda hop: early_message(hop).wait_send())

    @pl.when(me < count - 1)
    def _():
        for copy in down:
            copy.wait_send()

    @pl.when(me > 0)
    def _():
        for copy in up:
            copy.wait_send()


def body(
    exposure,
    row_bases,
    col_bases,
    coefficients,
    warp_rows,
    warp_cols,
    variance,
    footprint,
    slot_index,
):
    blocks, side = warp_rows.shape[2:4]
    columns = exposure.shape[2]
    basis_count, taps = row_bases.shape
    peers, count = lax.axis_size("src"), lax.axis_size("tile")
    capacity = max(2, 2 * blocks // count)
    slots, sends = TILES_DEV * peers * peers, count * capacity
    reach = taps // 2
    tall = -(-(side + taps - 1) // 16) * 16
    tables, places = wave_tables(
        taps, side, tall, side + taps - 1
    )
    spectra = places[0][1]
    near, far = pl.BlockSpec(memory_space=pltpu.VMEM), pl.BlockSpec(memory_space=pl.ANY)
    parts, per = len(PARTS), slots // peers
    early = blocks // capacity
    late = count - early
    narrow, wide, whole = jnp.bfloat16, jnp.float32, jnp.int32
    vmem, smem, dma = pltpu.VMEM, pltpu.SMEM, pltpu.SemaphoreType.DMA
    return pl.pallas_call(
        functools.partial(coadd_kernel, reach, capacity, places),
        in_specs=[far] * 4 + [near] * 6,
        out_specs=near,
        out_shape=jax.ShapeDtypeStruct((TILES_DEV, side, peers * side), wide),
        scratch_shapes=[
            vmem((side, columns), narrow),
            vmem((EDGE, columns), narrow),
            vmem((EDGE, columns), narrow),
            *[vmem((EDGE, columns // FOLDS + SPAN), narrow)] * 4,
            vmem((columns // SPAN + 1, spectra, SPAN), narrow),
            vmem((places[4][0], 2 * SPAN), narrow),
            vmem(tables.shape, wide),
            vmem((spectra, basis_count), wide),
            vmem((basis_count, 2 * SPAN), narrow),
            vmem((blocks, 1, basis_count), wide),
            vmem((8, sends), whole),
            vmem((8, sends), whole),
            vmem((count, 8, sends), whole),
            vmem((GROUP * spectra, 2 * SPAN), wide),
            vmem((GROUP * spectra, 2 * SPAN), wide),
            vmem((GROUP * side, spectra), narrow),
            vmem((GROUP * side, 2 * SPAN), narrow),
            vmem((blocks, side, side), narrow),
            vmem((blocks, side, side), narrow),
            vmem((blocks, side, side), narrow),
            vmem((early, capacity, side, side), narrow),
            vmem((early * capacity, side, side), narrow),
            vmem((early * capacity, side, side), wide),
            vmem((slots, side, side), wide),
            vmem((count, 8, sends), whole),
            vmem((8, sends), whole),
            vmem((8, sends), wide),
            vmem((slots, sends), wide),
            vmem((peers - 1, slots, sends), wide),
            vmem((slots, 1, sends), wide),
            vmem((late * capacity, max(PARTS), side), wide),
            smem((8, sends), whole),
            smem((8, sends), whole),
            smem((8, sends), wide),
            dma((4,)),
            dma((4,)),
            dma((early,)),
            dma((early,)),
            dma((parts, late)),
            dma((parts, late)),
            dma((count,)),
            dma((count,)),
            dma((4,)),
            dma((3,)),
            dma((parts, peers - 1)),
            dma((parts, peers - 1)),
            dma((peers - 1,)),
            dma((peers - 1,)),
            *[vmem((late, capacity, high, side), narrow) for high in PARTS],
            *[vmem((late * capacity, high, side), narrow) for high in PARTS],
            *[vmem((peers, per, high, side), narrow) for high in PARTS],
            *[vmem((peers - 1, per, high, side), narrow) for high in PARTS],
        ],
        compiler_params=pltpu.CompilerParams(
            collective_id=0, has_side_effects=True, vmem_limit_bytes=60 * 1024 * 1024
        ),
        cost_estimate=pl.CostEstimate(flops=4 << 30, bytes_accessed=10 << 20, transcendentals=0),
    )(
        exposure[0], warp_rows[0, 0], warp_cols[0, 0], tables, row_bases, col_bases,
        coefficients[0].transpose(2, 0, 1), variance[0], footprint.reshape(1, blocks), slot_index[0],
    )


def solution(mesh):
    placed = (
        P("src", "tile", None),
        P(),
        P(),
        P("src", "tile", None, None),
        P("src", "tile", None, None, None),
        P("src", "tile", None, None, None),
        P("src", "tile", None),
        P("src", "tile", None, None),
        P("src", "tile", None),
    )
    return jax.shard_map(
        body, mesh=mesh, in_specs=placed, out_specs=P("tile", "src", None), check_vma=False
    )
```

```python
import functools

import jax
import jax.numpy as jnp
import numpy as np
from jax import lax
from jax.experimental import pallas as pl
from jax.experimental.pallas import tpu as pltpu
from jax.sharding import PartitionSpec as P

TILES_DEV = 4


EDGE = 16
FOLDS = 4
GROUP = 8
SPAN = 128


def wave_tables(taps, side, tall, wide):
    low, lanes = -(-(tall // 2 + 1) // 16) * 16, SPAN
    u, v = np.arange(low), np.arange(lanes)
    keep_u, keep_v = u <= tall // 2, v <= wide // 2
    twice_u = np.where((u == 0) | (2 * u == tall), 1.0, 2.0) * keep_u
    twice_v = np.where((v == 0) | (2 * v == wide), 1.0, 2.0) * keep_v
    turn = lambda one, other, length: 2.0 * np.pi / length * (np.outer(one, other) % length)
    reach, edge = taps // 2, np.arange(EDGE)
    fold = edge % (reach - EDGE)
    starts = (reach + np.arange(side), reach - EDGE + edge, reach + side + edge, fold, reach + side + EDGE + fold)
    down = turn(u, np.concatenate(starts), tall)
    rows_in = np.concatenate([np.cos(down), np.sin(down)]) * np.tile(keep_u, 2)[:, None]
    back = turn(np.arange(side), u, tall)
    rows_out = np.concatenate([np.cos(back) * twice_u, -np.sin(back) * twice_u], axis=1) / tall
    along = turn(np.arange(2 * side), v, wide)
    inside = (np.arange(2 * side) < wide)[:, None]
    cols_in = np.concatenate([np.cos(along), -np.sin(along)], axis=1) * inside * np.tile(keep_v, 2)
    front = turn(v, np.arange(side), wide)
    cols_out = np.concatenate([np.cos(front), -np.sin(front)]) * np.tile(twice_v, 2)[:, None] / wide
    tap_u, tap_v = turn(u, np.arange(taps), tall), turn(np.arange(taps), v, wide)
    row_taps = np.concatenate([np.cos(tap_u), np.sin(tap_u)]) * np.tile(keep_u, 2)[:, None]
    col_taps = np.concatenate([np.cos(tap_v), np.sin(tap_v)], axis=1) * np.tile(keep_v, 2)
    places, rows = [], []
    for table in (rows_in, rows_out, cols_in, cols_out, row_taps, col_taps):
        places.append((sum(part.shape[0] for part in rows), *table.shape))
        rows.append(np.pad(table, ((0, -table.shape[0] % 16), (0, 2 * side - table.shape[1]))))
    return jnp.asarray(np.concatenate(rows), jnp.float32), places


MESH = pl.DeviceIdType.MESH
LINE, CORES = 4, 2
PARTS = (32, 32, 32, 32)
WEIGHT_UNIT = 512.0


def greet(sides):
    barrier = pltpu.get_barrier_semaphore()
    for axis, count, me in sides:
        for hop in range(1, count):
            pl.semaphore_signal(
                barrier, inc=1, device_id={axis: lax.rem(me + hop, count)}, device_id_type=MESH
            )
    return barrier, sum(count - 1 for _, count, _ in sides)


def receiver(me, hop, count):
    turn = lax.rem(hop + 1, count)
    pair = turn // CORES
    dx = lax.rem(pair, LINE)
    dz = lax.rem(pair // LINE + pair, LINE)
    z, x, core = me // (LINE * CORES), lax.rem(me // CORES, LINE), lax.rem(me, CORES)
    sign = 1 - 2 * core
    z, x = lax.rem(z + sign * dz + LINE, LINE), lax.rem(x + sign * dx + LINE, LINE)
    core = lax.rem(core + turn, CORES)
    return (z * LINE + x) * CORES + core


def hop_to(owner, me):
    wide, line = LINE * CORES, LINE - 1
    sign = 1 - 2 * lax.rem(me, CORES)
    dz = (sign * (owner // wide - me // wide)) & line
    dx = (sign * (((owner // CORES) & line) - lax.rem(me // CORES, LINE))) & line
    dc = (owner - me) & (CORES - 1)
    turn = CORES * (LINE * ((dz - dx) & line) + dx) + dc
    return (turn - 1) & (LINE * wide - 1)


def route(me, capacity, owner_ref, slot_ref, variance_ref, route_table, fields):
    blocks, places = owner_ref.shape[1], route_table.shape[1]
    square = (blocks, blocks)
    down, along = (lax.broadcasted_iota(jnp.int32, square, axis) for axis in (0, 1))
    hop_along = jnp.broadcast_to(hop_to(owner_ref[...], me), square)
    hop_down = hop_along.T
    count = lambda mask: jnp.sum(mask.astype(jnp.int32), axis=1, keepdims=True)
    rank = count((hop_along == hop_down) & (along < down))
    position = rank + count(hop_along < hop_down)
    weight = (1.0 / variance_ref[...]).astype(jnp.bfloat16).astype(jnp.float32)
    units = (jnp.broadcast_to(weight, square).T * WEIGHT_UNIT).astype(jnp.int32)[:, :1]
    slot = jnp.broadcast_to(slot_ref[...], square).T[:, :1]
    table = (blocks, places)
    number = lax.broadcasted_iota(jnp.int32, table, 0)
    lane = lax.broadcasted_iota(jnp.int32, table, 1)
    found = lane == hop_down[:, :1] * capacity + rank
    pick = lambda mask, values: jnp.sum(jnp.where(mask, values, 0), axis=0, keepdims=True)
    order = pick(lane == position, number)
    source = pick(found, position)
    route_table[...] = jnp.concatenate([order, source] + [order] * (route_table.shape[0] - 2), axis=0)
    row = [pick(found, units), pick(found, slot)]
    fields[...] = jnp.concatenate(row + [jnp.zeros_like(row[0])] * (fields.shape[0] - 2), axis=0)


def fold_rows(rows):
    part = rows.shape[1] // FOLDS
    zeros = jnp.zeros((rows.shape[0], SPAN), rows.dtype)
    quarters = []
    for fold in range(FOLDS):
        begin = fold * part
        ahead = rows[:, begin - SPAN : begin] if fold else zeros
        quarters.append(jnp.concatenate([ahead, rows[:, begin : begin + part]], axis=1))
    return jnp.concatenate(quarters, axis=0)


def transform_rows(reach, rows_in, exposure, edges, folds, strip):
    columns = exposure.shape[1]
    tiles = 4
    wide = tiles * SPAN
    per_fold = columns // wide // FOLDS
    fold_of_row = lax.broadcasted_iota(jnp.int32, (EDGE, 1), 0) // (EDGE // FOLDS)

    def rows(begin, width):
        return jnp.concatenate([ref[:, pl.ds(begin, width)] for ref in (exposure, *edges)], axis=0)

    def folded(fold, begin, width):
        pieces = [ref[:, pl.ds(begin, width)] for ref in folds]
        mine = fold_of_row == fold
        return jnp.concatenate([jnp.where(mine, piece, 0) for piece in pieces], axis=0)

    def spectra(window):
        return jnp.dot(rows_in[...], window, preferred_element_type=jnp.float32).astype(strip.dtype)

    def store(number, old):
        moved = spectra(old[:, SPAN - reach : SPAN - reach + wide])
        for tile in range(tiles):
            strip[number * tiles + tile] = moved[:, tile * SPAN : (tile + 1) * SPAN]

    def piece(number, carry):
        begin = pl.multiple_of(number * wide - SPAN, SPAN)
        inside = pl.multiple_of(lax.rem(number, per_fold) * wide, wide)
        over = wide + SPAN
        store(
            number,
            jnp.concatenate([rows(begin, over), folded(number // per_fold, inside, over)], axis=0),
        )
        return carry

    total = exposure.shape[0] + EDGE * (len(edges) + len(folds))
    zeros = jnp.zeros((total, SPAN), exposure.dtype)
    first = jnp.concatenate([rows(0, wide), folded(0, SPAN, wide)], axis=0)
    store(0, jnp.concatenate([zeros, first], axis=1))
    lax.fori_loop(1, columns // wide, piece, 0)
    last = [rows(columns - SPAN, SPAN), folded(FOLDS - 1, columns // FOLDS, SPAN)]
    last = jnp.concatenate([jnp.concatenate(last, axis=0), zeros], axis=1)
    strip[columns // SPAN] = spectra(last[:, SPAN - reach : 2 * SPAN - reach])


def match_group(
    step, route_smem, rows_out, cols_in, cols_out, row_wave, col_wave, coef_ref,
    strip, rows_ref, cols_ref, spectrum, response, warps, waves, warped,
):
    low = row_wave.shape[0] // 2
    side = warped.shape[1]
    numbers = [route_smem[0, step * GROUP + q] for q in range(GROUP)]
    windows = [jnp.concatenate([strip[number], strip[number + 1]], axis=1) for number in numbers]
    spectrum[...] = jnp.dot(
        jnp.concatenate(windows, axis=0), cols_in[...], preferred_element_type=jnp.float32
    )
    scaled = [(row_wave[...] * coef_ref[number]).astype(jnp.bfloat16) for number in numbers]
    response[...] = jnp.dot(
        jnp.concatenate(scaled, axis=0), col_wave[...], preferred_element_type=jnp.float32
    )
    warps[...] = jnp.dot(
        jnp.concatenate([rows_ref[number] for number in numbers], axis=0),
        rows_out[...],
        preferred_element_type=jnp.float32,
    ).astype(jnp.bfloat16)
    for q in range(GROUP):
        top = slice(q * 2 * low, q * 2 * low + low)
        end = slice(q * 2 * low + low, (q + 1) * 2 * low)
        p_re, p_im = spectrum[top, :SPAN], spectrum[top, SPAN:]
        q_re, q_im = spectrum[end, :SPAN], spectrum[end, SPAN:]
        a_re, a_im = response[top, :SPAN], response[top, SPAN:]
        b_re, b_im = response[end, :SPAN], response[end, SPAN:]
        even_re = p_re * a_re - p_im * a_im + q_re * b_re - q_im * b_im
        even_im = p_re * a_im + p_im * a_re + q_re * b_im + q_im * b_re
        odd_re = p_re * b_re - p_im * b_im - q_re * a_re + q_im * a_im
        odd_im = p_re * b_im + p_im * b_re - q_re * a_im - q_im * a_re
        stacked = jnp.concatenate(
            [
                jnp.concatenate([even_re, even_im], axis=1),
                jnp.concatenate([odd_re, odd_im], axis=1),
            ],
            axis=0,
        ).astype(jnp.bfloat16)
        waves[q * side : (q + 1) * side, :] = jnp.dot(
            warps[q * side : (q + 1) * side, :], stacked, preferred_element_type=jnp.float32
        ).astype(jnp.bfloat16)
    across = jnp.dot(waves[...], cols_out[...], preferred_element_type=jnp.float32).astype(
        jnp.bfloat16
    )
    for q in range(GROUP):
        warped[step * GROUP + q] = lax.dot_general(
            across[q * side : (q + 1) * side],
            cols_ref[numbers[q]],
            (((1,), (1,)), ((), ())),
            preferred_element_type=jnp.float32,
        ).astype(jnp.bfloat16)


def slot_order(label_in, table_int, table_float, weight_sum, slots):
    labels = label_in[0]
    for source in range(1, label_in.shape[0]):
        labels = labels + label_in[source]
    places = labels.shape[1]
    square = (places, places)
    down, along = (lax.broadcasted_iota(jnp.int32, square, axis) for axis in (0, 1))
    slot_along = jnp.broadcast_to(labels[1:2], square)
    weight_along = jnp.broadcast_to(labels[0:1].astype(jnp.float32) / WEIGHT_UNIT, square)
    slot_down, weight_down = slot_along.T, weight_along.T
    ahead = (slot_along < slot_down) | ((slot_along == slot_down) & (along < down))
    rank = jnp.sum(ahead.astype(jnp.int32), axis=1, keepdims=True)
    chosen = rank == along
    order = jnp.sum(jnp.where(chosen, down, 0), axis=0, keepdims=True)
    slot = jnp.sum(jnp.where(chosen, slot_down, 0), axis=0, keepdims=True)
    weight = jnp.sum(jnp.where(chosen, weight_down, 0.0), axis=0, keepdims=True)
    goes_on = ((slot == pltpu.roll(slot, 1, axis=1)) & (along[:1] > 0)).astype(jnp.float32)
    up_to = jnp.sum((slot_down <= along).astype(jnp.int32), axis=0, keepdims=True)
    inside = jnp.sum((slot_down == along).astype(jnp.int32), axis=0, keepdims=True)
    last = jnp.maximum(up_to - 1, 0)
    table_int[...] = jnp.concatenate([order, last] + [order] * (table_int.shape[0] - 2), axis=0)
    table_float[...] = jnp.concatenate(
        [weight, goes_on, (inside > 0).astype(jnp.float32)] + [weight] * (table_float.shape[0] - 3),
        axis=0,
    )
    mine = jnp.where(slot_along[:slots] == down[:slots], weight_along[:slots], 0.0)
    weight_sum[...] = jnp.broadcast_to(jnp.sum(mine, axis=1, keepdims=True), (slots, places))


def coadd_kernel(
    reach, capacity, places, exposure_hbm, rows_hbm, cols_hbm, tables_hbm,
    row_bases, col_bases, coefficients, variance, owner, slot_index, coadd,
    exposure, before, after, fold_before, fold_after, fold_down, fold_up, strip, tables, wave_table, row_wave, col_wave, coef_ref,
    route_table, fields, labels,
    spectrum, response, warps, waves, warped, rows_ref, cols_ref,
    label_in, table_int, table_float, weight_sum, weight_in, scale, running,
    route_smem, int_smem, float_smem,
    halo_send, halo_recv, send_sem, recv_sem, label_send, label_recv, load_sem, table_sem,
    sum_send, sum_recv, weight_send, weight_recv, *pieces,
):
    parts = len(PARTS)
    outgoing, arrived, partial, gathered = (
        pieces[kind * parts : (kind + 1) * parts] for kind in range(4)
    )
    me, my_src = lax.axis_index("tile"), lax.axis_index("src")
    blocks, side = warped.shape[:2]
    count, peers = labels.shape[0], partial[0].shape[0]
    rows_of = [slice(sum(PARTS[:part]), sum(PARTS[: part + 1])) for part in range(parts)]
    tiles, across = coadd.shape[0], peers
    barrier, greetings = greet((("tile", count, me), ("src", peers, my_src)))
    loads = [
        pltpu.make_async_copy(from_ref, to_ref, load_sem.at[number])
        for number, (from_ref, to_ref) in enumerate(
            (
                (tables_hbm, wave_table),
                (exposure_hbm, exposure),
                (rows_hbm, rows_ref),
                (cols_hbm, cols_ref),
            )
        )
    ]
    for load in loads:
        load.start()
    route(me, capacity, owner, slot_index, variance, route_table, fields)
    move = pltpu.make_async_copy(route_table, route_smem, table_sem.at[0])
    move.start()
    by_block = jnp.concatenate([coefficients[k] for k in range(coefficients.shape[0])], axis=0).T
    for number in range(blocks):
        coef_ref[number] = by_block[number : number + 1, :]
    lane = lax.broadcasted_iota(jnp.int32, fields.shape, 1)
    for hop in range(count):
        moved = pltpu.roll(
            fields[...], lax.rem((me - hop + count) * capacity, lane.shape[1]), axis=1
        )
        labels[hop] = jnp.where(lane // capacity == me, moved, 0)
    loads[1].wait()
    spare = reach - EDGE
    fold_down[...] = fold_rows(exposure[side - 2 * EDGE : side - EDGE, :][EDGE - spare :, :])
    fold_up[...] = fold_rows(exposure[EDGE : 2 * EDGE, :][:spare, :])
    pl.semaphore_wait(barrier, greetings)

    def halo(number, from_ref, to_ref, neighbour):
        return pltpu.make_async_remote_copy(
            src_ref=from_ref,
            dst_ref=to_ref,
            send_sem=halo_send.at[number],
            recv_sem=halo_recv.at[number],
            device_id={"tile": neighbour},
            device_id_type=MESH,
        )

    below, above = lax.rem(me + 1, count), lax.rem(me + count - 1, count)
    down = (
        halo(0, exposure.at[pl.ds(side - EDGE, EDGE)], before, below),
        halo(1, fold_down, fold_before, below),
    )
    up = (halo(2, exposure.at[pl.ds(0, EDGE)], after, above), halo(3, fold_up, fold_after, above))

    @pl.when(me < count - 1)
    def _():
        for copy in down:
            copy.start()

    @pl.when(me > 0)
    def _():
        for copy in up:
            copy.start()

    @pl.when(me == 0)
    def _():
        before[...] = jnp.zeros_like(before)
        fold_before[...] = jnp.zeros_like(fold_before)

    @pl.when(me == count - 1)
    def _():
        after[...] = jnp.zeros_like(after)
        fold_after[...] = jnp.zeros_like(fold_after)

    def label_message(hop):
        return pltpu.make_async_remote_copy(
            src_ref=labels.at[hop],
            dst_ref=label_in.at[me],
            send_sem=label_send.at[hop],
            recv_sem=label_recv.at[hop],
            device_id={"tile": receiver(me, hop, count)},
            device_id_type=MESH,
        )

    def message(part, hop):
        return pltpu.make_async_remote_copy(
            src_ref=outgoing[part].at[hop],
            dst_ref=arrived[part].at[pl.ds(me * capacity, capacity)],
            send_sem=send_sem.at[part, hop],
            recv_sem=recv_sem.at[part, hop],
            device_id={"tile": receiver(me, hop, count)},
            device_id_type=MESH,
        )

    def each_hop(begin, end, act):
        def one(hop, carry):
            act(hop)
            return carry

        lax.fori_loop(begin, end, one, 0)

    def piece(hop, r, part):
        return warped[route_smem[1, hop * capacity + r], rows_of[part], :]

    def send(part, hop):
        for r in range(capacity):
            outgoing[part][hop, r] = piece(hop, r, part)
        message(part, hop).start()

    ready = GROUP // capacity
    steps = blocks // GROUP
    each_hop(0, count - 1, lambda hop: label_message(hop).start())
    warped[...] = jnp.zeros_like(warped)
    view = lambda ref, place: ref.at[pl.ds(place[0], place[1]), pl.ds(0, place[2])]
    rows_in, rows_out, cols_in, cols_out = (view(tables, place) for place in places[:4])
    row_taps, col_taps = (view(wave_table, place) for place in places[4:])
    loads[0].wait()
    tables[...] = wave_table[: tables.shape[0], :].astype(tables.dtype)
    row_wave[...] = lax.dot_general(
        row_taps[...],
        row_bases[...].astype(jnp.float32),
        (((1,), (1,)), ((), ())),
        precision=lax.Precision.HIGHEST,
        preferred_element_type=jnp.float32,
    )
    col_wave[...] = jnp.dot(
        col_bases[...].astype(jnp.float32),
        col_taps[...],
        precision=lax.Precision.HIGHEST,
        preferred_element_type=jnp.float32,
    ).astype(col_wave.dtype)
    for load in loads[2:]:
        load.wait()
    move.wait()

    @pl.when(me > 0)
    def _():
        for copy in down:
            copy.wait_recv()

    @pl.when(me < count - 1)
    def _():
        for copy in up:
            copy.wait_recv()

    transform_rows(reach, rows_in, exposure, (before, after), (fold_before, fold_after), strip)

    def group(step, carry):
        match_group(
            step, route_smem, rows_out, cols_in, cols_out, row_wave, col_wave, coef_ref,
            strip, rows_ref, cols_ref, spectrum, response, warps, waves, warped,
        )
        for hop in range(ready):
            for part in range(parts):
                send(part, step * ready + hop)
        return carry

    lax.fori_loop(0, steps, group, 0)
    for part in range(parts):
        each_hop(steps * ready, count - 1, lambda hop, part=part: send(part, hop))
        for r in range(capacity):
            arrived[part][me * capacity + r] = piece(count - 1, r, part)

    label_in[me] = labels[count - 1]
    each_hop(0, count - 1, lambda hop: label_message(hop).wait())
    slot_order(label_in, table_int, table_float, weight_sum, tiles * across * across)
    moves = [
        pltpu.make_async_copy(table_int, int_smem, table_sem.at[1]),
        pltpu.make_async_copy(table_float, float_smem, table_sem.at[2]),
    ]
    for move in moves:
        move.start()

    def to_peer(hop, from_ref, to_ref, send_sem, recv_sem):
        return pltpu.make_async_remote_copy(
            src_ref=from_ref,
            dst_ref=to_ref,
            send_sem=send_sem,
            recv_sem=recv_sem,
            device_id={"src": lax.rem(my_src + hop, peers)},
            device_id_type=MESH,
        )

    def weight_message(hop):
        return to_peer(
            hop, weight_sum, weight_in.at[hop - 1], weight_send.at[hop - 1], weight_recv.at[hop - 1]
        )

    def sum_message(part, hop):
        return to_peer(
            hop,
            partial[part].at[lax.rem(my_src + hop, peers)],
            gathered[part].at[hop - 1],
            sum_send.at[part, hop - 1],
            sum_recv.at[part, hop - 1],
        )

    for hop in range(1, peers):
        weight_message(hop).start()
    for move in moves:
        move.wait()

    def stack(part):
        high = PARTS[part]

        def add(place, total):
            block = arrived[part][int_smem[0, place]].astype(jnp.float32)
            total = total * float_smem[1, place] + float_smem[0, place] * block
            running[place, :high] = total
            return total

        lax.fori_loop(
            0, arrived[part].shape[0], add, jnp.zeros((high, side), jnp.float32), unroll=4
        )

        def take(slot, carry):
            row = lax.rem(slot // across, across)
            place = slot // (across * across) * across + lax.rem(slot, across)
            total = running[int_smem[1, slot], :high] * float_smem[2, slot]
            partial[part][row, place] = total.astype(jnp.bfloat16)
            return carry

        lax.fori_loop(0, tiles * across * across, take, 0, unroll=4)

    def finish(part):
        for hop in range(1, peers):
            sum_message(part, hop).wait()
        for tile in range(tiles):
            for column in range(across):
                place = tile * across + column
                total = partial[part][my_src, place].astype(jnp.float32)
                for hop in range(peers - 1):
                    total = total + gathered[part][hop, place].astype(jnp.float32)
                slot = (tile * across + my_src) * across + column
                coadd[tile, rows_of[part], column * side : (column + 1) * side] = total * scale[slot]

    for part in range(parts):
        each_hop(0, count - 1, lambda hop, part=part: message(part, hop).wait_recv())
        stack(part)
        for hop in range(1, peers):
            sum_message(part, hop).start()
        if part == 0:
            for hop in range(1, peers):
                weight_message(hop).wait()
            weight = weight_sum[...]
            for hop in range(peers - 1):
                weight = weight + weight_in[hop]
            factor = 1.0 / jnp.maximum(weight, 1.0)
            for slot in range(scale.shape[0]):
                scale[slot] = factor[slot : slot + 1]
        else:
            finish(part - 1)
    finish(parts - 1)
    for part in range(parts):
        each_hop(0, count - 1, lambda hop, part=part: message(part, hop).wait_send())

    @pl.when(me < count - 1)
    def _():
        for copy in down:
            copy.wait_send()

    @pl.when(me > 0)
    def _():
        for copy in up:
            copy.wait_send()


def body(
    exposure,
    row_bases,
    col_bases,
    coefficients,
    warp_rows,
    warp_cols,
    variance,
    footprint,
    slot_index,
):
    blocks, side = warp_rows.shape[2:4]
    columns = exposure.shape[2]
    basis_count, taps = row_bases.shape
    peers, count = lax.axis_size("src"), lax.axis_size("tile")
    capacity = max(2, 2 * blocks // count)
    slots, sends = TILES_DEV * peers * peers, count * capacity
    reach = taps // 2
    tall = -(-(side + taps - 1) // 16) * 16
    tables, places = wave_tables(
        taps, side, tall, side + taps - 1
    )
    spectra = places[0][1]
    near, far = pl.BlockSpec(memory_space=pltpu.VMEM), pl.BlockSpec(memory_space=pl.ANY)
    parts, per = len(PARTS), slots // peers
    narrow, wide, whole = jnp.bfloat16, jnp.float32, jnp.int32
    vmem, smem, dma = pltpu.VMEM, pltpu.SMEM, pltpu.SemaphoreType.DMA
    return pl.pallas_call(
        functools.partial(coadd_kernel, reach, capacity, places),
        in_specs=[far] * 4 + [near] * 6,
        out_specs=near,
        out_shape=jax.ShapeDtypeStruct((TILES_DEV, side, peers * side), wide),
        scratch_shapes=[
            vmem((side, columns), narrow),
            vmem((EDGE, columns), narrow),
            vmem((EDGE, columns), narrow),
            *[vmem((EDGE, columns // FOLDS + SPAN), narrow)] * 4,
            vmem((columns // SPAN + 1, spectra, SPAN), narrow),
            vmem((places[4][0], 2 * SPAN), narrow),
            vmem(tables.shape, wide),
            vmem((spectra, basis_count), wide),
            vmem((basis_count, 2 * SPAN), narrow),
            vmem((blocks, 1, basis_count), wide),
            vmem((8, sends), whole),
            vmem((8, sends), whole),
            vmem((count, 8, sends), whole),
            vmem((GROUP * spectra, 2 * SPAN), wide),
            vmem((GROUP * spectra, 2 * SPAN), wide),
            vmem((GROUP * side, spectra), narrow),
            vmem((GROUP * side, 2 * SPAN), narrow),
            vmem((blocks, side, side), narrow),
            vmem((blocks, side, side), narrow),
            vmem((blocks, side, side), narrow),
            vmem((count, 8, sends), whole),
            vmem((8, sends), whole),
            vmem((8, sends), wide),
            vmem((slots, sends), wide),
            vmem((peers - 1, slots, sends), wide),
            vmem((slots, 1, sends), wide),
            vmem((sends, max(PARTS), side), wide),
            smem((8, sends), whole),
            smem((8, sends), whole),
            smem((8, sends), wide),
            dma((4,)),
            dma((4,)),
            dma((parts, count)),
            dma((parts, count)),
            dma((count,)),
            dma((count,)),
            dma((4,)),
            dma((3,)),
            dma((parts, peers - 1)),
            dma((parts, peers - 1)),
            dma((peers - 1,)),
            dma((peers - 1,)),
            *[vmem((count, capacity, high, side), narrow) for high in PARTS],
            *[vmem((sends, high, side), narrow) for high in PARTS],
            *[vmem((peers, per, high, side), narrow) for high in PARTS],
            *[vmem((peers - 1, per, high, side), narrow) for high in PARTS],
        ],
        compiler_params=pltpu.CompilerParams(
            collective_id=0, has_side_effects=True, vmem_limit_bytes=60 * 1024 * 1024
        ),
        cost_estimate=pl.CostEstimate(flops=4 << 30, bytes_accessed=10 << 20, transcendentals=0),
    )(
        exposure[0], warp_rows[0, 0], warp_cols[0, 0], tables, row_bases, col_bases,
        coefficients[0].transpose(2, 0, 1), variance[0], footprint.reshape(1, blocks), slot_index[0],
    )


def solution(mesh):
    placed = (
        P("src", "tile", None),
        P(),
        P(),
        P("src", "tile", None, None),
        P("src", "tile", None, None, None),
        P("src", "tile", None, None, None),
        P("src", "tile", None),
        P("src", "tile", None, None),
        P("src", "tile", None),
    )
    return jax.shard_map(
        body, mesh=mesh, in_specs=placed, out_specs=P("tile", "src", None), check_vma=False
    )
```

```python
import functools

import jax
import jax.numpy as jnp
import numpy as np
from jax import lax
from jax.experimental import pallas as pl
from jax.experimental.pallas import tpu as pltpu
from jax.sharding import PartitionSpec as P

TILES_DEV = 4


EDGE = 16
FOLDS = 4
GROUP = 8
SPAN = 128


def wave_tables(taps, side, tall, wide):
    low, lanes = -(-(tall // 2 + 1) // 16) * 16, SPAN
    u, v = np.arange(low), np.arange(lanes)
    keep_u, keep_v = u <= tall // 2, v <= wide // 2
    twice_u = np.where((u == 0) | (2 * u == tall), 1.0, 2.0) * keep_u
    twice_v = np.where((v == 0) | (2 * v == wide), 1.0, 2.0) * keep_v
    turn = lambda one, other, length: 2.0 * np.pi / length * (np.outer(one, other) % length)
    reach, edge = taps // 2, np.arange(EDGE)
    fold = edge % (reach - EDGE)
    starts = (reach + np.arange(side), reach - EDGE + edge, reach + side + edge, fold, reach + side + EDGE + fold)
    down = turn(u, np.concatenate(starts), tall)
    rows_in = np.concatenate([np.cos(down), np.sin(down)]) * np.tile(keep_u, 2)[:, None]
    back = turn(np.arange(side), u, tall)
    rows_out = np.concatenate([np.cos(back) * twice_u, -np.sin(back) * twice_u], axis=1) / tall
    along = turn(np.arange(2 * side), v, wide)
    inside = (np.arange(2 * side) < wide)[:, None]
    cols_in = np.concatenate([np.cos(along), -np.sin(along)], axis=1) * inside * np.tile(keep_v, 2)
    front = turn(v, np.arange(side), wide)
    cols_out = np.concatenate([np.cos(front), -np.sin(front)]) * np.tile(twice_v, 2)[:, None] / wide
    tap_u, tap_v = turn(u, np.arange(taps), tall), turn(np.arange(taps), v, wide)
    row_taps = np.concatenate([np.cos(tap_u), np.sin(tap_u)]) * np.tile(keep_u, 2)[:, None]
    col_taps = np.concatenate([np.cos(tap_v), np.sin(tap_v)], axis=1) * np.tile(keep_v, 2)
    places, rows = [], []
    for table in (rows_in, rows_out, cols_in, cols_out, row_taps, col_taps):
        places.append((sum(part.shape[0] for part in rows), *table.shape))
        rows.append(np.pad(table, ((0, -table.shape[0] % 16), (0, 2 * side - table.shape[1]))))
    return jnp.asarray(np.concatenate(rows), jnp.float32), places


MESH = pl.DeviceIdType.MESH
LINE, CORES = 4, 2
PARTS = (32, 32, 32, 32)
WEIGHT_UNIT = 512.0


def greet(sides):
    barrier = pltpu.get_barrier_semaphore()
    for axis, count, me in sides:
        for hop in range(1, count):
            pl.semaphore_signal(
                barrier, inc=1, device_id={axis: lax.rem(me + hop, count)}, device_id_type=MESH
            )
    return barrier, sum(count - 1 for _, count, _ in sides)


def receiver(me, hop, count):
    turn = lax.rem(hop + 1, count)
    pair = turn // CORES
    dx = lax.rem(pair, LINE)
    dz = lax.rem(pair // LINE + pair, LINE)
    z, x, core = me // (LINE * CORES), lax.rem(me // CORES, LINE), lax.rem(me, CORES)
    sign = 1 - 2 * core
    z, x = lax.rem(z + sign * dz + LINE, LINE), lax.rem(x + sign * dx + LINE, LINE)
    core = lax.rem(core + turn, CORES)
    return (z * LINE + x) * CORES + core


def hop_to(owner, me):
    wide, line = LINE * CORES, LINE - 1
    sign = 1 - 2 * lax.rem(me, CORES)
    dz = (sign * (owner // wide - me // wide)) & line
    dx = (sign * (((owner // CORES) & line) - lax.rem(me // CORES, LINE))) & line
    dc = (owner - me) & (CORES - 1)
    turn = CORES * (LINE * ((dz - dx) & line) + dx) + dc
    return (turn - 1) & (LINE * wide - 1)


def route(me, capacity, owner_ref, slot_ref, variance_ref, route_table, fields):
    blocks, places = owner_ref.shape[1], route_table.shape[1]
    square = (blocks, blocks)
    down, along = (lax.broadcasted_iota(jnp.int32, square, axis) for axis in (0, 1))
    hop_along = jnp.broadcast_to(hop_to(owner_ref[...], me), square)
    hop_down = hop_along.T
    count = lambda mask: jnp.sum(mask.astype(jnp.int32), axis=1, keepdims=True)
    rank = count((hop_along == hop_down) & (along < down))
    position = rank + count(hop_along < hop_down)
    weight = (1.0 / variance_ref[...]).astype(jnp.bfloat16).astype(jnp.float32)
    units = (jnp.broadcast_to(weight, square).T * WEIGHT_UNIT).astype(jnp.int32)[:, :1]
    slot = jnp.broadcast_to(slot_ref[...], square).T[:, :1]
    table = (blocks, places)
    number = lax.broadcasted_iota(jnp.int32, table, 0)
    lane = lax.broadcasted_iota(jnp.int32, table, 1)
    found = lane == hop_down[:, :1] * capacity + rank
    pick = lambda mask, values: jnp.sum(jnp.where(mask, values, 0), axis=0, keepdims=True)
    order = pick(lane == position, number)
    source = pick(found, position)
    route_table[...] = jnp.concatenate([order, source] + [order] * (route_table.shape[0] - 2), axis=0)
    row = [pick(found, units), pick(found, slot)]
    fields[...] = jnp.concatenate(row + [jnp.zeros_like(row[0])] * (fields.shape[0] - 2), axis=0)


def fold_rows(rows):
    part = rows.shape[1] // FOLDS
    zeros = jnp.zeros((rows.shape[0], SPAN), rows.dtype)
    quarters = []
    for fold in range(FOLDS):
        begin = fold * part
        ahead = rows[:, begin - SPAN : begin] if fold else zeros
        quarters.append(jnp.concatenate([ahead, rows[:, begin : begin + part]], axis=1))
    return jnp.concatenate(quarters, axis=0)


def each_window(reach, columns, rows, use):
    wide = 4 * SPAN

    def store(number, old):
        use(number * 4, old[:, SPAN - reach : SPAN - reach + wide])

    def piece(number, carry):
        store(number, rows(number, pl.multiple_of(number * wide - SPAN, SPAN), wide + SPAN))
        return carry

    first = rows(0, 0, wide)
    zeros = jnp.zeros((first.shape[0], SPAN), first.dtype)
    store(0, jnp.concatenate([zeros, first], axis=1))
    lax.fori_loop(1, columns // wide, piece, 0)
    last = jnp.concatenate([rows(columns // wide, columns - SPAN, SPAN), zeros], axis=1)
    use(columns // SPAN, last[:, SPAN - reach : 2 * SPAN - reach])


def transform_own(reach, rows_in, exposure, sums):
    def use(entry, window):
        part = jnp.dot(
            rows_in[...][:, : exposure.shape[0]], window, preferred_element_type=jnp.float32
        )
        for tile in range(window.shape[1] // SPAN):
            sums[entry + tile] = part[:, tile * SPAN : (tile + 1) * SPAN]

    rows = lambda number, begin, width: exposure[:, pl.ds(begin, width)]
    each_window(reach, exposure.shape[1], rows, use)


def transform_halos(reach, rows_in, exposure, edges, folds, sums, strip):
    columns = exposure.shape[1]
    per_fold = columns // FOLDS // (4 * SPAN)
    fold_of_row = lax.broadcasted_iota(jnp.int32, (EDGE, 1), 0) // (EDGE // FOLDS)

    def rows(number, begin, width):
        fold = jnp.minimum(number // per_fold, FOLDS - 1)
        inside = pl.multiple_of(begin + SPAN - fold * (columns // FOLDS), SPAN)
        mine = fold_of_row == fold
        halves = [ref[:, pl.ds(begin, width)] for ref in edges]
        halves += [jnp.where(mine, ref[:, pl.ds(inside, width)], 0) for ref in folds]
        return jnp.concatenate(halves, axis=0)

    def use(entry, window):
        part = jnp.dot(
            rows_in[...][:, exposure.shape[0] :], window, preferred_element_type=jnp.float32
        )
        for tile in range(window.shape[1] // SPAN):
            total = part[:, tile * SPAN : (tile + 1) * SPAN] + sums[entry + tile]
            strip[entry + tile] = total.astype(strip.dtype)

    each_window(reach, columns, rows, use)


def match_group(
    begin, size, route_smem, rows_out, cols_in, cols_out, row_wave, col_wave, coef_ref,
    strip, rows_ref, cols_ref, spectrum, response, warps, waves, warped,
):
    low = row_wave.shape[0] // 2
    side = warped.shape[1]
    numbers = [route_smem[0, begin + q] for q in range(size)]
    depth = size * 2 * low
    windows = [jnp.concatenate([strip[number], strip[number + 1]], axis=1) for number in numbers]
    spectrum[:depth] = jnp.dot(
        jnp.concatenate(windows, axis=0), cols_in[...], preferred_element_type=jnp.float32
    )
    scaled = [(row_wave[...] * coef_ref[number]).astype(jnp.bfloat16) for number in numbers]
    response[:depth] = jnp.dot(
        jnp.concatenate(scaled, axis=0), col_wave[...], preferred_element_type=jnp.float32
    )
    warps[: size * side] = jnp.dot(
        jnp.concatenate([rows_ref[number] for number in numbers], axis=0),
        rows_out[...],
        preferred_element_type=jnp.float32,
    ).astype(jnp.bfloat16)
    for q in range(size):
        top = slice(q * 2 * low, q * 2 * low + low)
        end = slice(q * 2 * low + low, (q + 1) * 2 * low)
        p_re, p_im = spectrum[top, :SPAN], spectrum[top, SPAN:]
        q_re, q_im = spectrum[end, :SPAN], spectrum[end, SPAN:]
        a_re, a_im = response[top, :SPAN], response[top, SPAN:]
        b_re, b_im = response[end, :SPAN], response[end, SPAN:]
        even_re = p_re * a_re - p_im * a_im + q_re * b_re - q_im * b_im
        even_im = p_re * a_im + p_im * a_re + q_re * b_im + q_im * b_re
        odd_re = p_re * b_re - p_im * b_im - q_re * a_re + q_im * a_im
        odd_im = p_re * b_im + p_im * b_re - q_re * a_im - q_im * a_re
        stacked = jnp.concatenate(
            [
                jnp.concatenate([even_re, even_im], axis=1),
                jnp.concatenate([odd_re, odd_im], axis=1),
            ],
            axis=0,
        ).astype(jnp.bfloat16)
        waves[q * side : (q + 1) * side, :] = jnp.dot(
            warps[q * side : (q + 1) * side, :], stacked, preferred_element_type=jnp.float32
        ).astype(jnp.bfloat16)
    across = jnp.dot(waves[: size * side], cols_out[...], preferred_element_type=jnp.float32).astype(
        jnp.bfloat16
    )
    for q in range(size):
        warped[begin + q] = lax.dot_general(
            across[q * side : (q + 1) * side],
            cols_ref[numbers[q]],
            (((1,), (1,)), ((), ())),
            preferred_element_type=jnp.float32,
        ).astype(jnp.bfloat16)


def slot_order(label_in, table_int, table_float, weight_sum, slots):
    labels = label_in[0]
    for source in range(1, label_in.shape[0]):
        labels = labels + label_in[source]
    places = labels.shape[1]
    square = (places, places)
    down, along = (lax.broadcasted_iota(jnp.int32, square, axis) for axis in (0, 1))
    slot_along = jnp.broadcast_to(labels[1:2], square)
    weight_along = jnp.broadcast_to(labels[0:1].astype(jnp.float32) / WEIGHT_UNIT, square)
    slot_down, weight_down = slot_along.T, weight_along.T
    ahead = (slot_along < slot_down) | ((slot_along == slot_down) & (along < down))
    rank = jnp.sum(ahead.astype(jnp.int32), axis=1, keepdims=True)
    chosen = rank == along
    order = jnp.sum(jnp.where(chosen, down, 0), axis=0, keepdims=True)
    slot = jnp.sum(jnp.where(chosen, slot_down, 0), axis=0, keepdims=True)
    weight = jnp.sum(jnp.where(chosen, weight_down, 0.0), axis=0, keepdims=True)
    goes_on = ((slot == pltpu.roll(slot, 1, axis=1)) & (along[:1] > 0)).astype(jnp.float32)
    up_to = jnp.sum((slot_down <= along).astype(jnp.int32), axis=0, keepdims=True)
    inside = jnp.sum((slot_down == along).astype(jnp.int32), axis=0, keepdims=True)
    last = jnp.maximum(up_to - 1, 0)
    table_int[...] = jnp.concatenate([order, last] + [order] * (table_int.shape[0] - 2), axis=0)
    table_float[...] = jnp.concatenate(
        [weight, goes_on, (inside > 0).astype(jnp.float32)] + [weight] * (table_float.shape[0] - 3),
        axis=0,
    )
    mine = jnp.where(slot_along[:slots] == down[:slots], weight_along[:slots], 0.0)
    weight_sum[...] = jnp.broadcast_to(jnp.sum(mine, axis=1, keepdims=True), (slots, places))


def coadd_kernel(
    reach, capacity, places, exposure_hbm, rows_hbm, cols_hbm, tables_hbm,
    row_bases, col_bases, coefficients, variance, owner, slot_index, coadd,
    exposure, before, after, fold_before, fold_after, fold_down, fold_up, sums, strip, tables, wave_table, row_wave, col_wave, coef_ref,
    route_table, fields, labels,
    spectrum, response, warps, waves, warped, rows_ref, cols_ref,
    label_in, table_int, table_float, weight_sum, weight_in, scale, running,
    route_smem, int_smem, float_smem,
    halo_send, halo_recv, send_sem, recv_sem, label_send, label_recv, load_sem, table_sem,
    sum_send, sum_recv, weight_send, weight_recv, *pieces,
):
    parts = len(PARTS)
    outgoing, arrived, partial, gathered = (
        pieces[kind * parts : (kind + 1) * parts] for kind in range(4)
    )
    me, my_src = lax.axis_index("tile"), lax.axis_index("src")
    blocks, side = warped.shape[:2]
    count, peers = labels.shape[0], partial[0].shape[0]
    rows_of = [slice(sum(PARTS[:part]), sum(PARTS[: part + 1])) for part in range(parts)]
    tiles, across = coadd.shape[0], peers
    barrier, greetings = greet((("tile", count, me), ("src", peers, my_src)))
    loads = [
        pltpu.make_async_copy(from_ref, to_ref, load_sem.at[number])
        for number, (from_ref, to_ref) in enumerate(
            (
                (tables_hbm, wave_table),
                (exposure_hbm, exposure),
                (rows_hbm, rows_ref),
                (cols_hbm, cols_ref),
            )
        )
    ]
    for load in loads:
        load.start()
    route(me, capacity, owner, slot_index, variance, route_table, fields)
    move = pltpu.make_async_copy(route_table, route_smem, table_sem.at[0])
    move.start()
    by_block = jnp.concatenate([coefficients[k] for k in range(coefficients.shape[0])], axis=0).T
    for number in range(blocks):
        coef_ref[number] = by_block[number : number + 1, :]
    lane = lax.broadcasted_iota(jnp.int32, fields.shape, 1)
    for hop in range(count):
        moved = pltpu.roll(
            fields[...], lax.rem((me - hop + count) * capacity, lane.shape[1]), axis=1
        )
        labels[hop] = jnp.where(lane // capacity == me, moved, 0)
    loads[1].wait()
    spare = reach - EDGE
    fold_down[...] = fold_rows(exposure[side - 2 * EDGE : side - EDGE, :][EDGE - spare :, :])
    fold_up[...] = fold_rows(exposure[EDGE : 2 * EDGE, :][:spare, :])
    pl.semaphore_wait(barrier, greetings)

    def halo(number, from_ref, to_ref, neighbour):
        return pltpu.make_async_remote_copy(
            src_ref=from_ref,
            dst_ref=to_ref,
            send_sem=halo_send.at[number],
            recv_sem=halo_recv.at[number],
            device_id={"tile": neighbour},
            device_id_type=MESH,
        )

    below, above = lax.rem(me + 1, count), lax.rem(me + count - 1, count)
    down = (
        halo(0, exposure.at[pl.ds(side - EDGE, EDGE)], before, below),
        halo(1, fold_down, fold_before, below),
    )
    up = (halo(2, exposure.at[pl.ds(0, EDGE)], after, above), halo(3, fold_up, fold_after, above))

    @pl.when(me < count - 1)
    def _():
        for copy in down:
            copy.start()

    @pl.when(me > 0)
    def _():
        for copy in up:
            copy.start()

    @pl.when(me == 0)
    def _():
        before[...] = jnp.zeros_like(before)
        fold_before[...] = jnp.zeros_like(fold_before)

    @pl.when(me == count - 1)
    def _():
        after[...] = jnp.zeros_like(after)
        fold_after[...] = jnp.zeros_like(fold_after)

    def label_message(hop):
        return pltpu.make_async_remote_copy(
            src_ref=labels.at[hop],
            dst_ref=label_in.at[me],
            send_sem=label_send.at[hop],
            recv_sem=label_recv.at[hop],
            device_id={"tile": receiver(me, hop, count)},
            device_id_type=MESH,
        )

    def message(part, hop):
        return pltpu.make_async_remote_copy(
            src_ref=outgoing[part].at[hop],
            dst_ref=arrived[part].at[pl.ds(me * capacity, capacity)],
            send_sem=send_sem.at[part, hop],
            recv_sem=recv_sem.at[part, hop],
            device_id={"tile": receiver(me, hop, count)},
            device_id_type=MESH,
        )

    def each_hop(begin, end, act):
        def one(hop, carry):
            act(hop)
            return carry

        lax.fori_loop(begin, end, one, 0)

    def piece(hop, r, part):
        return warped[route_smem[1, hop * capacity + r], rows_of[part], :]

    def send(part, hop):
        for r in range(capacity):
            outgoing[part][hop, r] = piece(hop, r, part)
        message(part, hop).start()

    ready = GROUP // capacity
    steps = blocks // GROUP
    each_hop(0, count - 1, lambda hop: label_message(hop).start())
    warped[...] = jnp.zeros_like(warped)
    view = lambda ref, place: ref.at[pl.ds(place[0], place[1]), pl.ds(0, place[2])]
    rows_in, rows_out, cols_in, cols_out = (view(tables, place) for place in places[:4])
    row_taps, col_taps = (view(wave_table, place) for place in places[4:])
    loads[0].wait()
    tables[...] = wave_table[: tables.shape[0], :].astype(tables.dtype)
    row_wave[...] = lax.dot_general(
        row_taps[...],
        row_bases[...].astype(jnp.float32),
        (((1,), (1,)), ((), ())),
        precision=lax.Precision.HIGHEST,
        preferred_element_type=jnp.float32,
    )
    col_wave[...] = jnp.dot(
        col_bases[...].astype(jnp.float32),
        col_taps[...],
        precision=lax.Precision.HIGHEST,
        preferred_element_type=jnp.float32,
    ).astype(col_wave.dtype)
    transform_own(reach, rows_in, exposure, sums)
    for load in loads[2:]:
        load.wait()
    move.wait()

    @pl.when(me > 0)
    def _():
        for copy in down:
            copy.wait_recv()

    @pl.when(me < count - 1)
    def _():
        for copy in up:
            copy.wait_recv()

    transform_halos(reach, rows_in, exposure, (before, after), (fold_before, fold_after), sums, strip)

    def group(size, step, carry):
        match_group(
            step * size, size, route_smem, rows_out, cols_in, cols_out, row_wave, col_wave, coef_ref,
            strip, rows_ref, cols_ref, spectrum, response, warps, waves, warped,
        )
        for number in range(size // capacity):
            for part in range(parts):
                send(part, step * (size // capacity) + number)
        return carry

    lax.fori_loop(0, ready, functools.partial(group, capacity), 0)
    lax.fori_loop(1, steps, functools.partial(group, GROUP), 0)
    for part in range(parts):
        each_hop(steps * ready, count - 1, lambda hop, part=part: send(part, hop))
        for r in range(capacity):
            arrived[part][me * capacity + r] = piece(count - 1, r, part)

    label_in[me] = labels[count - 1]
    each_hop(0, count - 1, lambda hop: label_message(hop).wait())
    slot_order(label_in, table_int, table_float, weight_sum, tiles * across * across)
    moves = [
        pltpu.make_async_copy(table_int, int_smem, table_sem.at[1]),
        pltpu.make_async_copy(table_float, float_smem, table_sem.at[2]),
    ]
    for move in moves:
        move.start()

    def to_peer(hop, from_ref, to_ref, send_sem, recv_sem):
        return pltpu.make_async_remote_copy(
            src_ref=from_ref,
            dst_ref=to_ref,
            send_sem=send_sem,
            recv_sem=recv_sem,
            device_id={"src": lax.rem(my_src + hop, peers)},
            device_id_type=MESH,
        )

    def weight_message(hop):
        return to_peer(
            hop, weight_sum, weight_in.at[hop - 1], weight_send.at[hop - 1], weight_recv.at[hop - 1]
        )

    def sum_message(part, hop):
        return to_peer(
            hop,
            partial[part].at[lax.rem(my_src + hop, peers)],
            gathered[part].at[hop - 1],
            sum_send.at[part, hop - 1],
            sum_recv.at[part, hop - 1],
        )

    for hop in range(1, peers):
        weight_message(hop).start()
    for move in moves:
        move.wait()

    def stack(part):
        high = PARTS[part]

        def add(place, total):
            block = arrived[part][int_smem[0, place]].astype(jnp.float32)
            total = total * float_smem[1, place] + float_smem[0, place] * block
            running[place, :high] = total
            return total

        lax.fori_loop(
            0, arrived[part].shape[0], add, jnp.zeros((high, side), jnp.float32), unroll=4
        )

        def take(slot, carry):
            row = lax.rem(slot // across, across)
            place = slot // (across * across) * across + lax.rem(slot, across)
            total = running[int_smem[1, slot], :high] * float_smem[2, slot]
            partial[part][row, place] = total.astype(jnp.bfloat16)
            return carry

        lax.fori_loop(0, tiles * across * across, take, 0, unroll=4)

    def finish(part):
        for hop in range(1, peers):
            sum_message(part, hop).wait()
        for tile in range(tiles):
            for column in range(across):
                place = tile * across + column
                total = partial[part][my_src, place].astype(jnp.float32)
                for hop in range(peers - 1):
                    total = total + gathered[part][hop, place].astype(jnp.float32)
                slot = (tile * across + my_src) * across + column
                coadd[tile, rows_of[part], column * side : (column + 1) * side] = total * scale[slot]

    for part in range(parts):
        each_hop(0, count - 1, lambda hop, part=part: message(part, hop).wait_recv())
        stack(part)
        for hop in range(1, peers):
            sum_message(part, hop).start()
        if part == 0:
            for hop in range(1, peers):
                weight_message(hop).wait()
            weight = weight_sum[...]
            for hop in range(peers - 1):
                weight = weight + weight_in[hop]
            factor = 1.0 / jnp.maximum(weight, 1.0)
            for slot in range(scale.shape[0]):
                scale[slot] = factor[slot : slot + 1]
        else:
            finish(part - 1)
    finish(parts - 1)
    for part in range(parts):
        each_hop(0, count - 1, lambda hop, part=part: message(part, hop).wait_send())

    @pl.when(me < count - 1)
    def _():
        for copy in down:
            copy.wait_send()

    @pl.when(me > 0)
    def _():
        for copy in up:
            copy.wait_send()


def body(
    exposure,
    row_bases,
    col_bases,
    coefficients,
    warp_rows,
    warp_cols,
    variance,
    footprint,
    slot_index,
):
    blocks, side = warp_rows.shape[2:4]
    columns = exposure.shape[2]
    basis_count, taps = row_bases.shape
    peers, count = lax.axis_size("src"), lax.axis_size("tile")
    capacity = max(2, 2 * blocks // count)
    slots, sends = TILES_DEV * peers * peers, count * capacity
    reach = taps // 2
    tall = -(-(side + taps - 1) // 16) * 16
    tables, places = wave_tables(
        taps, side, tall, side + taps - 1
    )
    spectra = places[0][1]
    near, far = pl.BlockSpec(memory_space=pltpu.VMEM), pl.BlockSpec(memory_space=pl.ANY)
    parts, per = len(PARTS), slots // peers
    narrow, wide, whole = jnp.bfloat16, jnp.float32, jnp.int32
    vmem, smem, dma = pltpu.VMEM, pltpu.SMEM, pltpu.SemaphoreType.DMA
    return pl.pallas_call(
        functools.partial(coadd_kernel, reach, capacity, places),
        in_specs=[far] * 4 + [near] * 6,
        out_specs=near,
        out_shape=jax.ShapeDtypeStruct((TILES_DEV, side, peers * side), wide),
        scratch_shapes=[
            vmem((side, columns), narrow),
            vmem((EDGE, columns), narrow),
            vmem((EDGE, columns), narrow),
            *[vmem((EDGE, columns // FOLDS + SPAN), narrow)] * 4,
            vmem((columns // SPAN + 1, spectra, SPAN), wide),
            vmem((columns // SPAN + 1, spectra, SPAN), narrow),
            vmem((places[4][0], 2 * SPAN), narrow),
            vmem(tables.shape, wide),
            vmem((spectra, basis_count), wide),
            vmem((basis_count, 2 * SPAN), narrow),
            vmem((blocks, 1, basis_count), wide),
            vmem((8, sends), whole),
            vmem((8, sends), whole),
            vmem((count, 8, sends), whole),
            vmem((GROUP * spectra, 2 * SPAN), wide),
            vmem((GROUP * spectra, 2 * SPAN), wide),
            vmem((GROUP * side, spectra), narrow),
            vmem((GROUP * side, 2 * SPAN), narrow),
            vmem((blocks, side, side), narrow),
            vmem((blocks, side, side), narrow),
            vmem((blocks, side, side), narrow),
            vmem((count, 8, sends), whole),
            vmem((8, sends), whole),
            vmem((8, sends), wide),
            vmem((slots, sends), wide),
            vmem((peers - 1, slots, sends), wide),
            vmem((slots, 1, sends), wide),
            vmem((sends, max(PARTS), side), wide),
            smem((8, sends), whole),
            smem((8, sends), whole),
            smem((8, sends), wide),
            dma((4,)),
            dma((4,)),
            dma((parts, count)),
            dma((parts, count)),
            dma((count,)),
            dma((count,)),
            dma((4,)),
            dma((3,)),
            dma((parts, peers - 1)),
            dma((parts, peers - 1)),
            dma((peers - 1,)),
            dma((peers - 1,)),
            *[vmem((count, capacity, high, side), narrow) for high in PARTS],
            *[vmem((sends, high, side), narrow) for high in PARTS],
            *[vmem((peers, per, high, side), narrow) for high in PARTS],
            *[vmem((peers - 1, per, high, side), narrow) for high in PARTS],
        ],
        compiler_params=pltpu.CompilerParams(
            collective_id=0, has_side_effects=True, vmem_limit_bytes=60 * 1024 * 1024
        ),
        cost_estimate=pl.CostEstimate(flops=4 << 30, bytes_accessed=10 << 20, transcendentals=0),
    )(
        exposure[0], warp_rows[0, 0], warp_cols[0, 0], tables, row_bases, col_bases,
        coefficients[0].transpose(2, 0, 1), variance[0], footprint.reshape(1, blocks), slot_index[0],
    )


def solution(mesh):
    placed = (
        P("src", "tile", None),
        P(),
        P(),
        P("src", "tile", None, None),
        P("src", "tile", None, None, None),
        P("src", "tile", None, None, None),
        P("src", "tile", None),
        P("src", "tile", None, None),
        P("src", "tile", None),
    )
    return jax.shard_map(
        body, mesh=mesh, in_specs=placed, out_specs=P("tile", "src", None), check_vma=False
    )
```

```python
import functools

import jax
import jax.numpy as jnp
import numpy as np
from jax import lax
from jax.experimental import pallas as pl
from jax.experimental.pallas import tpu as pltpu
from jax.sharding import PartitionSpec as P

TILES_DEV = 4


EDGE = 16
FOLDS = 4
GROUP = 8
SPAN = 128


def wave_tables(taps, side, tall, wide):
    low, lanes = -(-(tall // 2 + 1) // 16) * 16, SPAN
    u, v = np.arange(low), np.arange(lanes)
    keep_u, keep_v = u <= tall // 2, v <= wide // 2
    twice_u = np.where((u == 0) | (2 * u == tall), 1.0, 2.0) * keep_u
    twice_v = np.where((v == 0) | (2 * v == wide), 1.0, 2.0) * keep_v
    turn = lambda one, other, length: 2.0 * np.pi / length * (np.outer(one, other) % length)
    reach, edge = taps // 2, np.arange(EDGE)
    fold = edge % (reach - EDGE)
    starts = (reach + np.arange(side), reach - EDGE + edge, reach + side + edge, fold, reach + side + EDGE + fold)
    down = turn(u, np.concatenate(starts), tall)
    rows_in = np.concatenate([np.cos(down), np.sin(down)]) * np.tile(keep_u, 2)[:, None]
    back = turn(np.arange(side), u, tall)
    rows_out = np.concatenate([np.cos(back) * twice_u, -np.sin(back) * twice_u], axis=1) / tall
    along = turn(np.arange(2 * side), v, wide)
    inside = (np.arange(2 * side) < wide)[:, None]
    cols_in = np.concatenate([np.cos(along), -np.sin(along)], axis=1) * inside * np.tile(keep_v, 2)
    front = turn(v, np.arange(side), wide)
    cols_out = np.concatenate([np.cos(front), -np.sin(front)]) * np.tile(twice_v, 2)[:, None] / wide
    tap_u, tap_v = turn(u, np.arange(taps), tall), turn(np.arange(taps), v, wide)
    row_taps = np.concatenate([np.cos(tap_u), np.sin(tap_u)]) * np.tile(keep_u, 2)[:, None]
    col_taps = np.concatenate([np.cos(tap_v), np.sin(tap_v)], axis=1) * np.tile(keep_v, 2)
    places, rows = [], []
    for table in (rows_in, rows_out, cols_in, cols_out, row_taps, col_taps):
        places.append((sum(part.shape[0] for part in rows), *table.shape))
        rows.append(np.pad(table, ((0, -table.shape[0] % 16), (0, 2 * side - table.shape[1]))))
    return jnp.asarray(np.concatenate(rows), jnp.float32), places


MESH = pl.DeviceIdType.MESH
LINE, CORES = 4, 2
PARTS = (32, 32, 32, 32)
WEIGHT_UNIT = 512.0


def greet(sides):
    barrier = pltpu.get_barrier_semaphore()
    for axis, count, me in sides:
        for hop in range(1, count):
            pl.semaphore_signal(
                barrier, inc=1, device_id={axis: lax.rem(me + hop, count)}, device_id_type=MESH
            )
    return barrier, sum(count - 1 for _, count, _ in sides)


def receiver(me, hop, count):
    turn = lax.rem(hop + 1, count)
    pair = turn // CORES
    dx = lax.rem(pair, LINE)
    dz = lax.rem(pair // LINE + pair, LINE)
    z, x, core = me // (LINE * CORES), lax.rem(me // CORES, LINE), lax.rem(me, CORES)
    sign = 1 - 2 * core
    z, x = lax.rem(z + sign * dz + LINE, LINE), lax.rem(x + sign * dx + LINE, LINE)
    core = lax.rem(core + turn, CORES)
    return (z * LINE + x) * CORES + core


def hop_to(owner, me):
    wide, line = LINE * CORES, LINE - 1
    sign = 1 - 2 * lax.rem(me, CORES)
    dz = (sign * (owner // wide - me // wide)) & line
    dx = (sign * (((owner // CORES) & line) - lax.rem(me // CORES, LINE))) & line
    dc = (owner - me) & (CORES - 1)
    turn = CORES * (LINE * ((dz - dx) & line) + dx) + dc
    return (turn - 1) & (LINE * wide - 1)


def route(me, capacity, owner_ref, slot_ref, variance_ref, route_table, fields):
    blocks, places = owner_ref.shape[1], route_table.shape[1]
    square = (blocks, blocks)
    down, along = (lax.broadcasted_iota(jnp.int32, square, axis) for axis in (0, 1))
    hop_along = jnp.broadcast_to(hop_to(owner_ref[...], me), square)
    hop_down = hop_along.T
    count = lambda mask: jnp.sum(mask.astype(jnp.int32), axis=1, keepdims=True)
    rank = count((hop_along == hop_down) & (along < down))
    position = rank + count(hop_along < hop_down)
    weight = (1.0 / variance_ref[...]).astype(jnp.bfloat16).astype(jnp.float32)
    units = (jnp.broadcast_to(weight, square).T * WEIGHT_UNIT).astype(jnp.int32)[:, :1]
    slot = jnp.broadcast_to(slot_ref[...], square).T[:, :1]
    table = (blocks, places)
    number = lax.broadcasted_iota(jnp.int32, table, 0)
    lane = lax.broadcasted_iota(jnp.int32, table, 1)
    found = lane == hop_down[:, :1] * capacity + rank
    pick = lambda mask, values: jnp.sum(jnp.where(mask, values, 0), axis=0, keepdims=True)
    order = pick(lane == position, number)
    source = pick(found, position)
    route_table[...] = jnp.concatenate([order, source] + [order] * (route_table.shape[0] - 2), axis=0)
    row = [pick(found, units), pick(found, slot)]
    fields[...] = jnp.concatenate(row + [jnp.zeros_like(row[0])] * (fields.shape[0] - 2), axis=0)


def fold_rows(rows):
    part = rows.shape[1] // FOLDS
    zeros = jnp.zeros((rows.shape[0], SPAN), rows.dtype)
    quarters = []
    for fold in range(FOLDS):
        begin = fold * part
        ahead = rows[:, begin - SPAN : begin] if fold else zeros
        quarters.append(jnp.concatenate([ahead, rows[:, begin : begin + part]], axis=1))
    return jnp.concatenate(quarters, axis=0)


def each_window(reach, columns, rows, use):
    wide = 4 * SPAN

    def store(number, old):
        use(number * 4, old[:, SPAN - reach : SPAN - reach + wide])

    def piece(number, carry):
        store(number, rows(number, pl.multiple_of(number * wide - SPAN, SPAN), wide + SPAN))
        return carry

    first = rows(0, 0, wide)
    zeros = jnp.zeros((first.shape[0], SPAN), first.dtype)
    store(0, jnp.concatenate([zeros, first], axis=1))
    lax.fori_loop(1, columns // wide, piece, 0)
    last = jnp.concatenate([rows(columns // wide, columns - SPAN, SPAN), zeros], axis=1)
    use(columns // SPAN, last[:, SPAN - reach : 2 * SPAN - reach])


def transform_own(reach, rows_in, exposure, sums):
    def use(entry, window):
        part = jnp.dot(
            rows_in[...][:, : exposure.shape[0]], window, preferred_element_type=jnp.float32
        )
        for tile in range(window.shape[1] // SPAN):
            sums[entry + tile] = part[:, tile * SPAN : (tile + 1) * SPAN]

    rows = lambda number, begin, width: exposure[:, pl.ds(begin, width)]
    each_window(reach, exposure.shape[1], rows, use)


def transform_halos(reach, rows_in, exposure, edges, folds, sums, strip):
    columns = exposure.shape[1]
    per_fold = columns // FOLDS // (4 * SPAN)
    fold_of_row = lax.broadcasted_iota(jnp.int32, (EDGE, 1), 0) // (EDGE // FOLDS)

    def rows(number, begin, width):
        fold = jnp.minimum(number // per_fold, FOLDS - 1)
        inside = pl.multiple_of(begin + SPAN - fold * (columns // FOLDS), SPAN)
        mine = fold_of_row == fold
        halves = [ref[:, pl.ds(begin, width)] for ref in edges]
        halves += [jnp.where(mine, ref[:, pl.ds(inside, width)], 0) for ref in folds]
        return jnp.concatenate(halves, axis=0)

    def use(entry, window):
        part = jnp.dot(
            rows_in[...][:, exposure.shape[0] :], window, preferred_element_type=jnp.float32
        )
        for tile in range(window.shape[1] // SPAN):
            total = part[:, tile * SPAN : (tile + 1) * SPAN] + sums[entry + tile]
            strip[entry + tile] = total.astype(strip.dtype)

    each_window(reach, columns, rows, use)


def match_group(
    begin, size, route_smem, rows_out, cols_in, cols_out, row_wave, col_wave, coef_ref,
    strip, rows_ref, cols_ref, spectrum, response, warps, waves, warped,
):
    low = row_wave.shape[0] // 2
    side = warped.shape[1]
    numbers = [route_smem[0, begin + q] for q in range(size)]
    depth = size * 2 * low
    windows = [jnp.concatenate([strip[number], strip[number + 1]], axis=1) for number in numbers]
    spectrum[:depth] = jnp.dot(
        jnp.concatenate(windows, axis=0), cols_in[...], preferred_element_type=jnp.float32
    )
    scaled = [(row_wave[...] * coef_ref[number]).astype(jnp.bfloat16) for number in numbers]
    response[:depth] = jnp.dot(
        jnp.concatenate(scaled, axis=0), col_wave[...], preferred_element_type=jnp.float32
    )
    warps[: size * side] = jnp.dot(
        jnp.concatenate([rows_ref[number] for number in numbers], axis=0),
        rows_out[...],
        preferred_element_type=jnp.float32,
    ).astype(jnp.bfloat16)
    for q in range(size):
        top = slice(q * 2 * low, q * 2 * low + low)
        end = slice(q * 2 * low + low, (q + 1) * 2 * low)
        p_re, p_im = spectrum[top, :SPAN], spectrum[top, SPAN:]
        q_re, q_im = spectrum[end, :SPAN], spectrum[end, SPAN:]
        a_re, a_im = response[top, :SPAN], response[top, SPAN:]
        b_re, b_im = response[end, :SPAN], response[end, SPAN:]
        even_re = p_re * a_re - p_im * a_im + q_re * b_re - q_im * b_im
        even_im = p_re * a_im + p_im * a_re + q_re * b_im + q_im * b_re
        odd_re = p_re * b_re - p_im * b_im - q_re * a_re + q_im * a_im
        odd_im = p_re * b_im + p_im * b_re - q_re * a_im - q_im * a_re
        stacked = jnp.concatenate(
            [
                jnp.concatenate([even_re, even_im], axis=1),
                jnp.concatenate([odd_re, odd_im], axis=1),
            ],
            axis=0,
        ).astype(jnp.bfloat16)
        waves[q * side : (q + 1) * side, :] = jnp.dot(
            warps[q * side : (q + 1) * side, :], stacked, preferred_element_type=jnp.float32
        ).astype(jnp.bfloat16)
    across = jnp.dot(waves[: size * side], cols_out[...], preferred_element_type=jnp.float32).astype(
        jnp.bfloat16
    )
    for q in range(size):
        warped[begin + q] = lax.dot_general(
            across[q * side : (q + 1) * side],
            cols_ref[numbers[q]],
            (((1,), (1,)), ((), ())),
            preferred_element_type=jnp.float32,
        ).astype(jnp.bfloat16)


def slot_order(label_in, table_int, table_float, weight_sum, slots):
    labels = label_in[0]
    for source in range(1, label_in.shape[0]):
        labels = labels + label_in[source]
    places = labels.shape[1]
    square = (places, places)
    down, along = (lax.broadcasted_iota(jnp.int32, square, axis) for axis in (0, 1))
    slot_along = jnp.broadcast_to(labels[1:2], square)
    weight_along = jnp.broadcast_to(labels[0:1].astype(jnp.float32) / WEIGHT_UNIT, square)
    slot_down, weight_down = slot_along.T, weight_along.T
    ahead = (slot_along < slot_down) | ((slot_along == slot_down) & (along < down))
    rank = jnp.sum(ahead.astype(jnp.int32), axis=1, keepdims=True)
    chosen = rank == along
    order = jnp.sum(jnp.where(chosen, down, 0), axis=0, keepdims=True)
    slot = jnp.sum(jnp.where(chosen, slot_down, 0), axis=0, keepdims=True)
    weight = jnp.sum(jnp.where(chosen, weight_down, 0.0), axis=0, keepdims=True)
    goes_on = ((slot == pltpu.roll(slot, 1, axis=1)) & (along[:1] > 0)).astype(jnp.float32)
    up_to = jnp.sum((slot_down <= along).astype(jnp.int32), axis=0, keepdims=True)
    inside = jnp.sum((slot_down == along).astype(jnp.int32), axis=0, keepdims=True)
    last = jnp.maximum(up_to - 1, 0)
    table_int[...] = jnp.concatenate([order, last] + [order] * (table_int.shape[0] - 2), axis=0)
    table_float[...] = jnp.concatenate(
        [weight, goes_on, (inside > 0).astype(jnp.float32)] + [weight] * (table_float.shape[0] - 3),
        axis=0,
    )
    mine = jnp.where(slot_along[:slots] == down[:slots], weight_along[:slots], 0.0)
    weight_sum[...] = jnp.broadcast_to(jnp.sum(mine, axis=1, keepdims=True), (slots, places))


def coadd_kernel(
    reach, capacity, places, exposure_hbm, rows_hbm, cols_hbm, tables_hbm,
    row_bases, col_bases, coefficients, variance, owner, slot_index, coadd,
    exposure, before, after, fold_before, fold_after, fold_down, fold_up, sums, strip, tables, wave_table, row_wave, col_wave, coef_ref,
    route_table, fields, labels,
    spectrum, response, warps, waves, warped, rows_ref, cols_ref,
    label_in, table_int, table_float, weight_sum, weight_in, scale, running,
    route_smem, int_smem, float_smem,
    halo_send, halo_recv, send_sem, recv_sem, label_send, label_recv, load_sem, table_sem,
    sum_send, sum_recv, weight_send, weight_recv, *pieces,
):
    parts = len(PARTS)
    outgoing, arrived, partial, gathered = (
        pieces[kind * parts : (kind + 1) * parts] for kind in range(4)
    )
    me, my_src = lax.axis_index("tile"), lax.axis_index("src")
    blocks, side = warped.shape[:2]
    count, peers = labels.shape[0], partial[0].shape[0]
    rows_of = [slice(sum(PARTS[:part]), sum(PARTS[: part + 1])) for part in range(parts)]
    tiles, across = coadd.shape[0], peers
    barrier, greetings = greet((("tile", count, me), ("src", peers, my_src)))
    loads = [
        pltpu.make_async_copy(from_ref, to_ref, load_sem.at[number])
        for number, (from_ref, to_ref) in enumerate(
            (
                (tables_hbm, wave_table),
                (exposure_hbm, exposure),
                (rows_hbm, rows_ref),
                (cols_hbm, cols_ref),
            )
        )
    ]
    for load in loads:
        load.start()
    route(me, capacity, owner, slot_index, variance, route_table, fields)
    move = pltpu.make_async_copy(route_table, route_smem, table_sem.at[0])
    move.start()
    by_block = jnp.concatenate([coefficients[k] for k in range(coefficients.shape[0])], axis=0).T
    for number in range(blocks):
        coef_ref[number] = by_block[number : number + 1, :]
    lane = lax.broadcasted_iota(jnp.int32, fields.shape, 1)
    for hop in range(count):
        moved = pltpu.roll(
            fields[...], lax.rem((me - hop + count) * capacity, lane.shape[1]), axis=1
        )
        labels[hop] = jnp.where(lane // capacity == me, moved, 0)
    loads[1].wait()
    spare = reach - EDGE
    fold_down[...] = fold_rows(exposure[side - 2 * EDGE : side - EDGE, :][EDGE - spare :, :])
    fold_up[...] = fold_rows(exposure[EDGE : 2 * EDGE, :][:spare, :])
    pl.semaphore_wait(barrier, greetings)

    def halo(number, from_ref, to_ref, neighbour):
        return pltpu.make_async_remote_copy(
            src_ref=from_ref,
            dst_ref=to_ref,
            send_sem=halo_send.at[number],
            recv_sem=halo_recv.at[number],
            device_id={"tile": neighbour},
            device_id_type=MESH,
        )

    below, above = lax.rem(me + 1, count), lax.rem(me + count - 1, count)
    down = (
        halo(0, exposure.at[pl.ds(side - EDGE, EDGE)], before, below),
        halo(1, fold_down, fold_before, below),
    )
    up = (halo(2, exposure.at[pl.ds(0, EDGE)], after, above), halo(3, fold_up, fold_after, above))

    @pl.when(me < count - 1)
    def _():
        for copy in down:
            copy.start()

    @pl.when(me > 0)
    def _():
        for copy in up:
            copy.start()

    @pl.when(me == 0)
    def _():
        before[...] = jnp.zeros_like(before)
        fold_before[...] = jnp.zeros_like(fold_before)

    @pl.when(me == count - 1)
    def _():
        after[...] = jnp.zeros_like(after)
        fold_after[...] = jnp.zeros_like(fold_after)

    def label_message(hop):
        return pltpu.make_async_remote_copy(
            src_ref=labels.at[hop],
            dst_ref=label_in.at[me],
            send_sem=label_send.at[hop],
            recv_sem=label_recv.at[hop],
            device_id={"tile": receiver(me, hop, count)},
            device_id_type=MESH,
        )

    def message(part, hop):
        return pltpu.make_async_remote_copy(
            src_ref=outgoing[part].at[hop],
            dst_ref=arrived[part].at[pl.ds(me * capacity, capacity)],
            send_sem=send_sem.at[part, hop],
            recv_sem=recv_sem.at[part, hop],
            device_id={"tile": receiver(me, hop, count)},
            device_id_type=MESH,
        )

    def each_hop(begin, end, act):
        def one(hop, carry):
            act(hop)
            return carry

        lax.fori_loop(begin, end, one, 0)

    def piece(hop, r, part):
        return warped[route_smem[1, hop * capacity + r], rows_of[part], :]

    def send(part, hop):
        for r in range(capacity):
            outgoing[part][hop, r] = piece(hop, r, part)
        message(part, hop).start()

    ready = GROUP // capacity
    steps = blocks // GROUP
    each_hop(0, count - 1, lambda hop: label_message(hop).start())
    warped[...] = jnp.zeros_like(warped)
    view = lambda ref, place: ref.at[pl.ds(place[0], place[1]), pl.ds(0, place[2])]
    rows_in, rows_out, cols_in, cols_out = (view(tables, place) for place in places[:4])
    row_taps, col_taps = (view(wave_table, place) for place in places[4:])
    loads[0].wait()
    tables[...] = wave_table[: tables.shape[0], :].astype(tables.dtype)
    row_wave[...] = lax.dot_general(
        row_taps[...],
        row_bases[...].astype(jnp.float32),
        (((1,), (1,)), ((), ())),
        precision=lax.Precision.HIGHEST,
        preferred_element_type=jnp.float32,
    )
    col_wave[...] = jnp.dot(
        col_bases[...].astype(jnp.float32),
        col_taps[...],
        precision=lax.Precision.HIGHEST,
        preferred_element_type=jnp.float32,
    ).astype(col_wave.dtype)
    transform_own(reach, rows_in, exposure, sums)
    for load in loads[2:]:
        load.wait()
    move.wait()

    @pl.when(me > 0)
    def _():
        for copy in down:
            copy.wait_recv()

    @pl.when(me < count - 1)
    def _():
        for copy in up:
            copy.wait_recv()

    transform_halos(reach, rows_in, exposure, (before, after), (fold_before, fold_after), sums, strip)

    def group(size, step, carry):
        match_group(
            step * size, size, route_smem, rows_out, cols_in, cols_out, row_wave, col_wave, coef_ref,
            strip, rows_ref, cols_ref, spectrum, response, warps, waves, warped,
        )
        for number in range(size // capacity):
            for part in range(parts):
                send(part, step * (size // capacity) + number)
        return carry

    lax.fori_loop(0, ready, functools.partial(group, capacity), 0)
    lax.fori_loop(1, steps, functools.partial(group, GROUP), 0)
    for part in range(parts):
        each_hop(steps * ready, count - 1, lambda hop, part=part: send(part, hop))
        for r in range(capacity):
            arrived[part][me * capacity + r] = piece(count - 1, r, part)

    label_in[me] = labels[count - 1]
    each_hop(0, count - 1, lambda hop: label_message(hop).wait())
    slot_order(label_in, table_int, table_float, weight_sum, tiles * across * across)
    moves = [
        pltpu.make_async_copy(table_int, int_smem, table_sem.at[1]),
        pltpu.make_async_copy(table_float, float_smem, table_sem.at[2]),
    ]
    for move in moves:
        move.start()

    def to_peer(hop, from_ref, to_ref, send_sem, recv_sem):
        return pltpu.make_async_remote_copy(
            src_ref=from_ref,
            dst_ref=to_ref,
            send_sem=send_sem,
            recv_sem=recv_sem,
            device_id={"src": lax.rem(my_src + hop, peers)},
            device_id_type=MESH,
        )

    def weight_message(hop):
        return to_peer(
            hop, weight_sum, weight_in.at[hop - 1], weight_send.at[hop - 1], weight_recv.at[hop - 1]
        )

    def sum_message(part, hop):
        return to_peer(
            hop,
            partial[part].at[lax.rem(my_src + hop, peers)],
            gathered[part].at[hop - 1],
            sum_send.at[part, hop - 1],
            sum_recv.at[part, hop - 1],
        )

    for hop in range(1, peers):
        weight_message(hop).start()
    for move in moves:
        move.wait()

    def stack(part):
        high = PARTS[part]

        def add(place, total):
            block = arrived[part][int_smem[0, place]].astype(jnp.float32)
            total = total * float_smem[1, place] + float_smem[0, place] * block
            running[place, :high] = total
            return total

        lax.fori_loop(
            0, arrived[part].shape[0], add, jnp.zeros((high, side), jnp.float32), unroll=16
        )

        def take(slot, carry):
            row = lax.rem(slot // across, across)
            place = slot // (across * across) * across + lax.rem(slot, across)
            total = running[int_smem[1, slot], :high] * float_smem[2, slot]
            partial[part][row, place] = total.astype(jnp.bfloat16)
            return carry

        lax.fori_loop(0, tiles * across * across, take, 0, unroll=8)

    def finish(part):
        for hop in range(1, peers):
            sum_message(part, hop).wait()
        for tile in range(tiles):
            for column in range(across):
                place = tile * across + column
                total = partial[part][my_src, place].astype(jnp.float32)
                for hop in range(peers - 1):
                    total = total + gathered[part][hop, place].astype(jnp.float32)
                slot = (tile * across + my_src) * across + column
                coadd[tile, rows_of[part], column * side : (column + 1) * side] = total * scale[slot]

    for part in range(parts):
        each_hop(0, count - 1, lambda hop, part=part: message(part, hop).wait_recv())
        stack(part)
        for hop in range(1, peers):
            sum_message(part, hop).start()
        if part == 0:
            for hop in range(1, peers):
                weight_message(hop).wait()
            weight = weight_sum[...]
            for hop in range(peers - 1):
                weight = weight + weight_in[hop]
            factor = 1.0 / jnp.maximum(weight, 1.0)
            for slot in range(scale.shape[0]):
                scale[slot] = factor[slot : slot + 1]
        else:
            finish(part - 1)
    finish(parts - 1)
    for part in range(parts):
        each_hop(0, count - 1, lambda hop, part=part: message(part, hop).wait_send())

    @pl.when(me < count - 1)
    def _():
        for copy in down:
            copy.wait_send()

    @pl.when(me > 0)
    def _():
        for copy in up:
            copy.wait_send()


def body(
    exposure,
    row_bases,
    col_bases,
    coefficients,
    warp_rows,
    warp_cols,
    variance,
    footprint,
    slot_index,
):
    blocks, side = warp_rows.shape[2:4]
    columns = exposure.shape[2]
    basis_count, taps = row_bases.shape
    peers, count = lax.axis_size("src"), lax.axis_size("tile")
    capacity = max(2, 2 * blocks // count)
    slots, sends = TILES_DEV * peers * peers, count * capacity
    reach = taps // 2
    tall = -(-(side + taps - 1) // 16) * 16
    tables, places = wave_tables(
        taps, side, tall, side + taps - 1
    )
    spectra = places[0][1]
    near, far = pl.BlockSpec(memory_space=pltpu.VMEM), pl.BlockSpec(memory_space=pl.ANY)
    parts, per = len(PARTS), slots // peers
    narrow, wide, whole = jnp.bfloat16, jnp.float32, jnp.int32
    vmem, smem, dma = pltpu.VMEM, pltpu.SMEM, pltpu.SemaphoreType.DMA
    return pl.pallas_call(
        functools.partial(coadd_kernel, reach, capacity, places),
        in_specs=[far] * 4 + [near] * 6,
        out_specs=near,
        out_shape=jax.ShapeDtypeStruct((TILES_DEV, side, peers * side), wide),
        scratch_shapes=[
            vmem((side, columns), narrow),
            vmem((EDGE, columns), narrow),
            vmem((EDGE, columns), narrow),
            *[vmem((EDGE, columns // FOLDS + SPAN), narrow)] * 4,
            vmem((columns // SPAN + 1, spectra, SPAN), wide),
            vmem((columns // SPAN + 1, spectra, SPAN), narrow),
            vmem((places[4][0], 2 * SPAN), narrow),
            vmem(tables.shape, wide),
            vmem((spectra, basis_count), wide),
            vmem((basis_count, 2 * SPAN), narrow),
            vmem((blocks, 1, basis_count), wide),
            vmem((8, sends), whole),
            vmem((8, sends), whole),
            vmem((count, 8, sends), whole),
            vmem((GROUP * spectra, 2 * SPAN), wide),
            vmem((GROUP * spectra, 2 * SPAN), wide),
            vmem((GROUP * side, spectra), narrow),
            vmem((GROUP * side, 2 * SPAN), narrow),
            vmem((blocks, side, side), narrow),
            vmem((blocks, side, side), narrow),
            vmem((blocks, side, side), narrow),
            vmem((count, 8, sends), whole),
            vmem((8, sends), whole),
            vmem((8, sends), wide),
            vmem((slots, sends), wide),
            vmem((peers - 1, slots, sends), wide),
            vmem((slots, 1, sends), wide),
            vmem((sends, max(PARTS), side), wide),
            smem((8, sends), whole),
            smem((8, sends), whole),
            smem((8, sends), wide),
            dma((4,)),
            dma((4,)),
            dma((parts, count)),
            dma((parts, count)),
            dma((count,)),
            dma((count,)),
            dma((4,)),
            dma((3,)),
            dma((parts, peers - 1)),
            dma((parts, peers - 1)),
            dma((peers - 1,)),
            dma((peers - 1,)),
            *[vmem((count, capacity, high, side), narrow) for high in PARTS],
            *[vmem((sends, high, side), narrow) for high in PARTS],
            *[vmem((peers, per, high, side), narrow) for high in PARTS],
            *[vmem((peers - 1, per, high, side), narrow) for high in PARTS],
        ],
        compiler_params=pltpu.CompilerParams(
            collective_id=0, has_side_effects=True, vmem_limit_bytes=60 * 1024 * 1024
        ),
        cost_estimate=pl.CostEstimate(flops=4 << 30, bytes_accessed=10 << 20, transcendentals=0),
    )(
        exposure[0], warp_rows[0, 0], warp_cols[0, 0], tables, row_bases, col_bases,
        coefficients[0].transpose(2, 0, 1), variance[0], footprint.reshape(1, blocks), slot_index[0],
    )


def solution(mesh):
    placed = (
        P("src", "tile", None),
        P(),
        P(),
        P("src", "tile", None, None),
        P("src", "tile", None, None, None),
        P("src", "tile", None, None, None),
        P("src", "tile", None),
        P("src", "tile", None, None),
        P("src", "tile", None),
    )
    return jax.shard_map(
        body, mesh=mesh, in_specs=placed, out_specs=P("tile", "src", None), check_vma=False
    )
```

```python
import functools

import jax
import jax.numpy as jnp
import numpy as np
from jax import lax
from jax.experimental import pallas as pl
from jax.experimental.pallas import tpu as pltpu
from jax.sharding import PartitionSpec as P

TILES_DEV = 4


EDGE = 16
FOLDS = 4
GROUP = 8
SPAN = 128


def wave_tables(taps, side, tall, wide):
    low, lanes = -(-(tall // 2 + 1) // 16) * 16, SPAN
    u, v = np.arange(low), np.arange(lanes)
    keep_u, keep_v = u <= tall // 2, v <= wide // 2
    twice_u = np.where((u == 0) | (2 * u == tall), 1.0, 2.0) * keep_u
    twice_v = np.where((v == 0) | (2 * v == wide), 1.0, 2.0) * keep_v
    turn = lambda one, other, length: 2.0 * np.pi / length * (np.outer(one, other) % length)
    reach, edge = taps // 2, np.arange(EDGE)
    fold = edge % (reach - EDGE)
    starts = (reach + np.arange(side), reach - EDGE + edge, reach + side + edge, fold, reach + side + EDGE + fold)
    down = turn(u, np.concatenate(starts), tall)
    rows_in = np.concatenate([np.cos(down), np.sin(down)]) * np.tile(keep_u, 2)[:, None]
    back = turn(np.arange(side), u, tall)
    rows_out = np.concatenate([np.cos(back) * twice_u, -np.sin(back) * twice_u], axis=1) / tall
    along = turn(np.arange(2 * side), v, wide)
    inside = (np.arange(2 * side) < wide)[:, None]
    cols_in = np.concatenate([np.cos(along), -np.sin(along)], axis=1) * inside * np.tile(keep_v, 2)
    front = turn(v, np.arange(side), wide)
    cols_out = np.concatenate([np.cos(front), -np.sin(front)]) * np.tile(twice_v, 2)[:, None] / wide
    tap_u, tap_v = turn(u, np.arange(taps), tall), turn(np.arange(taps), v, wide)
    row_taps = np.concatenate([np.cos(tap_u), np.sin(tap_u)]) * np.tile(keep_u, 2)[:, None]
    col_taps = np.concatenate([np.cos(tap_v), np.sin(tap_v)], axis=1) * np.tile(keep_v, 2)
    places, rows = [], []
    for table in (rows_in, rows_out, cols_in, cols_out, row_taps, col_taps):
        places.append((sum(part.shape[0] for part in rows), *table.shape))
        rows.append(np.pad(table, ((0, -table.shape[0] % 16), (0, 2 * side - table.shape[1]))))
    return jnp.asarray(np.concatenate(rows), jnp.float32), places


MESH = pl.DeviceIdType.MESH
LINE, CORES = 4, 2
PARTS = (32, 32, 32, 32)
WEIGHT_UNIT = 512.0


def greet(sides):
    barrier = pltpu.get_barrier_semaphore()
    for axis, count, me in sides:
        for hop in range(1, count):
            pl.semaphore_signal(
                barrier, inc=1, device_id={axis: lax.rem(me + hop, count)}, device_id_type=MESH
            )
    return barrier, sum(count - 1 for _, count, _ in sides)


def receiver(me, hop, count):
    turn = lax.rem(hop + 1, count)
    pair = turn // CORES
    dx = lax.rem(pair, LINE)
    dz = lax.rem(pair // LINE + pair, LINE)
    z, x, core = me // (LINE * CORES), lax.rem(me // CORES, LINE), lax.rem(me, CORES)
    sign = 1 - 2 * core
    z, x = lax.rem(z + sign * dz + LINE, LINE), lax.rem(x + sign * dx + LINE, LINE)
    core = lax.rem(core + turn, CORES)
    return (z * LINE + x) * CORES + core


def hop_to(owner, me):
    wide, line = LINE * CORES, LINE - 1
    sign = 1 - 2 * lax.rem(me, CORES)
    dz = (sign * (owner // wide - me // wide)) & line
    dx = (sign * (((owner // CORES) & line) - lax.rem(me // CORES, LINE))) & line
    dc = (owner - me) & (CORES - 1)
    turn = CORES * (LINE * ((dz - dx) & line) + dx) + dc
    return (turn - 1) & (LINE * wide - 1)


def route(me, capacity, owner_ref, slot_ref, variance_ref, route_table, fields):
    blocks, places = owner_ref.shape[1], route_table.shape[1]
    square = (blocks, blocks)
    down, along = (lax.broadcasted_iota(jnp.int32, square, axis) for axis in (0, 1))
    hop_along = jnp.broadcast_to(hop_to(owner_ref[...], me), square)
    hop_down = hop_along.T
    count = lambda mask: jnp.sum(mask.astype(jnp.int32), axis=1, keepdims=True)
    rank = count((hop_along == hop_down) & (along < down))
    position = rank + count(hop_along < hop_down)
    weight = (1.0 / variance_ref[...]).astype(jnp.bfloat16).astype(jnp.float32)
    units = (jnp.broadcast_to(weight, square).T * WEIGHT_UNIT).astype(jnp.int32)[:, :1]
    slot = jnp.broadcast_to(slot_ref[...], square).T[:, :1]
    table = (blocks, places)
    number = lax.broadcasted_iota(jnp.int32, table, 0)
    lane = lax.broadcasted_iota(jnp.int32, table, 1)
    found = lane == hop_down[:, :1] * capacity + rank
    pick = lambda mask, values: jnp.sum(jnp.where(mask, values, 0), axis=0, keepdims=True)
    order = pick(lane == position, number)
    source = pick(found, position)
    route_table[...] = jnp.concatenate([order, source] + [order] * (route_table.shape[0] - 2), axis=0)
    row = [pick(found, units), pick(found, slot)]
    fields[...] = jnp.concatenate(row + [jnp.zeros_like(row[0])] * (fields.shape[0] - 2), axis=0)


def fold_rows(rows):
    part = rows.shape[1] // FOLDS
    zeros = jnp.zeros((rows.shape[0], SPAN), rows.dtype)
    quarters = []
    for fold in range(FOLDS):
        begin = fold * part
        ahead = rows[:, begin - SPAN : begin] if fold else zeros
        quarters.append(jnp.concatenate([ahead, rows[:, begin : begin + part]], axis=1))
    return jnp.concatenate(quarters, axis=0)


def each_window(reach, columns, rows, use):
    wide = 4 * SPAN

    def store(number, old):
        use(number * 4, old[:, SPAN - reach : SPAN - reach + wide])

    def piece(number, carry):
        store(number, rows(number, pl.multiple_of(number * wide - SPAN, SPAN), wide + SPAN))
        return carry

    first = rows(0, 0, wide)
    zeros = jnp.zeros((first.shape[0], SPAN), first.dtype)
    store(0, jnp.concatenate([zeros, first], axis=1))
    lax.fori_loop(1, columns // wide, piece, 0)
    last = jnp.concatenate([rows(columns // wide, columns - SPAN, SPAN), zeros], axis=1)
    use(columns // SPAN, last[:, SPAN - reach : 2 * SPAN - reach])


def transform_own(reach, rows_in, exposure, sums):
    def use(entry, window):
        part = jnp.dot(
            rows_in[...][:, : exposure.shape[0]], window, preferred_element_type=jnp.float32
        )
        for tile in range(window.shape[1] // SPAN):
            sums[entry + tile] = part[:, tile * SPAN : (tile + 1) * SPAN]

    rows = lambda number, begin, width: exposure[:, pl.ds(begin, width)]
    each_window(reach, exposure.shape[1], rows, use)


def transform_halos(reach, rows_in, exposure, edges, folds, sums, strip):
    columns = exposure.shape[1]
    per_fold = columns // FOLDS // (4 * SPAN)
    fold_of_row = lax.broadcasted_iota(jnp.int32, (EDGE, 1), 0) // (EDGE // FOLDS)

    def rows(number, begin, width):
        fold = jnp.minimum(number // per_fold, FOLDS - 1)
        inside = pl.multiple_of(begin + SPAN - fold * (columns // FOLDS), SPAN)
        mine = fold_of_row == fold
        halves = [ref[:, pl.ds(begin, width)] for ref in edges]
        halves += [jnp.where(mine, ref[:, pl.ds(inside, width)], 0) for ref in folds]
        return jnp.concatenate(halves, axis=0)

    def use(entry, window):
        part = jnp.dot(
            rows_in[...][:, exposure.shape[0] :], window, preferred_element_type=jnp.float32
        )
        for tile in range(window.shape[1] // SPAN):
            total = part[:, tile * SPAN : (tile + 1) * SPAN] + sums[entry + tile]
            strip[entry + tile] = total.astype(strip.dtype)

    each_window(reach, columns, rows, use)


def match_group(
    begin, size, route_smem, rows_out, cols_in, cols_out, row_wave, col_wave, coef_ref,
    strip, rows_ref, cols_ref, spectrum, response, warps, waves, warped,
):
    low = row_wave.shape[0] // 2
    side = warped.shape[1]
    numbers = [route_smem[0, begin + q] for q in range(size)]
    depth = size * 2 * low
    windows = [jnp.concatenate([strip[number], strip[number + 1]], axis=1) for number in numbers]
    spectrum[:depth] = jnp.dot(
        jnp.concatenate(windows, axis=0), cols_in[...], preferred_element_type=jnp.float32
    )
    scaled = [(row_wave[...] * coef_ref[number]).astype(jnp.bfloat16) for number in numbers]
    response[:depth] = jnp.dot(
        jnp.concatenate(scaled, axis=0), col_wave[...], preferred_element_type=jnp.float32
    )
    warps[: size * side] = jnp.dot(
        jnp.concatenate([rows_ref[number] for number in numbers], axis=0),
        rows_out[...],
        preferred_element_type=jnp.float32,
    ).astype(jnp.bfloat16)
    for q in range(size):
        top = slice(q * 2 * low, q * 2 * low + low)
        end = slice(q * 2 * low + low, (q + 1) * 2 * low)
        p_re, p_im = spectrum[top, :SPAN], spectrum[top, SPAN:]
        q_re, q_im = spectrum[end, :SPAN], spectrum[end, SPAN:]
        a_re, a_im = response[top, :SPAN], response[top, SPAN:]
        b_re, b_im = response[end, :SPAN], response[end, SPAN:]
        even_re = p_re * a_re - p_im * a_im + q_re * b_re - q_im * b_im
        even_im = p_re * a_im + p_im * a_re + q_re * b_im + q_im * b_re
        odd_re = p_re * b_re - p_im * b_im - q_re * a_re + q_im * a_im
        odd_im = p_re * b_im + p_im * b_re - q_re * a_im - q_im * a_re
        stacked = jnp.concatenate(
            [
                jnp.concatenate([even_re, even_im], axis=1),
                jnp.concatenate([odd_re, odd_im], axis=1),
            ],
            axis=0,
        ).astype(jnp.bfloat16)
        waves[q * side : (q + 1) * side, :] = jnp.dot(
            warps[q * side : (q + 1) * side, :], stacked, preferred_element_type=jnp.float32
        ).astype(jnp.bfloat16)
    across = jnp.dot(waves[: size * side], cols_out[...], preferred_element_type=jnp.float32).astype(
        jnp.bfloat16
    )
    for q in range(size):
        warped[begin + q] = lax.dot_general(
            across[q * side : (q + 1) * side],
            cols_ref[numbers[q]],
            (((1,), (1,)), ((), ())),
            preferred_element_type=jnp.float32,
        ).astype(jnp.bfloat16)


def slot_order(label_in, table_int, table_float, weight_sum, slots):
    labels = label_in[0]
    for source in range(1, label_in.shape[0]):
        labels = labels + label_in[source]
    places = labels.shape[1]
    square = (places, places)
    down, along = (lax.broadcasted_iota(jnp.int32, square, axis) for axis in (0, 1))
    slot_along = jnp.broadcast_to(labels[1:2], square)
    weight_along = jnp.broadcast_to(labels[0:1].astype(jnp.float32) / WEIGHT_UNIT, square)
    slot_down, weight_down = slot_along.T, weight_along.T
    ahead = (slot_along < slot_down) | ((slot_along == slot_down) & (along < down))
    rank = jnp.sum(ahead.astype(jnp.int32), axis=1, keepdims=True)
    chosen = rank == along
    order = jnp.sum(jnp.where(chosen, down, 0), axis=0, keepdims=True)
    slot = jnp.sum(jnp.where(chosen, slot_down, 0), axis=0, keepdims=True)
    weight = jnp.sum(jnp.where(chosen, weight_down, 0.0), axis=0, keepdims=True)
    goes_on = ((slot == pltpu.roll(slot, 1, axis=1)) & (along[:1] > 0)).astype(jnp.float32)
    up_to = jnp.sum((slot_down <= along).astype(jnp.int32), axis=0, keepdims=True)
    inside = jnp.sum((slot_down == along).astype(jnp.int32), axis=0, keepdims=True)
    last = jnp.maximum(up_to - 1, 0)
    table_int[...] = jnp.concatenate([order, last] + [order] * (table_int.shape[0] - 2), axis=0)
    table_float[...] = jnp.concatenate(
        [weight, goes_on, (inside > 0).astype(jnp.float32)] + [weight] * (table_float.shape[0] - 3),
        axis=0,
    )
    mine = jnp.where(slot_along[:slots] == down[:slots], weight_along[:slots], 0.0)
    weight_sum[...] = jnp.broadcast_to(jnp.sum(mine, axis=1, keepdims=True), (slots, places))


def coadd_kernel(
    reach, capacity, places, exposure_hbm, rows_hbm, cols_hbm, tables_hbm,
    row_bases, col_bases, coefficients, variance, owner, slot_index, coadd,
    exposure, before, after, fold_before, fold_after, fold_down, fold_up, sums, strip, tables, wave_table, row_wave, col_wave, coef_ref,
    route_table, fields, labels,
    spectrum, response, warps, waves, warped, rows_ref, cols_ref,
    label_in, table_int, table_float, weight_sum, weight_in, scale, running,
    route_smem, int_smem, float_smem,
    halo_send, halo_recv, send_sem, recv_sem, label_send, label_recv, load_sem, table_sem,
    sum_send, sum_recv, weight_send, weight_recv, *pieces,
):
    parts = len(PARTS)
    outgoing, arrived, partial, gathered = (
        pieces[kind * parts : (kind + 1) * parts] for kind in range(4)
    )
    me, my_src = lax.axis_index("tile"), lax.axis_index("src")
    blocks, side = warped.shape[:2]
    count, peers = labels.shape[0], partial[0].shape[0]
    rows_of = [slice(sum(PARTS[:part]), sum(PARTS[: part + 1])) for part in range(parts)]
    tiles, across = coadd.shape[0], peers
    barrier, greetings = greet((("tile", count, me), ("src", peers, my_src)))
    loads = [
        pltpu.make_async_copy(from_ref, to_ref, load_sem.at[number])
        for number, (from_ref, to_ref) in enumerate(
            (
                (tables_hbm, wave_table),
                (exposure_hbm, exposure),
                (rows_hbm, rows_ref),
                (cols_hbm, cols_ref),
            )
        )
    ]
    for load in loads:
        load.start()
    route(me, capacity, owner, slot_index, variance, route_table, fields)
    move = pltpu.make_async_copy(route_table, route_smem, table_sem.at[0])
    move.start()
    by_block = jnp.concatenate([coefficients[k] for k in range(coefficients.shape[0])], axis=0).T
    for number in range(blocks):
        coef_ref[number] = by_block[number : number + 1, :]
    lane = lax.broadcasted_iota(jnp.int32, fields.shape, 1)
    for hop in range(count):
        moved = pltpu.roll(
            fields[...], lax.rem((me - hop + count) * capacity, lane.shape[1]), axis=1
        )
        labels[hop] = jnp.where(lane // capacity == me, moved, 0)
    loads[1].wait()
    spare = reach - EDGE
    fold_down[...] = fold_rows(exposure[side - 2 * EDGE : side - EDGE, :][EDGE - spare :, :])
    fold_up[...] = fold_rows(exposure[EDGE : 2 * EDGE, :][:spare, :])
    pl.semaphore_wait(barrier, greetings)

    def halo(number, from_ref, to_ref, neighbour):
        return pltpu.make_async_remote_copy(
            src_ref=from_ref,
            dst_ref=to_ref,
            send_sem=halo_send.at[number],
            recv_sem=halo_recv.at[number],
            device_id={"tile": neighbour},
            device_id_type=MESH,
        )

    below, above = lax.rem(me + 1, count), lax.rem(me + count - 1, count)
    down = (
        halo(0, exposure.at[pl.ds(side - EDGE, EDGE)], before, below),
        halo(1, fold_down, fold_before, below),
    )
    up = (halo(2, exposure.at[pl.ds(0, EDGE)], after, above), halo(3, fold_up, fold_after, above))

    @pl.when(me < count - 1)
    def _():
        for copy in down:
            copy.start()

    @pl.when(me > 0)
    def _():
        for copy in up:
            copy.start()

    @pl.when(me == 0)
    def _():
        before[...] = jnp.zeros_like(before)
        fold_before[...] = jnp.zeros_like(fold_before)

    @pl.when(me == count - 1)
    def _():
        after[...] = jnp.zeros_like(after)
        fold_after[...] = jnp.zeros_like(fold_after)

    def label_message(hop):
        return pltpu.make_async_remote_copy(
            src_ref=labels.at[hop],
            dst_ref=label_in.at[me],
            send_sem=label_send.at[hop],
            recv_sem=label_recv.at[hop],
            device_id={"tile": receiver(me, hop, count)},
            device_id_type=MESH,
        )

    def message(part, hop):
        return pltpu.make_async_remote_copy(
            src_ref=outgoing[part].at[hop],
            dst_ref=arrived[part].at[pl.ds(me * capacity, capacity)],
            send_sem=send_sem.at[part, hop],
            recv_sem=recv_sem.at[part, hop],
            device_id={"tile": receiver(me, hop, count)},
            device_id_type=MESH,
        )

    def each_hop(begin, end, act):
        def one(hop, carry):
            act(hop)
            return carry

        lax.fori_loop(begin, end, one, 0)

    def piece(hop, r, part):
        return warped[route_smem[1, hop * capacity + r], rows_of[part], :]

    def send(part, hop):
        for r in range(capacity):
            outgoing[part][hop, r] = piece(hop, r, part)
        message(part, hop).start()

    ready = GROUP // capacity
    steps = blocks // GROUP
    each_hop(0, count - 1, lambda hop: label_message(hop).start())
    warped[...] = jnp.zeros_like(warped)
    view = lambda ref, place: ref.at[pl.ds(place[0], place[1]), pl.ds(0, place[2])]
    rows_in, rows_out, cols_in, cols_out = (view(tables, place) for place in places[:4])
    row_taps, col_taps = (view(wave_table, place) for place in places[4:])
    loads[0].wait()
    tables[...] = wave_table[: tables.shape[0], :].astype(tables.dtype)
    row_wave[...] = lax.dot_general(
        row_taps[...],
        row_bases[...].astype(jnp.float32),
        (((1,), (1,)), ((), ())),
        precision=lax.Precision.HIGHEST,
        preferred_element_type=jnp.float32,
    )
    col_wave[...] = jnp.dot(
        col_bases[...].astype(jnp.float32),
        col_taps[...],
        precision=lax.Precision.HIGHEST,
        preferred_element_type=jnp.float32,
    ).astype(col_wave.dtype)
    transform_own(reach, rows_in, exposure, sums)
    for load in loads[2:]:
        load.wait()
    move.wait()

    @pl.when(me > 0)
    def _():
        for copy in down:
            copy.wait_recv()

    @pl.when(me < count - 1)
    def _():
        for copy in up:
            copy.wait_recv()

    transform_halos(reach, rows_in, exposure, (before, after), (fold_before, fold_after), sums, strip)

    def group(size, step, carry):
        match_group(
            step * size, size, route_smem, rows_out, cols_in, cols_out, row_wave, col_wave, coef_ref,
            strip, rows_ref, cols_ref, spectrum, response, warps, waves, warped,
        )
        for number in range(size // capacity):
            for part in range(parts):
                send(part, step * (size // capacity) + number)
        return carry

    lax.fori_loop(0, ready, functools.partial(group, capacity), 0)
    lax.fori_loop(1, steps, functools.partial(group, GROUP), 0)
    for part in range(parts):
        first, rest = steps * ready, count - 1 - steps * ready
        turned = lambda hop, part=part: send(part, first + lax.rem(hop + 4 * part, rest))
        each_hop(0, rest, turned)
        for r in range(capacity):
            arrived[part][me * capacity + r] = piece(count - 1, r, part)

    label_in[me] = labels[count - 1]
    each_hop(0, count - 1, lambda hop: label_message(hop).wait())
    slot_order(label_in, table_int, table_float, weight_sum, tiles * across * across)
    moves = [
        pltpu.make_async_copy(table_int, int_smem, table_sem.at[1]),
        pltpu.make_async_copy(table_float, float_smem, table_sem.at[2]),
    ]
    for move in moves:
        move.start()

    def to_peer(hop, from_ref, to_ref, send_sem, recv_sem):
        return pltpu.make_async_remote_copy(
            src_ref=from_ref,
            dst_ref=to_ref,
            send_sem=send_sem,
            recv_sem=recv_sem,
            device_id={"src": lax.rem(my_src + hop, peers)},
            device_id_type=MESH,
        )

    def weight_message(hop):
        return to_peer(
            hop, weight_sum, weight_in.at[hop - 1], weight_send.at[hop - 1], weight_recv.at[hop - 1]
        )

    def sum_message(part, hop):
        return to_peer(
            hop,
            partial[part].at[lax.rem(my_src + hop, peers)],
            gathered[part].at[hop - 1],
            sum_send.at[part, hop - 1],
            sum_recv.at[part, hop - 1],
        )

    for hop in range(1, peers):
        weight_message(hop).start()
    for move in moves:
        move.wait()

    def stack(part):
        high = PARTS[part]

        def add(place, total):
            block = arrived[part][int_smem[0, place]].astype(jnp.float32)
            total = total * float_smem[1, place] + float_smem[0, place] * block
            running[place, :high] = total
            return total

        lax.fori_loop(
            0, arrived[part].shape[0], add, jnp.zeros((high, side), jnp.float32), unroll=4
        )

        def take(slot, carry):
            row = lax.rem(slot // across, across)
            place = slot // (across * across) * across + lax.rem(slot, across)
            total = running[int_smem[1, slot], :high] * float_smem[2, slot]
            partial[part][row, place] = total.astype(jnp.bfloat16)
            return carry

        lax.fori_loop(0, tiles * across * across, take, 0, unroll=4)

    def finish(part):
        for hop in range(1, peers):
            sum_message(part, hop).wait()
        for tile in range(tiles):
            for column in range(across):
                place = tile * across + column
                total = partial[part][my_src, place].astype(jnp.float32)
                for hop in range(peers - 1):
                    total = total + gathered[part][hop, place].astype(jnp.float32)
                slot = (tile * across + my_src) * across + column
                coadd[tile, rows_of[part], column * side : (column + 1) * side] = total * scale[slot]

    for part in range(parts):
        each_hop(0, count - 1, lambda hop, part=part: message(part, hop).wait_recv())
        stack(part)
        for hop in range(1, peers):
            sum_message(part, hop).start()
        if part == 0:
            for hop in range(1, peers):
                weight_message(hop).wait()
            weight = weight_sum[...]
            for hop in range(peers - 1):
                weight = weight + weight_in[hop]
            factor = 1.0 / jnp.maximum(weight, 1.0)
            for slot in range(scale.shape[0]):
                scale[slot] = factor[slot : slot + 1]
        else:
            finish(part - 1)
    finish(parts - 1)
    for part in range(parts):
        each_hop(0, count - 1, lambda hop, part=part: message(part, hop).wait_send())

    @pl.when(me < count - 1)
    def _():
        for copy in down:
            copy.wait_send()

    @pl.when(me > 0)
    def _():
        for copy in up:
            copy.wait_send()


def body(
    exposure,
    row_bases,
    col_bases,
    coefficients,
    warp_rows,
    warp_cols,
    variance,
    footprint,
    slot_index,
):
    blocks, side = warp_rows.shape[2:4]
    columns = exposure.shape[2]
    basis_count, taps = row_bases.shape
    peers, count = lax.axis_size("src"), lax.axis_size("tile")
    capacity = max(2, 2 * blocks // count)
    slots, sends = TILES_DEV * peers * peers, count * capacity
    reach = taps // 2
    tall = -(-(side + taps - 1) // 16) * 16
    tables, places = wave_tables(
        taps, side, tall, side + taps - 1
    )
    spectra = places[0][1]
    near, far = pl.BlockSpec(memory_space=pltpu.VMEM), pl.BlockSpec(memory_space=pl.ANY)
    parts, per = len(PARTS), slots // peers
    narrow, wide, whole = jnp.bfloat16, jnp.float32, jnp.int32
    vmem, smem, dma = pltpu.VMEM, pltpu.SMEM, pltpu.SemaphoreType.DMA
    return pl.pallas_call(
        functools.partial(coadd_kernel, reach, capacity, places),
        in_specs=[far] * 4 + [near] * 6,
        out_specs=near,
        out_shape=jax.ShapeDtypeStruct((TILES_DEV, side, peers * side), wide),
        scratch_shapes=[
            vmem((side, columns), narrow),
            vmem((EDGE, columns), narrow),
            vmem((EDGE, columns), narrow),
            *[vmem((EDGE, columns // FOLDS + SPAN), narrow)] * 4,
            vmem((columns // SPAN + 1, spectra, SPAN), wide),
            vmem((columns // SPAN + 1, spectra, SPAN), narrow),
            vmem((places[4][0], 2 * SPAN), narrow),
            vmem(tables.shape, wide),
            vmem((spectra, basis_count), wide),
            vmem((basis_count, 2 * SPAN), narrow),
            vmem((blocks, 1, basis_count), wide),
            vmem((8, sends), whole),
            vmem((8, sends), whole),
            vmem((count, 8, sends), whole),
            vmem((GROUP * spectra, 2 * SPAN), wide),
            vmem((GROUP * spectra, 2 * SPAN), wide),
            vmem((GROUP * side, spectra), narrow),
            vmem((GROUP * side, 2 * SPAN), narrow),
            vmem((blocks, side, side), narrow),
            vmem((blocks, side, side), narrow),
            vmem((blocks, side, side), narrow),
            vmem((count, 8, sends), whole),
            vmem((8, sends), whole),
            vmem((8, sends), wide),
            vmem((slots, sends), wide),
            vmem((peers - 1, slots, sends), wide),
            vmem((slots, 1, sends), wide),
            vmem((sends, max(PARTS), side), wide),
            smem((8, sends), whole),
            smem((8, sends), whole),
            smem((8, sends), wide),
            dma((4,)),
            dma((4,)),
            dma((parts, count)),
            dma((parts, count)),
            dma((count,)),
            dma((count,)),
            dma((4,)),
            dma((3,)),
            dma((parts, peers - 1)),
            dma((parts, peers - 1)),
            dma((peers - 1,)),
            dma((peers - 1,)),
            *[vmem((count, capacity, high, side), narrow) for high in PARTS],
            *[vmem((sends, high, side), narrow) for high in PARTS],
            *[vmem((peers, per, high, side), narrow) for high in PARTS],
            *[vmem((peers - 1, per, high, side), narrow) for high in PARTS],
        ],
        compiler_params=pltpu.CompilerParams(
            collective_id=0, has_side_effects=True, vmem_limit_bytes=60 * 1024 * 1024
        ),
        cost_estimate=pl.CostEstimate(flops=4 << 30, bytes_accessed=10 << 20, transcendentals=0),
    )(
        exposure[0], warp_rows[0, 0], warp_cols[0, 0], tables, row_bases, col_bases,
        coefficients[0].transpose(2, 0, 1), variance[0], footprint.reshape(1, blocks), slot_index[0],
    )


def solution(mesh):
    placed = (
        P("src", "tile", None),
        P(),
        P(),
        P("src", "tile", None, None),
        P("src", "tile", None, None, None),
        P("src", "tile", None, None, None),
        P("src", "tile", None),
        P("src", "tile", None, None),
        P("src", "tile", None),
    )
    return jax.shard_map(
        body, mesh=mesh, in_specs=placed, out_specs=P("tile", "src", None), check_vma=False
    )
```
